32 devices in a mesh: dp: 4 (over z), expert: 4 (over x, core), stream: 2 (over y).
Axes of the slice: x: 2, y: 2, z: 4, core: 2. Of those that a mesh axis runs over, the one named last changes fastest.
Arguments:
- patches: bfloat16 [32768, 768], P(('dp', 'expert', 'stream')), may hold values from -6 to 6
- cond: bfloat16 [128, 768], P(('dp', 'expert', 'stream')), may hold values from -6 to 6
- long_pack: int32 [32], P(('dp', 'expert', 'stream')), may hold values from 0 to 1
- routes: int32 [32768, 2], P(('dp', 'expert', 'stream')), may hold values from 0 to 7, all different within a row; in each aligned block of 1024 rows (0 to 1023, 1024 to 2047, ...) at most 320 rows name the same one
- ada_weight: bfloat16 [768, 4608], P('dp'), may hold values from -0.21875 to 0.21875
- qkv_weight: bfloat16 [768, 2304], P('dp'), may hold values from -0.21875 to 0.21875
- out_weight: bfloat16 [768, 768], P('dp'), may hold values from -0.625 to 0.625
- router_weight: bfloat16 [768, 8], P('dp'), may hold values from -0.15625 to 0.15625
- shared_up: bfloat16 [768, 3072], P('dp'), may hold values from -0.21875 to 0.21875
- shared_down: bfloat16 [3072, 768], P('dp'), may hold values from -0.109375 to 0.109375
- expert_up: bfloat16 [8, 768, 3072], P(('expert', 'stream'), 'dp'), may hold values from -0.21875 to 0.21875
- expert_down: bfloat16 [8, 3072, 768], P(('expert', 'stream'), 'dp'), may hold values from -0.109375 to 0.109375
- out_grad: bfloat16 [32768, 768], P(('dp', 'expert', 'stream')), may hold values from -6 to 6
Outputs:
- block_out: bfloat16 [32768, 768], P(('dp', 'expert', 'stream'))
- patches_grad: float32 [32768, 768], P(('dp', 'expert', 'stream'))
- cond_grad: float32 [128, 768], P(('dp', 'expert', 'stream'))
- ada_weight_grad: float32 [768, 4608], P('dp', ('expert', 'stream'))
- qkv_weight_grad: float32 [768, 2304], P('dp', ('expert', 'stream'))
- out_weight_grad: float32 [768, 768], P('dp', ('expert', 'stream'))
- router_weight_grad: float32 [768, 8], P('dp', ('expert', 'stream'))
- shared_up_grad: float32 [768, 3072], P('dp', ('expert', 'stream'))
- shared_down_grad: float32 [3072, 768], P('dp', ('expert', 'stream'))
- expert_up_grad: float32 [8, 768, 3072], P(('expert', 'stream'), 'dp')
- expert_down_grad: float32 [8, 3072, 768], P(('expert', 'stream'), 'dp')
The draws below stay inside these ranges and needn't reach their ends.
Inputs may be any that keep to these rules, and one draw needn't show every extreme that they name: `long_pack`: 1: pack of one image of 1024 patches; 0: four images of 256 patches. `routes`: each row names 2 different experts; among the rows of one device no expert is named more than 320 times, and that number is reached.
All inputs are finite; a program needn't handle non-finite values.
Results may differ from the reference program's by a relative error of at most 0.02.
The reference program's roundings to bfloat16 on the way count: a program that leaves them out, or rounds other values in their place, can miss the bound.
Values may be sent and summed in bfloat16 or wider, within the bound.
No kernel may reach another device: no remote copies, remote signals or barrier semaphores. Data moves between devices by JAX's collectives and lax.ppermute only.
A program may use at most 256 MiB of HBM per device.

```python
import math
from functools import partial
import jax
import jax.numpy as jnp
import numpy as np
from jax import lax

D = 768
HEADS = 12
HEAD = 64
FF = 3072
TOP = 2
PACK = 1024
EXPERTS = 8
TOK_DEV = 1024
PACKS = 32
SLOTS = 128
TOKENS = 32768
CAP = 320


def set_ends(drawn, own_key, low, top_value):
    place = [jax.random.randint(jax.random.fold_in(own_key, axis), (), 0, length) for axis, length in enumerate(drawn.shape)]
    widest = drawn.shape.index(max(drawn.shape))
    neighbour = place[:widest] + [(place[widest] + 1) % drawn.shape[widest]] + place[widest + 1:]
    return drawn.at[tuple(place)].set(low).at[tuple(neighbour)].set(top_value)


def levels(rng, extent, split, smallest, top_value):
    factor_of = 1.0
    for axis_at, blocks in split:
        heights = jax.random.uniform(jax.random.fold_in(jax.random.fold_in(rng, 6), axis_at), (blocks,), jnp.float32, smallest / len(split), top_value / len(split))
        factor_of = factor_of * jnp.repeat(jnp.exp(heights), extent[axis_at] // blocks).reshape((-1,) + (1,) * (len(extent) - 1 - axis_at))
    return factor_of


def shared_out(own_key, own, number, rows, amount, top, most, lean):
    ranking = jax.random.permutation(own_key, amount)
    packed, common = shares(amount, rows * top, most, lean, True), shares(amount, rows * top, most, lean, False)
    places = jnp.arange(amount)

    def named(sizes, rotation):
        used = int((sizes > 0).sum())
        fixed = max(1, used // 4)
        shifted = fixed + (places - fixed + rotation * (used - fixed)) % max(1, amount - fixed)
        return jnp.zeros((amount,), jnp.int32).at[ranking[jnp.where(places < fixed, places, shifted)]].set(jnp.asarray(sizes, jnp.int32))

    sizes = jnp.where(number % 4 == 0, named(packed, number // 4), named(common, number - number // 4 - 1))
    mixed = jax.random.permutation(jax.random.fold_in(own, 3), amount)
    source_of, taker = mixed[0:amount // 2 * 2:2], mixed[1:amount // 2 * 2:2]
    slack = jnp.minimum(sizes[source_of] - 1, most - sizes[taker]) // 2
    slack = jnp.where((source_of == ranking[0]) | (taker == ranking[0]) | (sizes[taker] == 0), 0, jnp.maximum(slack, 0))
    shifted = jax.random.randint(jax.random.fold_in(own, 4), (amount // 2,), 0, 1 << 20) % (slack + 1)
    sizes = sizes.at[source_of].add(-shifted).at[taker].add(shifted)
    items = jnp.searchsorted(jnp.cumsum(sizes), jnp.arange(rows * top), side="right").astype(jnp.int32)
    table = items.reshape(top, rows).T
    table = table[jax.random.permutation(jax.random.fold_in(own, 1), rows)]
    rotation = jax.random.randint(jax.random.fold_in(own, 2), (rows, 1), 0, top)
    return jnp.take_along_axis(table, (jnp.arange(top)[None, :] + rotation) % top, axis=1)


def shares(amount, total, bound, slope, full):
    portions = [(1 << 20) // math.isqrt(rank ** slope) + 1 for rank in range(1, amount + 1)]
    largest = bound if full else min(bound, max(-(-total // amount), total * portions[0] // sum(portions)))
    least = 1 if total - largest >= amount - 1 else 0
    given, rest = [largest] + [least] * (amount - 1), total - largest - least * (amount - 1)
    while rest > 0:
        candidates = [i for i in range(1, amount) if given[i] < largest] or [i for i in range(1, amount) if given[i] < bound]
        mass, budget = sum([portions[i] for i in candidates]), rest
        for i in candidates:
            addition = min(bound - given[i], max(1, budget * portions[i] // mass), rest)
            given[i] = given[i] + addition
            rest = rest - addition
    return np.array(given)


def normal_values(rng, dims, scale, bound, shards=(), held_as=jnp.bfloat16):
    level = levels(rng, dims, shards, -0.22, 0.18) if shards else 1.0
    drawn = jax.random.normal(rng, dims, jnp.float32) * scale * level
    return jnp.minimum(jnp.maximum(drawn, -bound), bound).astype(held_as)


def setup_inputs(seed: int = 0) -> dict:
    seeds = jax.random.split(jax.random.key(seed), 14)
    patches = normal_values(seeds[0], (TOKENS, D), 1.0, 6.0, ((0, 32),))
    cond = normal_values(seeds[1], (SLOTS, D), 1.0, 6.0, ((0, 32),))
    long_pack = set_ends(jax.random.randint(seeds[2], (PACKS,), 0, 2), jax.random.fold_in(seeds[2], 1), 0, 1).astype(jnp.int32)
    routes_keys = jax.random.split(jax.random.fold_in(seeds[3], 1), TOKENS // TOK_DEV)
    routes_turns = jax.random.permutation(jax.random.fold_in(seeds[3], 3), TOKENS // TOK_DEV)
    routes = jax.vmap(lambda own, number: shared_out(jax.random.fold_in(seeds[3], 2), own, number, TOK_DEV, EXPERTS, TOP, CAP, 1))(routes_keys, routes_turns).reshape((TOKENS, TOP))
    ada_weight = normal_values(seeds[4], (D, 6 * D), D ** -0.5, 0.21875, ((0, 4),))
    qkv_weight = normal_values(seeds[5], (D, 3 * D), D ** -0.5, 0.21875, ((0, 4),))
    out_weight = normal_values(seeds[6], (D, D), (D // 8) ** -0.5, 0.625, ((0, 4),))
    router_weight = normal_values(seeds[7], (D, EXPERTS), (2 * D) ** -0.5, 0.15625, ((0, 4),))
    shared_up = normal_values(seeds[8], (D, FF), D ** -0.5, 0.21875, ((0, 4),))
    shared_down = normal_values(seeds[9], (FF, D), FF ** -0.5, 0.109375, ((0, 4),))
    expert_up = normal_values(seeds[10], (EXPERTS, D, FF), D ** -0.5, 0.21875, ((0, 8), (1, 4)))
    expert_down = normal_values(seeds[11], (EXPERTS, FF, D), FF ** -0.5, 0.109375, ((0, 8), (1, 4)))
    out_grad = normal_values(seeds[12], (TOKENS, D), 1.0, 6.0, ((0, 32),))
    return {"patches": patches, "cond": cond, "long_pack": long_pack, "routes": routes, "ada_weight": ada_weight, "qkv_weight": qkv_weight, "out_weight": out_weight, "router_weight": router_weight, "shared_up": shared_up, "shared_down": shared_down, "expert_up": expert_up, "expert_down": expert_down, "out_grad": out_grad}


HIGHEST_PRECISION = lax.Precision.HIGHEST
EPSILON = 1e-06
MASKED = -1e+30

@jax.custom_vjp
def low(v):
    return lax.optimization_barrier(v.astype(jnp.bfloat16)).astype(jnp.float32)

@jax.custom_vjp
def low_back(v):
    return v

def low_keep(v):
    return (low(v), None)

def low_pass(kept, grad):
    return (grad,)

def back_keep(v):
    return (v, None)

def back_low(kept, grad):
    return (low(grad),)
low.defvjp(low_keep, low_pass)
low_back.defvjp(back_keep, back_low)

def dense(left_side, right_side):
    return jnp.dot(left_side, right_side, precision=HIGHEST_PRECISION)

def layer_norm(values):
    centre = values - lax.optimization_barrier(jnp.mean(values, axis=-1, keepdims=True))
    spread = lax.optimization_barrier(jnp.mean(centre * centre, axis=-1, keepdims=True))
    return centre * lax.rsqrt(spread + EPSILON)

def gelu_tanh(values):
    return jax.nn.gelu(values, approximate=True)

def slot_places(route_rows, expert_count, capacity):
    pair_ids = route_rows.reshape(-1).astype(jnp.int32)
    onehot = (pair_ids[:, None] == jnp.arange(expert_count, dtype=jnp.int32)[None, :]).astype(jnp.int32)
    rank_values = (jnp.cumsum(onehot, axis=0) - onehot).astype(jnp.int32)
    slot_index = lax.optimization_barrier(jnp.sum(rank_values * onehot, axis=1)).astype(jnp.int32)
    destinations = (pair_ids * capacity + slot_index).astype(jnp.int32)
    pair_count = pair_ids.shape[0]
    sources = jnp.full((expert_count * capacity,), pair_count, jnp.int32).at[destinations].set(jnp.arange(pair_count, dtype=jnp.int32))
    return (destinations, sources)

def to_units(flat, pack_count):
    length = flat.shape[0] // pack_count
    shaped = flat.reshape(pack_count, length, HEADS // 2, 2, HEAD)
    return jnp.transpose(shaped, (0, 2, 1, 3, 4)).reshape(-1, length, 2, HEAD)

def from_units(units, pack_count):
    length = units.shape[1]
    shaped = units.reshape(pack_count, HEADS // 2, length, 2, HEAD)
    return jnp.transpose(shaped, (0, 2, 1, 3, 4)).reshape(pack_count * length, HEADS * HEAD)

def attend_unit(block_unit):
    queries, keys, values, long_flag = block_unit
    length = queries.shape[0]
    position = jnp.arange(length, dtype=jnp.int32)
    image = jnp.where(long_flag == 1, 0, position // (length // 4))
    same = image[:, None] == image[None, :]
    scores = jnp.einsum('qhd,khd->hqk', queries, keys, precision=HIGHEST_PRECISION) * (1.0 / math.sqrt(HEAD))
    scores = jnp.where(same[None], low_back(scores), MASKED)
    summit = lax.optimization_barrier(jnp.max(scores, axis=-1, keepdims=True))
    weights = jnp.exp(scores - summit)
    probabilities = low(weights / lax.optimization_barrier(jnp.sum(weights, axis=-1, keepdims=True)))
    attended = jnp.einsum('hqk,khd->qhd', probabilities, values, precision=HIGHEST_PRECISION)
    return low(low_back(attended))

def expert_unit(block_unit):
    rows_in, weight_up, weight_down = block_unit
    expert_pre = low_back(dense(rows_in, weight_up))
    return low(low_back(dense(low(gelu_tanh(expert_pre)), weight_down)))

def forward(routes, long_pack, patches, cond, ada_weight, qkv_weight, out_weight, router_weight, shared_up, shared_down, expert_up, expert_down):
    pack_count = long_pack.shape[0]
    feature_rows = patches.shape[1]
    quarter = PACK // 4
    modulation = low_back(dense(low(jax.nn.silu(cond)), ada_weight))
    blocks = modulation.reshape(pack_count, 4, 6 * feature_rows)
    chosen = jnp.where((long_pack == 1)[:, None, None], blocks[:, :1, :], blocks)[:, :, None, :]
    shift_one, scale_one, gate_one, shift_two, scale_two, gate_two = [chosen[..., part_index * feature_rows:(part_index + 1) * feature_rows] for part_index in range(6)]
    tokens = patches.reshape(pack_count, 4, quarter, feature_rows)
    first_in = low(layer_norm(tokens) * (1.0 + scale_one) + shift_one).reshape(-1, feature_rows)
    joined = low(low_back(dense(first_in, qkv_weight)))
    queries, keys, values = [to_units(joined[:, part_index * feature_rows:(part_index + 1) * feature_rows], pack_count) for part_index in range(3)]
    long_flags = jnp.repeat(long_pack, HEADS // 2)
    attended = from_units(lax.map(jax.checkpoint(attend_unit), (queries, keys, values, long_flags)), pack_count)
    attention = low_back(dense(attended, out_weight)).reshape(pack_count, 4, quarter, feature_rows)
    middle = tokens + gate_one * attention
    second_in = low(layer_norm(middle) * (1.0 + scale_two) + shift_two).reshape(-1, feature_rows)
    shared_pre = low_back(dense(second_in, shared_up))
    shared = low_back(dense(low(gelu_tanh(shared_pre)), shared_down))
    logits = low_back(dense(second_in, router_weight))
    gate_values = jax.nn.softmax(jnp.take_along_axis(logits, routes, axis=1), axis=1)
    device_count = TOKENS // TOK_DEV
    destinations, sources = jax.vmap(lambda route_rows: slot_places(route_rows, EXPERTS, CAP))(routes.reshape(device_count, TOK_DEV, TOP))
    padded = jnp.concatenate([second_in.reshape(device_count, TOK_DEV, feature_rows), jnp.zeros((device_count, 1, feature_rows), jnp.float32)], axis=1)
    sent = jax.vmap(lambda rows_in, picks: rows_in[picks // TOP])(padded, sources)
    sent = low_back(sent).reshape(device_count, EXPERTS, CAP, feature_rows)
    by_expert = jnp.transpose(sent, (1, 0, 2, 3)).reshape(EXPERTS, device_count * CAP, feature_rows)
    returned = lax.map(jax.checkpoint(expert_unit), (by_expert, expert_up, expert_down))
    returned = jnp.transpose(returned.reshape(EXPERTS, device_count, CAP, feature_rows), (1, 0, 2, 3)).reshape(device_count, EXPERTS * CAP, feature_rows)
    expert_out = jax.vmap(lambda rows_in, picks: rows_in[picks])(returned, destinations).reshape(-1, TOP, feature_rows)
    mixture = shared + lax.optimization_barrier(jnp.sum(gate_values[:, :, None] * expert_out, axis=1))
    block_out = middle + gate_two * mixture.reshape(pack_count, 4, quarter, feature_rows)
    return block_out.reshape(-1, feature_rows)

def reference(patches, cond, long_pack, routes, ada_weight, qkv_weight, out_weight, router_weight, shared_up, shared_down, expert_up, expert_down, out_grad):
    floats = tuple((argument.astype(jnp.float32) for argument in (patches, cond, ada_weight, qkv_weight, out_weight, router_weight, shared_up, shared_down, expert_up, expert_down)))
    result, pullback = jax.vjp(partial(forward, routes, long_pack), *floats)
    grads = pullback(out_grad.astype(jnp.float32))
    return (result.astype(jnp.bfloat16), grads[0], grads[1], grads[2], grads[3], grads[4], grads[5], grads[6], grads[7], grads[8], grads[9])
```

```python
import math

import jax
import jax.numpy as jnp
from jax import lax
from jax.sharding import PartitionSpec as P

HEADS = 12
HEAD = 64
TOP = 2
CAP = 320


EPSILON = 1e-06
MASKED = -1e30
WIDE_TYPE = jnp.float32
NARROW_TYPE = jnp.bfloat16


def product_plain_operands(left_side, right_side):
    return jnp.dot(left_side, right_side, preferred_element_type=WIDE_TYPE)


def product_left_operand(left_side, right_side):
    return lax.dot_general(
        left_side, right_side, (((0,), (0,)), ((), ())), preferred_element_type=WIDE_TYPE
    )


def product_right_operand(left_side, right_side):
    return lax.dot_general(
        left_side, right_side, (((1,), (1,)), ((), ())), preferred_element_type=WIDE_TYPE
    )


def normalize(values):
    centre = values - jnp.mean(values, axis=-1, keepdims=True)
    spread = jnp.mean(centre * centre, axis=-1, keepdims=True)
    reciprocal = lax.rsqrt(spread + EPSILON)
    return (centre * reciprocal, reciprocal)


def normalize_back(gradient, normed, reciprocal):
    return reciprocal * (
        gradient
        - jnp.mean(gradient, axis=-1, keepdims=True)
        - normed * jnp.mean(gradient * normed, axis=-1, keepdims=True)
    )


def gelu_tanh(values):
    return jax.nn.gelu(values, approximate=True)


def gelu_back(values, gradient):
    return jax.vjp(gelu_tanh, values)[1](gradient)[0]


PLANE = ("expert", "stream")
CORE, SIDES = 2, (4, 1, 5)


def flip(value, mask):
    count = lax.axis_size(PLANE)
    return lax.ppermute(value, PLANE, [(index, index ^ mask) for index in range(count)])


def plane_gather(piece):
    me = lax.axis_index(PLANE)
    near = jnp.stack([piece] + [flip(piece, mask) for mask in SIDES])
    far = flip(near, CORE)
    result = jnp.zeros((8,) + piece.shape, piece.dtype)
    for place, mask in enumerate((0,) + SIDES):
        result = lax.dynamic_update_index_in_dim(result, near[place], me ^ mask, 0)
        result = lax.dynamic_update_index_in_dim(result, far[place], me ^ mask ^ CORE, 0)
    return result


def plane_scatter(parts):
    me = lax.axis_index(PLANE)
    chip_x, core, chip_y = me // 4, (me // 2) % 2, me % 2
    grid = parts.reshape((2, 2, 2) + parts.shape[1:])
    kept = lax.dynamic_index_in_dim(grid, core, 1, keepdims=False)
    sent = lax.dynamic_index_in_dim(grid, 1 - core, 1, keepdims=False)
    pair = kept.astype(WIDE_TYPE) + flip(sent, CORE).astype(WIDE_TYPE)
    pair = pair.reshape((4,) + parts.shape[1:])
    narrow = pair.astype(NARROW_TYPE)
    place = 2 * chip_x + chip_y
    total = lax.dynamic_index_in_dim(pair, place, 0, keepdims=False)
    for mask, other in ((4, 2), (1, 1), (5, 3)):
        piece = lax.dynamic_index_in_dim(narrow, place ^ other, 0, keepdims=False)
        total = total + flip(piece, mask).astype(WIDE_TYPE)
    return total


def slot_of_routes(route_rows, expert_count, capacity):
    pair_ids = route_rows.reshape(-1)
    onehot = (pair_ids[:, None] == jnp.arange(expert_count, dtype=jnp.int32)[None, :]).astype(
        jnp.int32
    )
    rank_values = jnp.cumsum(onehot, axis=0) - onehot
    slot_index = jnp.sum(rank_values * onehot, axis=1)
    return (pair_ids * capacity + slot_index).reshape(route_rows.shape)


def to_units(flat, pack_count):
    length = flat.shape[0] // pack_count
    shaped = flat.reshape(pack_count, length, HEADS // 2, 2, HEAD)
    return jnp.transpose(shaped, (0, 2, 1, 3, 4)).reshape(-1, length, 2, HEAD)


def from_units(units, pack_count):
    length = units.shape[1]
    shaped = units.reshape(pack_count, HEADS // 2, length, 2, HEAD)
    return jnp.transpose(shaped, (0, 2, 1, 3, 4)).reshape(pack_count * length, HEADS * HEAD)


def masked_scores(queries, keys, long_flag):
    length = queries.shape[0]
    position = jnp.arange(length, dtype=jnp.int32)
    image = jnp.where(long_flag == 1, 0, position // (length // 4))
    same = image[:, None] == image[None, :]
    scores = jnp.einsum("qhd,khd->hqk", queries, keys, preferred_element_type=WIDE_TYPE) * (
        1.0 / math.sqrt(HEAD)
    )
    return jnp.where(same[None], scores, MASKED)


def attend_forward(block_unit):
    queries, keys, values, long_flag = block_unit
    scores = masked_scores(queries, keys, long_flag)
    summit = jnp.max(scores, axis=-1, keepdims=True)
    weights = jnp.exp(scores - summit)
    row_total = jnp.sum(weights, axis=-1, keepdims=True)
    probabilities = (weights / row_total).astype(NARROW_TYPE)
    attended = jnp.einsum("hqk,khd->qhd", probabilities, values, preferred_element_type=WIDE_TYPE)
    return (attended.astype(NARROW_TYPE), summit[..., 0] + jnp.log(row_total[..., 0]))


def attend_backward(block_unit):
    queries, keys, values, long_flag, log_total, grad_attended = block_unit
    scale_factor = 1.0 / math.sqrt(HEAD)
    scores = masked_scores(queries, keys, long_flag)
    probabilities = jnp.exp(scores - log_total[..., None])
    grad_values = jnp.einsum(
        "hqk,qhd->khd",
        probabilities.astype(NARROW_TYPE),
        grad_attended,
        preferred_element_type=WIDE_TYPE,
    )
    grad_probs = jnp.einsum("qhd,khd->hqk", grad_attended, values, preferred_element_type=WIDE_TYPE)
    centre = jnp.sum(probabilities * grad_probs, axis=-1, keepdims=True)
    grad_scores = (probabilities * (grad_probs - centre)).astype(NARROW_TYPE)
    grad_queries = (
        jnp.einsum("hqk,khd->qhd", grad_scores, keys, preferred_element_type=WIDE_TYPE)
        * scale_factor
    )
    grad_keys = (
        jnp.einsum("hqk,qhd->khd", grad_scores, queries, preferred_element_type=WIDE_TYPE)
        * scale_factor
    )
    return (grad_queries, grad_keys, grad_values)


def on_device(
    patches,
    cond,
    long_pack,
    routes,
    ada_weight,
    qkv_weight,
    out_weight,
    router_weight,
    shared_up,
    shared_down,
    expert_up,
    expert_down,
    out_grad,
):
    row_count, width = patches.shape
    pack_count = long_pack.shape[0]
    quarter = row_count // (4 * pack_count)
    hidden = shared_up.shape[1]
    depth = lax.axis_size("dp")
    experts = lax.axis_size(PLANE)
    capacity = CAP
    slots = experts * capacity
    local = qkv_weight.shape[0]
    slice_rows = local // experts
    plane_index = lax.axis_index(PLANE)

    def own(rows):
        return lax.dynamic_slice_in_dim(rows, plane_index * slice_rows, slice_rows, 0)

    down_rows = lax.dynamic_slice_in_dim(
        shared_down.reshape(4, local, width), plane_index * slice_rows, slice_rows, 1
    )
    first_group = lax.all_gather(own(qkv_weight), "dp", axis=0)
    second_group = lax.all_gather(
        jnp.concatenate(
            [
                own(out_weight),
                own(shared_up),
                jnp.transpose(down_rows, (1, 0, 2)).reshape(slice_rows, 4 * width),
                jnp.pad(own(router_weight), ((0, 0), (0, 128 - router_weight.shape[1]))),
            ],
            axis=1,
        ),
        "dp",
        axis=0,
    )

    def whole(group):
        gathered = plane_gather(group)
        return jnp.transpose(gathered, (1, 0, 2, 3)).reshape(width, -1)

    cond_wide = cond.astype(WIDE_TYPE)
    silu_cond = jax.nn.silu(cond_wide).astype(NARROW_TYPE)
    cond_rows = silu_cond.shape[0]
    silu_parts = lax.all_to_all(
        jnp.transpose(silu_cond.reshape(cond_rows, depth, local), (1, 0, 2)),
        "dp",
        split_axis=0,
        concat_axis=0,
        tiled=True,
    ).reshape(depth * cond_rows, local)
    partial = product_plain_operands(silu_parts, ada_weight)
    modulation = jnp.sum(
        lax.all_to_all(
            partial.reshape(depth, cond_rows, 6 * width), "dp", split_axis=0, concat_axis=0, tiled=True
        ),
        axis=0,
    )
    blocks = modulation.reshape(pack_count, 4, 6 * width)
    is_long = (long_pack == 1)[:, None, None]
    chosen = jnp.where(is_long, blocks[:, :1, :], blocks)[:, :, None, :]
    shift_one, scale_one, gate_one, shift_two, scale_two, gate_two = [
        chosen[..., part_index * width : (part_index + 1) * width] for part_index in range(6)
    ]

    places = slot_of_routes(routes, experts, capacity)
    slot_ids = jnp.arange(slots, dtype=jnp.int32)
    take_one = places[:, 0][:, None] == slot_ids[None, :]
    take_two = places[:, 1][:, None] == slot_ids[None, :]
    spread = jnp.logical_or(
        slot_ids[:, None] == places[:, 0][None, :], slot_ids[:, None] == places[:, 1][None, :]
    ).astype(NARROW_TYPE)

    def exchange(rows):
        return lax.all_to_all(
            rows.reshape((experts, capacity) + rows.shape[1:]),
            PLANE,
            split_axis=0,
            concat_axis=0,
            tiled=True,
        ).reshape(rows.shape)

    grad_out = out_grad.astype(WIDE_TYPE).reshape(pack_count, 4, quarter, width)
    grad_mixture = (grad_out * gate_two).reshape(row_count, width)
    grad_shared = grad_mixture.astype(NARROW_TYPE)
    mixture_rows = exchange(product_plain_operands(spread, grad_shared).astype(NARROW_TYPE))

    qkv_full = whole(first_group)
    tokens = patches.astype(WIDE_TYPE).reshape(pack_count, 4, quarter, width)
    normed_one, recip_one = normalize(tokens)
    first_in = (
        (normed_one * (1.0 + scale_one) + shift_one).astype(NARROW_TYPE).reshape(row_count, width)
    )
    joined = product_plain_operands(first_in, qkv_full).astype(NARROW_TYPE)
    queries, keys, values = [
        to_units(joined[:, part_index * width : (part_index + 1) * width], pack_count)
        for part_index in range(3)
    ]
    long_flags = jnp.repeat(long_pack, HEADS // 2)
    attended_units, log_total = lax.map(attend_forward, (queries, keys, values, long_flags))
    attended = from_units(attended_units, pack_count)
    rest = whole(second_group)
    out_full = rest[:, :width]
    up_full = rest[:, width : width + hidden]
    down_full = jnp.transpose(
        rest[:, width + hidden : width + 2 * hidden].reshape(depth, local, 4, width), (0, 2, 1, 3)
    ).reshape(hidden, width)
    router_full = rest[:, width + 2 * hidden : width + 2 * hidden + experts]
    attention = product_plain_operands(attended, out_full).reshape(pack_count, 4, quarter, width)
    middle = tokens + gate_one * attention
    normed_two, recip_two = normalize(middle)
    second_in = (
        (normed_two * (1.0 + scale_two) + shift_two).astype(NARROW_TYPE).reshape(row_count, width)
    )
    logits = product_plain_operands(second_in, router_full)
    onehot = (routes[:, :, None] == jnp.arange(experts, dtype=jnp.int32)[None, None, :]).astype(
        WIDE_TYPE
    )
    picked = jnp.sum(onehot * logits[:, None, :], axis=2)
    gate_values = jax.nn.softmax(picked, axis=1)
    slot_gates = jnp.sum(
        jnp.where(take_one, gate_values[:, :1], 0.0) + jnp.where(take_two, gate_values[:, 1:], 0.0),
        axis=0,
    )
    gates_there = exchange(slot_gates)
    expert_rows = exchange(product_plain_operands(spread, second_in).astype(NARROW_TYPE))

    expert_up_full = lax.all_gather(expert_up[0], "dp", axis=0, tiled=True)
    expert_down_full = lax.all_gather(expert_down[0], "dp", axis=0, tiled=True)
    expert_pre = product_plain_operands(expert_rows, expert_up_full)
    expert_hidden = gelu_tanh(expert_pre).astype(NARROW_TYPE)
    result_rows = product_plain_operands(expert_hidden, expert_down_full).astype(NARROW_TYPE)
    wide_rows = mixture_rows.astype(WIDE_TYPE)
    gate_dots = jnp.sum(result_rows.astype(WIDE_TYPE) * wide_rows, axis=1)
    expert_grad = (gates_there[:, None] * wide_rows).astype(NARROW_TYPE)
    grad_expert_pre = gelu_back(
        expert_pre, product_right_operand(expert_grad, expert_down_full)
    ).astype(NARROW_TYPE)
    grad_rows = product_right_operand(grad_expert_pre, expert_up_full).astype(NARROW_TYPE)
    grad_rows_back = exchange(grad_rows)
    gate_dots_back = exchange(gate_dots)
    result_back = exchange(result_rows)
    grad_expert_up = product_left_operand(expert_rows, grad_expert_pre)
    grad_expert_down = product_left_operand(expert_hidden, expert_grad)
    expert_up_grad = lax.psum_scatter(
        grad_expert_up.astype(NARROW_TYPE), "dp", scatter_dimension=0, tiled=True
    ).astype(WIDE_TYPE)[None]
    expert_down_grad = lax.psum_scatter(
        grad_expert_down.astype(NARROW_TYPE), "dp", scatter_dimension=0, tiled=True
    ).astype(WIDE_TYPE)[None]

    shared_pre = product_plain_operands(second_in, up_full)
    shared_hidden = gelu_tanh(shared_pre).astype(NARROW_TYPE)
    shared = product_plain_operands(shared_hidden, down_full)
    grad_shared_pre = gelu_back(shared_pre, product_right_operand(grad_shared, down_full)).astype(
        NARROW_TYPE
    )
    grad_up = product_left_operand(grad_shared_pre, second_in).astype(NARROW_TYPE)
    grad_down = product_left_operand(grad_shared, shared_hidden).astype(NARROW_TYPE)
    middle_parts = jnp.concatenate(
        [
            grad_up.reshape(experts, hidden // experts, width),
            jnp.transpose(
                grad_down.reshape(experts, width // experts, 4, hidden // 4), (0, 2, 1, 3)
            ).reshape(experts, 4 * width // experts, hidden // 4),
        ],
        axis=1,
    )
    middle_sum = plane_scatter(middle_parts).astype(NARROW_TYPE)
    up_sum = middle_sum[: hidden // experts].T
    down_sum = jnp.transpose(
        middle_sum[hidden // experts :].reshape(4, width // experts, hidden // 4), (0, 2, 1)
    ).reshape(hidden, width // experts)
    down_sum = jnp.transpose(
        down_sum.reshape(depth, 4, local, width // experts), (0, 2, 1, 3)
    ).reshape(width, 4 * width // experts)
    middle_final = lax.psum_scatter(
        jnp.concatenate([up_sum, down_sum], axis=1), "dp", scatter_dimension=0, tiled=True
    ).astype(WIDE_TYPE)
    shared_up_grad = middle_final[:, : hidden // experts]
    shared_down_grad = jnp.transpose(
        middle_final[:, hidden // experts :].reshape(local, 4, width // experts), (1, 0, 2)
    ).reshape(4 * local, width // experts)

    grad_gate = jnp.stack(
        [
            jnp.sum(jnp.where(take_one, gate_dots_back[None, :], 0.0), axis=1),
            jnp.sum(jnp.where(take_two, gate_dots_back[None, :], 0.0), axis=1),
        ],
        axis=1,
    )
    grad_picked = gate_values * (
        grad_gate - jnp.sum(gate_values * grad_gate, axis=1, keepdims=True)
    )
    grad_logits = jnp.sum(onehot * grad_picked[:, :, None], axis=1).astype(NARROW_TYPE)
    grad_router = product_left_operand(grad_logits, second_in)
    collect = jnp.logical_or(take_one, take_two).astype(NARROW_TYPE)
    grad_second = (
        product_right_operand(grad_shared_pre, up_full)
        + product_right_operand(grad_logits, router_full)
        + product_plain_operands(collect, grad_rows_back)
    )

    mixture = (
        shared
        + gate_values[:, :1] * product_plain_operands(take_one.astype(NARROW_TYPE), result_back)
        + gate_values[:, 1:] * product_plain_operands(take_two.astype(NARROW_TYPE), result_back)
    )
    mixture_blocks = mixture.reshape(pack_count, 4, quarter, width)
    block_out = (middle + gate_two * mixture_blocks).reshape(row_count, width).astype(NARROW_TYPE)
    grad_gate_two = jnp.sum(grad_out * mixture_blocks, axis=2)

    grad_second_blocks = grad_second.reshape(pack_count, 4, quarter, width)
    grad_shift_two = jnp.sum(grad_second_blocks, axis=2)
    grad_scale_two = jnp.sum(grad_second_blocks * normed_two, axis=2)
    grad_middle = grad_out + normalize_back(
        grad_second_blocks * (1.0 + scale_two), normed_two, recip_two
    )
    grad_gate_one = jnp.sum(grad_middle * attention, axis=2)
    grad_attention = (grad_middle * gate_one).reshape(row_count, width).astype(NARROW_TYPE)
    grad_out_weight = product_left_operand(grad_attention, attended)
    grad_attended = product_right_operand(grad_attention, out_full).astype(NARROW_TYPE)
    grad_units = to_units(grad_attended, pack_count)
    grad_queries, grad_keys, grad_values = lax.map(
        attend_backward, (queries, keys, values, long_flags, log_total, grad_units)
    )
    grad_joined = jnp.concatenate(
        [
            from_units(grad_queries, pack_count),
            from_units(grad_keys, pack_count),
            from_units(grad_values, pack_count),
        ],
        axis=1,
    ).astype(NARROW_TYPE)
    grad_qkv = product_left_operand(grad_joined, first_in)
    last_parts = jnp.concatenate(
        [
            grad_qkv.astype(NARROW_TYPE).reshape(experts, 3 * width // experts, width),
            grad_out_weight.astype(NARROW_TYPE).reshape(experts, width // experts, width),
            jnp.pad(grad_router.astype(NARROW_TYPE)[:, None, :], ((0, 0), (0, 15), (0, 0))),
        ],
        axis=1,
    )
    last_sum = plane_scatter(last_parts).astype(NARROW_TYPE)
    last_final = lax.psum_scatter(last_sum.T, "dp", scatter_dimension=0, tiled=True).astype(
        WIDE_TYPE
    )
    edge_one, edge_two = 3 * width // experts, 4 * width // experts
    qkv_weight_grad = last_final[:, :edge_one]
    out_weight_grad = last_final[:, edge_one:edge_two]
    router_weight_grad = last_final[:, edge_two : edge_two + 1]

    grad_first = product_right_operand(grad_joined, qkv_full).reshape(
        pack_count, 4, quarter, width
    )
    grad_shift_one = jnp.sum(grad_first, axis=2)
    grad_scale_one = jnp.sum(grad_first * normed_one, axis=2)
    patches_grad = (
        grad_middle + normalize_back(grad_first * (1.0 + scale_one), normed_one, recip_one)
    ).reshape(row_count, width)
    grad_chosen = jnp.concatenate(
        [
            grad_shift_one,
            grad_scale_one,
            grad_gate_one,
            grad_shift_two,
            grad_scale_two,
            grad_gate_two,
        ],
        axis=-1,
    )
    long_total = jnp.sum(grad_chosen, axis=1, keepdims=True)
    first_slot = (jnp.arange(4, dtype=jnp.int32) == 0)[None, :, None]
    grad_blocks = jnp.where(is_long, jnp.where(first_slot, long_total, 0.0), grad_chosen)
    grad_modulation = grad_blocks.reshape(cond_rows, 6 * width).astype(NARROW_TYPE)
    grad_all = lax.all_gather(grad_modulation, "dp", axis=0, tiled=True)
    silu_parts_grad = lax.all_to_all(
        product_right_operand(grad_all, ada_weight).reshape(depth, cond_rows, local),
        "dp",
        split_axis=0,
        concat_axis=0,
        tiled=True,
    )
    grad_silu = jnp.transpose(silu_parts_grad, (1, 0, 2)).reshape(cond_rows, width)
    cond_grad = jax.vjp(jax.nn.silu, cond_wide)[1](grad_silu)[0]
    silu_all = lax.all_gather(silu_parts, PLANE, axis=0, tiled=True)
    grad_columns = lax.all_to_all(
        jnp.transpose(
            grad_all.reshape(depth * cond_rows, experts, 6 * width // experts), (1, 0, 2)
        ),
        PLANE,
        split_axis=0,
        concat_axis=0,
        tiled=True,
    ).reshape(experts * depth * cond_rows, 6 * width // experts)
    ada_weight_grad = product_left_operand(silu_all, grad_columns)
    return (
        block_out,
        patches_grad,
        cond_grad,
        ada_weight_grad,
        qkv_weight_grad,
        out_weight_grad,
        router_weight_grad,
        shared_up_grad,
        shared_down_grad,
        expert_up_grad,
        expert_down_grad,
    )


def solution(mesh):
    in_specs = (
        P(("dp", "expert", "stream"), None),
        P(("dp", "expert", "stream"), None),
        P(("dp", "expert", "stream")),
        P(("dp", "expert", "stream"), None),
        P("dp", None),
        P("dp", None),
        P("dp", None),
        P("dp", None),
        P("dp", None),
        P("dp", None),
        P(("expert", "stream"), "dp", None),
        P(("expert", "stream"), "dp", None),
        P(("dp", "expert", "stream"), None),
    )
    out_specs = (
        P(("dp", "expert", "stream"), None),
        P(("dp", "expert", "stream"), None),
        P(("dp", "expert", "stream"), None),
        P("dp", ("expert", "stream")),
        P("dp", ("expert", "stream")),
        P("dp", ("expert", "stream")),
        P("dp", ("expert", "stream")),
        P("dp", ("expert", "stream")),
        P("dp", ("expert", "stream")),
        P(("expert", "stream"), "dp", None),
        P(("expert", "stream"), "dp", None),
    )
    return jax.shard_map(
        on_device, mesh=mesh, in_specs=in_specs, out_specs=out_specs, check_vma=False
    )
```

```python
import functools
import math

import jax
import jax.numpy as jnp
from jax import lax
from jax.experimental import pallas as pl
from jax.experimental.pallas import tpu as pltpu
from jax.sharding import PartitionSpec as P

HEAD = 64
TOP = 2
CAP = 320
SPARE = 16


EPSILON = 1e-06
ROOT = math.sqrt(2.0 / math.pi)
CUBE = 0.044715 * ROOT
MEBI = 1 << 20
WIDE_TYPE = jnp.float32
NARROW_TYPE = jnp.bfloat16


def product_plain_operands(left_side, right_side):
    return jnp.dot(left_side, right_side, preferred_element_type=WIDE_TYPE)


def product_left_operand(left_side, right_side):
    return lax.dot_general(
        left_side, right_side, (((0,), (0,)), ((), ())), preferred_element_type=WIDE_TYPE
    )


def product_right_operand(left_side, right_side):
    return lax.dot_general(
        left_side, right_side, (((1,), (1,)), ((), ())), preferred_element_type=WIDE_TYPE
    )


def contract(left_side, right_side, left_dim, right_dim):
    return lax.dot_general(
        left_side, right_side, (((left_dim,), (right_dim,)), ((), ())), preferred_element_type=WIDE_TYPE
    )

def attend_rows(joined_ref, attended_ref, total_ref, head, rows, columns):
    lanes = slice(head * HEAD, (head + 1) * HEAD)
    queries = joined_ref[0, rows, lanes] * (1.0 / 8.0)
    keys = joined_ref[1, columns, lanes]
    values = joined_ref[2, columns, lanes]
    scores = contract(queries.astype(NARROW_TYPE), keys, 1, 1)
    summit = jnp.max(scores, axis=1, keepdims=True)
    weights = jnp.exp(scores - summit)
    row_total = jnp.sum(weights, axis=1, keepdims=True)
    probabilities = (weights * (1.0 / row_total)).astype(NARROW_TYPE)
    attended_ref[rows, lanes] = contract(probabilities, values, 1, 0).astype(NARROW_TYPE)
    total_ref[rows, lanes] = jnp.broadcast_to(summit + jnp.log(row_total), (scores.shape[0], HEAD))

def attend_kernel(long_ref, joined_ref, attended_ref, total_ref):
    length = joined_ref.shape[1]
    quarter = length // 4
    for whole in (True, False):
        @pl.when((long_ref[0] == 1) == whole)
        def _():
            for head in range(2):
                for part in range(4):
                    rows = slice(part * quarter, (part + 1) * quarter)
                    attend_rows(joined_ref, attended_ref, total_ref, head, rows, slice(None) if whole else rows)

def attend(long_pack, joined):
    three, length, width = joined.shape
    return pl.pallas_call(
        attend_kernel,
        grid=(width // 128,),
        in_specs=[pl.BlockSpec(memory_space=pltpu.SMEM), pl.BlockSpec((3, length, 128), lambda pair: (0, 0, pair))],
        out_specs=[pl.BlockSpec((length, 128), lambda pair: (0, pair))] * 2,
        out_shape=[jax.ShapeDtypeStruct((length, width), NARROW_TYPE), jax.ShapeDtypeStruct((length, width), WIDE_TYPE)],
        compiler_params=pltpu.CompilerParams(vmem_limit_bytes=56 * MEBI),
        name="attend",
    )(long_pack, joined)

def attend_back_rows(joined_ref, total_ref, grad_ref, out_ref, keys_acc, values_acc, head, rows, columns):
    lanes = slice(head * HEAD, (head + 1) * HEAD)
    queries = joined_ref[0, rows, lanes]
    scaled = (queries * (1.0 / 8.0)).astype(NARROW_TYPE)
    keys = joined_ref[1, columns, lanes]
    values = joined_ref[2, columns, lanes]
    grads = grad_ref[rows, lanes]
    scores = contract(scaled, keys, 1, 1)
    probabilities = jnp.exp(scores - total_ref[rows, head * HEAD : head * HEAD + 1])
    grad_probs = contract(grads, values, 1, 1)
    product = probabilities * grad_probs
    centre = jnp.sum(product, axis=1, keepdims=True)
    grad_scores = (product - probabilities * centre).astype(NARROW_TYPE)
    out_ref[0, rows, lanes] = (contract(grad_scores, keys, 1, 0) * (1.0 / 8.0)).astype(NARROW_TYPE)
    keys_acc[lanes, columns] += contract(scaled.T, grad_scores, 1, 0)
    values_acc[lanes, columns] += contract(grads.T, probabilities.astype(NARROW_TYPE), 1, 0)

def attend_back_kernel(long_ref, joined_ref, total_ref, grad_ref, *refs):
    out_ref, keys_acc, values_acc = refs[-3:]
    length = joined_ref.shape[1]
    quarter = length // 4
    keys_acc[...] = jnp.zeros_like(keys_acc)
    values_acc[...] = jnp.zeros_like(values_acc)
    for whole in (True, False):
        @pl.when((long_ref[0] == 1) == whole)
        def _():
            for head in range(2):
                for part in range(4):
                    rows = slice(part * quarter, (part + 1) * quarter)
                    attend_back_rows(joined_ref, total_ref, grad_ref, out_ref, keys_acc, values_acc, head, rows, slice(None) if whole else rows)
    out_ref[1] = keys_acc[...].T.astype(NARROW_TYPE)
    out_ref[2] = values_acc[...].T.astype(NARROW_TYPE)

def attend_back(long_pack, joined, total, grad, after):
    three, length, width = joined.shape
    wide = pl.BlockSpec((3, length, 128), lambda pair: (0, 0, pair))
    flat = pl.BlockSpec((length, 128), lambda pair: (0, pair))
    return pl.pallas_call(
        attend_back_kernel,
        grid=(width // 128,),
        in_specs=[pl.BlockSpec(memory_space=pltpu.SMEM), wide, flat, flat]
        + [pl.BlockSpec(memory_space=pl.ANY)] * len(after),
        out_specs=wide,
        out_shape=jax.ShapeDtypeStruct((3, length, width), NARROW_TYPE),
        scratch_shapes=[pltpu.VMEM((128, length), WIDE_TYPE)] * 2,
        compiler_params=pltpu.CompilerParams(vmem_limit_bytes=56 * MEBI),
        name="attend_back",
    )(long_pack, joined, total, grad, *after)


def gelu_pair(values):
    square = values * values
    half = 0.5 * jnp.tanh(values * (CUBE * square + ROOT)) + 0.5
    result = values * half
    slope = half + result * (1.0 - half) * (6.0 * CUBE * square + 2.0 * ROOT)
    return result, slope


def expert_block(rows, grads, up, down):
    hidden, slope = gelu_pair(contract(rows, up, 1, 0))
    grad_pre = slope * contract(grads, down, 1, 1)
    return hidden.astype(NARROW_TYPE), grad_pre.astype(NARROW_TYPE)


def routed_kernel(
    rows_ref, grad_ref, gate_ref, weight_ref, out_ref, back_ref, dots_ref, hidden_ref, grad_pre_ref
):
    width = rows_ref.shape[1]
    count = weight_ref.shape[1] // (2 * width)
    rows = rows_ref[...]
    cotangent = grad_ref[...].astype(WIDE_TYPE)
    grads = (gate_ref[...] * cotangent).astype(NARROW_TYPE)
    out = jnp.zeros(rows.shape, WIDE_TYPE)
    back = jnp.zeros(rows.shape, WIDE_TYPE)
    for block in range(count):
        units = slice(block * width, (block + 1) * width)
        up = weight_ref[:, units]
        down = weight_ref[:, (count + block) * width : (count + block + 1) * width]
        hidden, grad_pre = expert_block(rows, grads, up, down)
        hidden_ref[:, units] = hidden
        grad_pre_ref[:, units] = grad_pre
        out += contract(hidden, down, 1, 0)
        back += contract(grad_pre, up, 1, 1)
    out = out.astype(NARROW_TYPE).astype(WIDE_TYPE)
    out_ref[...] = (gate_ref[...] * out).astype(NARROW_TYPE)
    back_ref[...] = back.astype(NARROW_TYPE)
    dots_ref[...] = jnp.sum(out * cotangent, axis=1, keepdims=True)


def routed_expert(rows, grads, gates, weights, after, block=512):
    count, width = rows.shape
    hidden = weights.shape[1] // 2
    narrow = jax.ShapeDtypeStruct((count, width), NARROW_TYPE)
    units = jax.ShapeDtypeStruct((count, hidden), NARROW_TYPE)
    return stepped(
        routed_kernel,
        count // block,
        (rows, grads, gates, weights),
        [row_block(block, width), row_block(block, width), row_block(block, 1), whole_block(weights)],
        [row_block(block, width), row_block(block, width), row_block(block, 1)]
        + [row_block(block, hidden)] * 2,
        [narrow, narrow, jax.ShapeDtypeStruct((count, 1), WIDE_TYPE), units, units],
        after,
        "routed_expert",
    )


def sums_kernel(
    steps, rows_ref, grad_ref, gate_ref, hidden_ref, grad_pre_ref, sums_ref, totals
):
    step = pl.program_id(0)
    width = rows_ref.shape[1]
    count = totals.shape[0] // 2

    @pl.when(step == 0)
    def _():
        totals[...] = jnp.zeros_like(totals)

    @pl.when(step < steps)
    def _():
        turned = rows_ref[...].T
        grads = (gate_ref[...] * grad_ref[...].astype(WIDE_TYPE)).astype(NARROW_TYPE)
        for block in range(count):
            units = slice(block * width, (block + 1) * width)
            totals[block] += contract(turned, grad_pre_ref[:, units], 1, 0)
            totals[count + block] += contract(hidden_ref[:, units], grads, 0, 0)

    @pl.when(step >= steps)
    def _():
        sums_ref[...] = totals[jnp.maximum(step - steps, 0)].astype(NARROW_TYPE)


def routed_sums(rows, grads, gates, hidden, grad_pre, side, after, block=512):
    total_rows, width = rows.shape
    half = hidden.shape[1] // 2
    count = half // width
    steps = total_rows // block

    def spec(columns, place):
        return pl.BlockSpec((block, columns), lambda step: (jnp.minimum(step, steps - 1), place))

    square = (width, width)
    return stepped(
        functools.partial(sums_kernel, steps),
        steps + 2 * count,
        (rows, grads, gates, hidden, grad_pre),
        [spec(width, 0), spec(width, 0), spec(1, 0), spec(half, side), spec(half, side)],
        pl.BlockSpec(square, lambda step: (0, jnp.maximum(step - steps, 0))),
        jax.ShapeDtypeStruct((width, 2 * half), NARROW_TYPE),
        after,
        "routed_sums",
        scratch_shapes=[pltpu.VMEM((2 * count,) + square, WIDE_TYPE)],
    )


def part_of_step(core, place):
    chip = lax.rem(place, 4)
    owner = jnp.where(place < 4, core, 1 - core)
    return 4 * (chip // 2) + 2 * owner + lax.rem(chip, 2)


def shared_kernel(
    local, steps, core_ref, rows_ref, grad_ref, up_ref, down_ref, out_ref, back_ref, kept_ref, sent_ref, totals
):
    step = pl.program_id(0)
    width = rows_ref.shape[1]
    count = totals.shape[0] // 2

    @pl.when(step == 0)
    def _():
        totals[...] = jnp.zeros_like(totals)

    @pl.when(step < steps)
    def _():
        rows, grads = rows_ref[...], grad_ref[...]
        turned = grads.T
        out = jnp.zeros(rows.shape, WIDE_TYPE)
        back = jnp.zeros(rows.shape, WIDE_TYPE)
        for block in range(count):
            units = slice(block * width, (block + 1) * width)
            up, down = up_ref[:, units], down_ref[:, units]
            hidden, grad_pre = expert_block(rows, grads, up, down)
            out += contract(hidden, down, 1, 0)
            back += contract(grad_pre, up, 1, 1)
            totals[block] += contract(grad_pre, rows, 0, 0)
            totals[count + block] += contract(turned, hidden, 1, 0)
        out_ref[...] = out
        back_ref[...] = back

    units = count * width // 8
    features = width // 8
    part = part_of_step(core_ref[0], jnp.maximum(step - steps, 0))

    def write(part_ref):
        for piece in range(units // local):
            number = part * (units // local) + piece
            start = pl.multiple_of((number // count) * local, 8)
            part_ref[0, piece * local : (piece + 1) * local] = totals[
                lax.rem(number, count), pl.ds(start, local)
            ].astype(NARROW_TYPE)
        for block in range(count):
            start = units + block * features
            part_ref[0, start : start + features] = totals[
                count + block, pl.ds(pl.multiple_of(part * features, 8), features)
            ].astype(NARROW_TYPE)

    @pl.when(jnp.logical_and(step >= steps, step < steps + 4))
    def _():
        write(kept_ref)

    @pl.when(step >= steps + 4)
    def _():
        write(sent_ref)


def part_specs(steps, rows, width):
    return [
        pl.BlockSpec((1, rows, width), lambda step, *_: (jnp.clip(step - steps, 0, 3), 0, 0)),
        pl.BlockSpec((1, rows, width), lambda step, *_: (jnp.clip(step - steps - 4, 0, 3), 0, 0)),
    ]


def own_core():
    return ((lax.axis_index(PLANE) // 2) % 2).reshape(1).astype(jnp.int32)


def shared_expert(rows, grads, weights, local, after, row_block=512):
    total_rows, width = rows.shape
    steps = total_rows // row_block
    count = 4
    row_spec = pl.BlockSpec((row_block, width), lambda step, core: (jnp.minimum(step, steps - 1), 0))

    def held(place):
        return pl.BlockSpec(
            (width, count * width), lambda step, core: (0, place), pipeline_mode=pl.Buffered(1)
        )

    def kernel(*refs):
        shared_kernel(local, steps, *refs[:5], *refs[5 + len(after) :])

    wide = jax.ShapeDtypeStruct((total_rows, width), WIDE_TYPE)
    return pl.pallas_call(
        kernel,
        grid_spec=pltpu.PrefetchScalarGridSpec(
            num_scalar_prefetch=1,
            grid=(steps + 8,),
            in_specs=[row_spec, row_spec, held(0), held(1)] + [ANYWHERE] * len(after),
            out_specs=[row_spec, row_spec] + part_specs(steps, width, width),
            scratch_shapes=[pltpu.VMEM((2 * count, width, width), WIDE_TYPE)],
        ),
        out_shape=[wide, wide] + [jax.ShapeDtypeStruct((4, width, width), NARROW_TYPE)] * 2,
        compiler_params=pltpu.CompilerParams(vmem_limit_bytes=60 * MEBI),
        name="shared_expert",
    )(own_core(), rows, grads, weights, weights, *after)


PLANE = ("expert", "stream")
CORE, SIDES = 2, (4, 1, 5)


def flip(value, mask):
    count = lax.axis_size(PLANE)
    return lax.ppermute(value, PLANE, [(index, index ^ mask) for index in range(count)])


def together(*values):
    return lax.optimization_barrier(values)


ANYWHERE = pl.BlockSpec(memory_space=pl.ANY)


def whole_block(operand):
    rank = len(operand.shape)
    return pl.BlockSpec(operand.shape, lambda *_: (0,) * rank, pipeline_mode=pl.Buffered(1))


def row_block(rows, columns):
    return pl.BlockSpec((rows, columns), lambda step, *_: (step, 0))


def column_block(operand, columns, place):
    return pl.BlockSpec(
        (operand.shape[0], columns), lambda step, *_: (0, place), pipeline_mode=pl.Buffered(1)
    )


def stepped(kernel, steps, operands, in_specs, out_specs, out_shape, after, name, **extra):
    given = len(operands)

    def body(*refs):
        kernel(*refs[:given], *refs[given + len(after) :])

    return pl.pallas_call(
        body,
        grid=(steps,),
        in_specs=list(in_specs) + [ANYWHERE] * len(after),
        out_specs=out_specs,
        out_shape=out_shape,
        compiler_params=pltpu.CompilerParams(vmem_limit_bytes=58 * MEBI),
        name=name,
        **extra,
    )(*operands, *after)


def depth_stack(piece):
    parts = jnp.broadcast_to(piece[None], (lax.axis_size("dp"),) + piece.shape)
    return lax.all_to_all(parts, "dp", split_axis=0, concat_axis=0, tiled=True)


def stack_kernel(*refs):
    for place, ref in enumerate(refs[:-1]):
        refs[-1][place] = ref[...]


def place_kernel(order_ref, near_ref, far_ref, out_ref):
    for place in range(4):
        chip = order_ref[place]
        first = 4 * (chip // 2) + lax.rem(chip, 2)
        out_ref[0, first + 2 * order_ref[4]] = near_ref[place, 0]
        out_ref[0, first + 2 * (1 - order_ref[4])] = far_ref[place, 0]


def side_gather(stacked):
    return [stacked] + [flip(stacked, mask) for mask in SIDES]


def near_slices(sides, after=()):
    depth, rows, columns = sides[0].shape
    slice_shape = (1, rows, columns)
    return stepped(
        stack_kernel,
        depth,
        sides,
        [pl.BlockSpec(slice_shape, lambda part: (part, 0, 0))] * 4,
        pl.BlockSpec((4,) + slice_shape, lambda part: (0, part, 0, 0)),
        jax.ShapeDtypeStruct((4, depth, rows, columns), sides[0].dtype),
        after,
        "stack_sides",
    )


def plane_gather(near):
    depth, rows, columns = near.shape[1:]
    slice_shape = (1, rows, columns)
    me = lax.axis_index(PLANE)
    chip = 2 * (me // 4) + me % 2
    far = flip(near, CORE)
    order = jnp.stack([chip, chip ^ 2, chip ^ 1, chip ^ 3, (me // 2) % 2]).astype(jnp.int32)
    source = pl.BlockSpec((4,) + slice_shape, lambda part, order: (0, part, 0, 0))
    placed = pl.pallas_call(
        place_kernel,
        grid_spec=pltpu.PrefetchScalarGridSpec(
            num_scalar_prefetch=1,
            grid=(depth,),
            in_specs=[source] * 2,
            out_specs=pl.BlockSpec((1, 8, rows, columns), lambda part, order: (part, 0, 0, 0)),
        ),
        out_shape=jax.ShapeDtypeStruct((depth, 8, rows, columns), near.dtype),
        compiler_params=pltpu.CompilerParams(vmem_limit_bytes=40 * MEBI),
        name="place_slices",
    )(order, near, far)
    return placed.reshape(depth * 8 * rows, columns)


def pair_kernel(place_ref, kept_ref, other_ref, *refs):
    own_ref, *side_refs = refs[-4:]
    place = place_ref[0]
    own_ref[...] = kept_ref[place].astype(WIDE_TYPE) + other_ref[place].astype(WIDE_TYPE)
    for side_ref, other in zip(side_refs, (2, 1, 3)):
        chip = place ^ other
        total = kept_ref[chip].astype(WIDE_TYPE) + other_ref[chip].astype(WIDE_TYPE)
        side_ref[...] = total.astype(NARROW_TYPE)


def finish_kernel(own_ref, *refs):
    total = own_ref[...]
    for ref in refs[:3]:
        total += ref[...].astype(WIDE_TYPE)
    refs[-1][...] = total.T.astype(NARROW_TYPE)


def pair_sum(kept, other, after=(), columns=256):
    me = lax.axis_index(PLANE)
    place = (2 * (me // 4) + me % 2).reshape(1).astype(jnp.int32)
    rows, width = kept.shape[1:]
    stack = pl.BlockSpec((4, rows, columns), lambda step, place: (0, 0, step))
    flat = pl.BlockSpec((rows, columns), lambda step, *_: (0, step))
    narrow = jax.ShapeDtypeStruct((rows, width), NARROW_TYPE)
    return pl.pallas_call(
        pair_kernel,
        grid_spec=pltpu.PrefetchScalarGridSpec(
            num_scalar_prefetch=1,
            grid=(width // columns,),
            in_specs=[stack, stack] + [ANYWHERE] * len(after),
            out_specs=[flat] * 4,
        ),
        out_shape=[jax.ShapeDtypeStruct((rows, width), WIDE_TYPE)] + [narrow] * 3,
        compiler_params=pltpu.CompilerParams(vmem_limit_bytes=40 * MEBI),
        name="pair_sum",
    )(place, kept, other, *after)


def side_sum(own, *sides, after=(), columns=256):
    rows, width = own.shape
    flat = pl.BlockSpec((rows, columns), lambda step, *_: (0, step))
    sides = [flip(side, mask) for side, mask in zip(sides, SIDES)]
    return pl.pallas_call(
        finish_kernel,
        grid=(width // columns,),
        in_specs=[flat] * 4 + [ANYWHERE] * len(after),
        out_specs=pl.BlockSpec((columns, rows), lambda step: (step, 0)),
        out_shape=jax.ShapeDtypeStruct((width, rows), NARROW_TYPE),
        compiler_params=pltpu.CompilerParams(vmem_limit_bytes=40 * MEBI),
        name="side_sum",
    )(own, *sides, *after)


def last_kernel(
    core_ref, joined_ref, first_ref, grad_ref, attended_ref, logits_ref, second_ref, kept_ref, sent_ref, totals, router
):
    step = pl.program_id(0)
    width = first_ref.shape[1]

    @pl.when(step < 3)
    def _():
        start = pl.multiple_of(step * width, 8)
        totals[pl.ds(start, width)] = contract(joined_ref[0], first_ref[...], 0, 0)

    @pl.when(step == 3)
    def _():
        totals[3 * width :] = contract(grad_ref[...], attended_ref[...], 0, 0)
        router[...] = contract(logits_ref[...], second_ref[...], 0, 0)

    part = part_of_step(core_ref[0], jnp.maximum(step - 4, 0))

    def write(part_ref):
        place = 0
        for start, rows in ((0, 3 * width // 8), (3 * width, width // 8)):
            first = pl.multiple_of(start + part * rows, 8)
            part_ref[0, place : place + rows] = totals[pl.ds(first, rows)].astype(NARROW_TYPE)
            place += rows
        number = lax.broadcasted_iota(jnp.int32, router.shape, 0)
        column = jnp.sum(jnp.where(number == part, router[...], 0.0), axis=0, keepdims=True)
        tail = part_ref.shape[1] - place
        row = lax.broadcasted_iota(jnp.int32, (tail, width), 0)
        part_ref[0, place:] = jnp.where(row == 0, column, 0.0).astype(NARROW_TYPE)

    @pl.when(jnp.logical_and(step >= 4, step < 8))
    def _():
        write(kept_ref)

    @pl.when(step >= 8)
    def _():
        write(sent_ref)


def last_gradients(grad_joined, first_in, grad_attention, attended, grad_logits, second_in):
    count, width = first_in.shape
    rows = width // 2 + 16
    flat = pl.BlockSpec((count, width), lambda step, core: (0, 0))
    thin = pl.BlockSpec((count, grad_logits.shape[1]), lambda step, core: (0, 0))
    return pl.pallas_call(
        last_kernel,
        grid_spec=pltpu.PrefetchScalarGridSpec(
            num_scalar_prefetch=1,
            grid=(12,),
            in_specs=[
                pl.BlockSpec((1, count, width), lambda step, core: (jnp.minimum(step, 2), 0, 0)),
                flat,
                flat,
                flat,
                thin,
                flat,
            ],
            out_specs=part_specs(4, rows, width),
            scratch_shapes=[
                pltpu.VMEM((4 * width, width), WIDE_TYPE),
                pltpu.VMEM((grad_logits.shape[1], width), WIDE_TYPE),
            ],
        ),
        out_shape=[jax.ShapeDtypeStruct((4, rows, width), NARROW_TYPE)] * 2,
        compiler_params=pltpu.CompilerParams(vmem_limit_bytes=56 * MEBI),
        name="last_gradients",
    )(own_core(), grad_joined, first_in, grad_attention, attended, grad_logits, second_in)


def depth_shift(value, shift):
    depth = lax.axis_size("dp")
    return lax.ppermute(value, "dp", [(index, (index + shift) % depth) for index in range(depth)])


def depth_scatter(parts):
    depth = lax.axis_size("dp")
    blocks = parts.reshape(depth, parts.shape[0] // depth, parts.shape[1])
    if depth > 8:
        blocks = lax.all_to_all(blocks, "dp", split_axis=0, concat_axis=0, tiled=True)
        return jnp.sum(blocks.astype(WIDE_TYPE), axis=0)
    me = lax.axis_index("dp")
    total = lax.dynamic_index_in_dim(blocks, me, 0, keepdims=False).astype(WIDE_TYPE)
    for shift in range(1, depth):
        part = lax.dynamic_index_in_dim(blocks, (me + shift) % depth, 0, keepdims=False)
        total = total + depth_shift(part, shift).astype(WIDE_TYPE)
    return total


def first_payload_kernel(place_ref, qkv_ref, out_ref, router_ref, cond_ref, payload_ref):
    del place_ref
    depth, rows, columns = payload_ref.shape
    slots = cond_ref.shape[0]
    local = cond_ref.shape[1] // depth
    qkv_end = qkv_ref.shape[1]
    out_end = qkv_end + out_ref.shape[1]
    router_end = out_end + 128
    silu = cond_ref[...].astype(WIDE_TYPE)
    silu = silu * jax.nn.sigmoid(silu)
    router = jnp.concatenate(
        [router_ref[...].astype(WIDE_TYPE), jnp.zeros((rows, 128 - router_ref.shape[1]), WIDE_TYPE)],
        axis=1,
    ).astype(NARROW_TYPE)
    payload_ref[...] = jnp.zeros_like(payload_ref)
    for part in range(depth):
        payload_ref[part, :, :qkv_end] = qkv_ref[...]
        payload_ref[part, :, qkv_end:out_end] = out_ref[...]
        payload_ref[part, :, out_end:router_end] = router
        tail = jnp.concatenate(
            [silu[:, part * local : (part + 1) * local], jnp.zeros((slots, columns - router_end - local), WIDE_TYPE)],
            axis=1,
        )
        tail = jnp.concatenate([tail, jnp.zeros((rows - slots, columns - router_end), WIDE_TYPE)], axis=0)
        payload_ref[part, :, router_end:] = tail.astype(NARROW_TYPE)


def first_payload(qkv, out, router, cond, depth, rows):
    place = lax.axis_index(PLANE).reshape(1).astype(jnp.int32)
    local = cond.shape[1] // depth
    columns = qkv.shape[1] + out.shape[1] + 128 + local + -local % 128

    def slice_of(operand):
        return pl.BlockSpec((rows, operand.shape[1]), lambda step, place: (place[0], 0))

    return pl.pallas_call(
        first_payload_kernel,
        grid_spec=pltpu.PrefetchScalarGridSpec(
            num_scalar_prefetch=1,
            grid=(1,),
            in_specs=[slice_of(qkv), slice_of(out), slice_of(router), whole_block(cond)],
            out_specs=pl.BlockSpec((depth, rows, columns), lambda step, place: (0, 0, 0)),
        ),
        out_shape=jax.ShapeDtypeStruct((depth, rows, columns), NARROW_TYPE),
        name="first_payload",
    )(place, qkv, out, router, cond)


def rest_payload_kernel(local, place_ref, up_ref, down_ref, *refs):
    del place_ref
    payload_ref = refs[-1]
    hidden = up_ref.shape[1]
    width = down_ref.shape[2]
    depth = hidden // (4 * local)
    for block in range(4):
        for part in range(depth):
            target = (block * depth + part) * local
            source = (part * 4 + block) * local
            payload_ref[:, target : target + local] = up_ref[:, source : source + local]
        start = hidden + block * width
        payload_ref[:, start : start + width] = down_ref[block]


def rest_payload(up, down, rows, after):
    place = lax.axis_index(PLANE).reshape(1).astype(jnp.int32)
    local, hidden = up.shape
    width = down.shape[1]
    shape = (rows, hidden + 4 * width)
    return pl.pallas_call(
        functools.partial(rest_payload_kernel, local),
        grid_spec=pltpu.PrefetchScalarGridSpec(
            num_scalar_prefetch=1,
            grid=(1,),
            in_specs=[
                pl.BlockSpec((rows, hidden), lambda step, place: (place[0], 0)),
                pl.BlockSpec((4, rows, width), lambda step, place: (0, place[0], 0)),
            ]
            + [ANYWHERE] * len(after),
            out_specs=pl.BlockSpec(shape, lambda step, place: (0, 0)),
        ),
        out_shape=jax.ShapeDtypeStruct(shape, NARROW_TYPE),
        name="rest_payload",
    )(place, up, down.reshape(4, local, width), *after)


def expert_payload_kernel(up_ref, down_ref, *refs):
    payload_ref = refs[-1]
    local, hidden = up_ref.shape
    width = down_ref.shape[1]
    depth = hidden // (4 * local)
    for block in range(4):
        for part in range(depth):
            target = (block * depth + part) * local
            source = (part * 4 + block) * local
            payload_ref[:, target : target + local] = up_ref[:, source : source + local]
        start = hidden + block * width
        payload_ref[:, start : start + width] = down_ref[block * local : (block + 1) * local, :]


def expert_payload(up, down, after):
    local, hidden = up.shape
    whole = pl.BlockSpec(memory_space=pltpu.VMEM)
    return pl.pallas_call(
        expert_payload_kernel,
        in_specs=[whole, whole] + [ANYWHERE] * len(after),
        out_specs=whole,
        out_shape=jax.ShapeDtypeStruct((local, hidden + 4 * down.shape[1]), up.dtype),
        name="expert_payload",
    )(up, down, *after)


def normalize_rows(values):
    centre = values - jnp.mean(values, axis=-1, keepdims=True)
    spread = jnp.mean(centre * centre, axis=-1, keepdims=True)
    reciprocal = lax.rsqrt(spread + EPSILON)
    return centre * reciprocal, reciprocal


def normalize_rows_back(gradient, normed, reciprocal):
    mean = jnp.mean(gradient, axis=-1, keepdims=True)
    along = jnp.mean(gradient * normed, axis=-1, keepdims=True)
    return reciprocal * (gradient - mean - normed * along)


def pick_slots(first, count, places_ref):
    patches = places_ref.shape[1]
    slot = first + lax.broadcasted_iota(jnp.int32, (count, patches), 0)
    return jnp.logical_or(slot == places_ref[0:1, :], slot == places_ref[1:2, :])


def one(mask):
    return jnp.where(mask, 1.0, 0.0).astype(NARROW_TYPE)


def mixture_kernel(grad_ref, mods_ref, places_ref, silu_ref, shared_ref, out_ref):
    step = pl.program_id(0)
    quarter = grad_ref.shape[0] // 4

    @pl.when(step == 0)
    def _():
        for part in range(4):
            rows = slice(part * quarter, (part + 1) * quarter)
            gradient = grad_ref[rows, :].astype(WIDE_TYPE) * mods_ref[part, 5:6, :]
            shared_ref[rows, :] = gradient.astype(NARROW_TYPE)

    taken = one(pick_slots(step * CAP, CAP, places_ref))
    out_ref[0, :CAP] = contract(taken, shared_ref[...], 1, 0).astype(NARROW_TYPE)
    out_ref[0, CAP:] = jnp.zeros((SPARE, out_ref.shape[2]), NARROW_TYPE)
    out_ref[0, CAP:, : silu_ref.shape[1]] = silu_ref[...]


def slot_block(width):
    return pl.BlockSpec((1, CAP + SPARE, width), lambda step: (step, 0, 0))


def spread_mixture(out_grad, mods, places, silu, after):
    count, width = out_grad.shape
    return stepped(
        mixture_kernel,
        8,
        (out_grad, mods, places, silu),
        [whole_block(operand) for operand in (out_grad, mods, places, silu)],
        [pl.BlockSpec((count, width), lambda step: (0, 0)), slot_block(width)],
        [
            jax.ShapeDtypeStruct((count, width), NARROW_TYPE),
            jax.ShapeDtypeStruct((8, CAP + SPARE, width), NARROW_TYPE),
        ],
        after,
        "spread_mixture",
    )


def first_kernel(patch_ref, mods_ref, weight_ref, first_ref, joined_ref):
    normed, _ = normalize_rows(patch_ref[...].astype(WIDE_TYPE))
    first = (normed * (1.0 + mods_ref[0, 1:2, :]) + mods_ref[0, 0:1, :]).astype(NARROW_TYPE)
    first_ref[...] = first
    width = first.shape[1]
    for part in range(3):
        columns = slice(part * width, (part + 1) * width)
        joined_ref[part] = contract(first, weight_ref[:, columns], 1, 0).astype(NARROW_TYPE)


def mods_block(mods):
    return pl.BlockSpec((1,) + mods.shape[1:], lambda step, *_: (step, 0, 0))


def first_half(patches, mods, weights, after):
    count, width = patches.shape
    quarter = count // 4
    rows = row_block(quarter, width)
    return stepped(
        first_kernel,
        4,
        (patches, mods, weights),
        [rows, mods_block(mods), column_block(weights, 3 * width, 0)],
        [rows, pl.BlockSpec((3, quarter, width), lambda step: (0, step, 0))],
        [
            jax.ShapeDtypeStruct((count, width), NARROW_TYPE),
            jax.ShapeDtypeStruct((3, count, width), NARROW_TYPE),
        ],
        after,
        "first_half",
    )


def second_kernel(
    attended_ref, patch_ref, mods_ref, routes_ref, out_ref, router_ref, attention_ref, middle_ref, second_ref, gates_ref, gate_rows_ref
):
    attention = contract(attended_ref[...], out_ref[...], 1, 0)
    attention_ref[...] = attention
    middle = patch_ref[...].astype(WIDE_TYPE) + mods_ref[0, 2:3, :] * attention
    middle_ref[...] = middle
    normed, _ = normalize_rows(middle)
    second = (normed * (1.0 + mods_ref[0, 4:5, :]) + mods_ref[0, 3:4, :]).astype(NARROW_TYPE)
    second_ref[...] = second
    logits = contract(second, router_ref[...], 1, 0)
    lane = lax.broadcasted_iota(jnp.int32, logits.shape, 1)
    picked = [
        jnp.sum(jnp.where(lane == routes_ref[:, k : k + 1], logits, 0.0), axis=1, keepdims=True)
        for k in range(TOP)
    ]
    summit = jnp.maximum(picked[0], picked[1])
    weights = [jnp.exp(value - summit) for value in picked]
    total = weights[0] + weights[1]
    gates = [weight / total for weight in weights]
    gates_ref[...] = jnp.concatenate(gates, axis=1)
    wide = jnp.where(lane == 0, gates[0], jnp.where(lane == 1, gates[1], 0.0))
    gate_rows_ref[...] = wide.T[0:TOP, :]


def second_half(attended, patches, mods, routes, weights, after):
    count, width = patches.shape
    quarter = count // 4
    rows = row_block(quarter, width)
    pair = row_block(quarter, TOP)
    wide = jax.ShapeDtypeStruct((count, width), WIDE_TYPE)
    return stepped(
        second_kernel,
        4,
        (attended, patches, mods, routes, weights, weights),
        [
            rows,
            rows,
            mods_block(mods),
            pair,
            column_block(weights, width, 3),
            column_block(weights, 128, 4 * width // 128),
        ],
        [rows, rows, rows, pair, pl.BlockSpec((TOP, quarter), lambda step: (0, step))],
        [
            wide,
            wide,
            jax.ShapeDtypeStruct((count, width), NARROW_TYPE),
            jax.ShapeDtypeStruct((count, TOP), WIDE_TYPE),
            jax.ShapeDtypeStruct((TOP, count), WIDE_TYPE),
        ],
        after,
        "second_half",
    )


def spread_kernel(second_ref, places_ref, gates_ref, rows_ref):
    slots = pick_slots(pl.program_id(0) * CAP, CAP, places_ref)
    rows_ref[0, :CAP] = contract(one(slots), second_ref[...], 1, 0).astype(NARROW_TYPE)
    slot = pl.program_id(0) * CAP + lax.broadcasted_iota(jnp.int32, slots.shape, 0)
    total = jnp.where(slot == places_ref[0:1, :], gates_ref[0:1, :], 0.0)
    total += jnp.where(slot == places_ref[1:2, :], gates_ref[1:2, :], 0.0)
    column = jnp.sum(total, axis=1, keepdims=True)
    gates = jnp.broadcast_to(column, (CAP, 128)).T[0:SPARE, :]
    row = lax.broadcasted_iota(jnp.int32, gates.shape, 0)
    terms = jnp.zeros(gates.shape, WIDE_TYPE)
    for number in range(3):
        term = gates.astype(NARROW_TYPE).astype(WIDE_TYPE)
        terms = jnp.where(row == number, term, terms)
        gates = gates - term
    rows_ref[0, CAP:] = jnp.zeros((SPARE, rows_ref.shape[2]), NARROW_TYPE)
    rows_ref[0, CAP:, :CAP] = terms.astype(NARROW_TYPE)


def spread_second(second_in, places, gates, after):
    width = second_in.shape[1]
    operands = (second_in, places, gates)
    return stepped(
        spread_kernel,
        8,
        operands,
        [whole_block(operand) for operand in operands],
        slot_block(width),
        jax.ShapeDtypeStruct((8, CAP + SPARE, width), NARROW_TYPE),
        after,
        "spread_second",
    )


def middle_kernel(
    back_ref,
    dots_ref,
    columns_ref,
    routes_ref,
    gates_ref,
    shared_ref,
    middle_ref,
    attention_ref,
    mods_ref,
    grad_ref,
    out_ref,
    router_ref,
    grad_middle_ref,
    grad_attention_ref,
    grad_attended_ref,
    grad_logits_ref,
    sums_ref,
):
    quarter, width = middle_ref.shape
    slot = lax.broadcasted_iota(jnp.int32, (quarter, back_ref.shape[0]), 1)
    takes = [slot == columns_ref[:, k : k + 1] for k in range(TOP)]
    collected = contract(one(jnp.logical_or(*takes)), back_ref[...], 1, 0)
    gates = [gates_ref[:, k : k + 1] for k in range(TOP)]
    grad_gate = [
        jnp.sum(jnp.where(take, dots_ref[...], 0.0), axis=1, keepdims=True) for take in takes
    ]
    centre = gates[0] * grad_gate[0] + gates[1] * grad_gate[1]
    lane = lax.broadcasted_iota(jnp.int32, grad_logits_ref.shape, 1)
    grad_logits = jnp.zeros(grad_logits_ref.shape, WIDE_TYPE)
    for k in range(TOP):
        picked = gates[k] * (grad_gate[k] - centre)
        grad_logits += jnp.where(lane == routes_ref[:, k : k + 1], picked, 0.0)
    grad_logits = grad_logits.astype(NARROW_TYPE)
    grad_logits_ref[...] = grad_logits
    grad_second = shared_ref[...] + contract(grad_logits, router_ref[...], 1, 1) + collected
    normed, reciprocal = normalize_rows(middle_ref[...])
    grad_middle = grad_ref[...].astype(WIDE_TYPE) + normalize_rows_back(
        grad_second * (1.0 + mods_ref[0, 4:5, :]), normed, reciprocal
    )
    grad_middle_ref[...] = grad_middle
    grad_attention = (grad_middle * mods_ref[0, 2:3, :]).astype(NARROW_TYPE)
    grad_attention_ref[...] = grad_attention
    grad_attended_ref[...] = contract(grad_attention, out_ref[...], 1, 1).astype(NARROW_TYPE)
    sums_ref[0] = jnp.concatenate(
        [
            jnp.sum(grad_middle * attention_ref[...], axis=0, keepdims=True),
            jnp.sum(grad_second, axis=0, keepdims=True),
            jnp.sum(grad_second * normed, axis=0, keepdims=True),
        ],
        axis=0,
    )


def sums_block(count, width):
    return pl.BlockSpec((1, count, width), lambda step: (step, 0, 0))


def middle_back(
    back, dots, columns, routes, gates, grad_shared, middle, attention, mods, out_grad, weights, after
):
    count, width = middle.shape
    quarter = count // 4
    rows, pair, lanes = row_block(quarter, width), row_block(quarter, TOP), row_block(quarter, 128)
    narrow = jax.ShapeDtypeStruct((count, width), NARROW_TYPE)
    return stepped(
        middle_kernel,
        4,
        (back, dots, columns, routes, gates, grad_shared, middle, attention, mods, out_grad, weights, weights),
        [whole_block(back), whole_block(dots), pair, pair, pair, rows, rows, rows]
        + [mods_block(mods), rows]
        + [column_block(weights, width, 3), column_block(weights, 128, 4 * width // 128)],
        [rows, rows, rows, lanes, sums_block(3, width)],
        [
            jax.ShapeDtypeStruct((count, width), WIDE_TYPE),
            narrow,
            narrow,
            jax.ShapeDtypeStruct((count, 128), NARROW_TYPE),
            jax.ShapeDtypeStruct((4, 3, width), WIDE_TYPE),
        ],
        after,
        "middle_back",
    )


def output_kernel(
    result_ref, columns_ref, shared_ref, middle_ref, mods_ref, grad_ref, out_ref, sums_ref
):
    quarter = middle_ref.shape[0]
    slot = lax.broadcasted_iota(jnp.int32, (quarter, result_ref.shape[0]), 1)
    takes = [slot == columns_ref[:, k : k + 1] for k in range(TOP)]
    mixture = shared_ref[...] + contract(one(jnp.logical_or(*takes)), result_ref[...], 1, 0)
    out_ref[...] = (middle_ref[...] + mods_ref[0, 5:6, :] * mixture).astype(NARROW_TYPE)
    sums_ref[0] = jnp.sum(grad_ref[...].astype(WIDE_TYPE) * mixture, axis=0, keepdims=True)


def block_output(result, columns, shared, middle, mods, out_grad, after):
    count, width = middle.shape
    quarter = count // 4
    rows, pair = row_block(quarter, width), row_block(quarter, TOP)
    return stepped(
        output_kernel,
        4,
        (result, columns, shared, middle, mods, out_grad),
        [whole_block(result), pair, rows, rows, mods_block(mods), rows],
        [rows, sums_block(1, width)],
        [
            jax.ShapeDtypeStruct((count, width), NARROW_TYPE),
            jax.ShapeDtypeStruct((4, 1, width), WIDE_TYPE),
        ],
        after,
        "block_output",
    )


def start_kernel(joined_ref, weight_ref, patch_ref, mods_ref, middle_ref, out_ref, sums_ref):
    width = patch_ref.shape[1]
    grad_first = jnp.zeros(patch_ref.shape, WIDE_TYPE)
    for part in range(3):
        columns = slice(part * width, (part + 1) * width)
        grad_first += contract(joined_ref[part], weight_ref[:, columns], 1, 1)
    normed, reciprocal = normalize_rows(patch_ref[...].astype(WIDE_TYPE))
    out_ref[...] = middle_ref[...] + normalize_rows_back(
        grad_first * (1.0 + mods_ref[0, 1:2, :]), normed, reciprocal
    )
    sums_ref[0] = jnp.concatenate(
        [
            jnp.sum(grad_first, axis=0, keepdims=True),
            jnp.sum(grad_first * normed, axis=0, keepdims=True),
        ],
        axis=0,
    )


def start_back(grad_joined, weights, patches, mods, grad_middle, after):
    count, width = patches.shape
    quarter = count // 4
    rows = row_block(quarter, width)
    return stepped(
        start_kernel,
        4,
        (grad_joined, weights, patches, mods, grad_middle),
        [
            pl.BlockSpec((3, quarter, width), lambda step: (0, step, 0)),
            column_block(weights, 3 * width, 0),
            rows,
            mods_block(mods),
            rows,
        ],
        [rows, sums_block(2, width)],
        [
            jax.ShapeDtypeStruct((count, width), WIDE_TYPE),
            jax.ShapeDtypeStruct((4, 2, width), WIDE_TYPE),
        ],
        after,
        "start_back",
    )


def expert_sums_kernel(early_ref, late_ref, up_ref, down_ref):
    local, hidden = up_ref.shape
    width = down_ref.shape[1]
    depth = hidden // (4 * local)
    for block in range(4):
        ref = (early_ref, late_ref)[block // 2]
        for part in range(depth):
            source = (block % 2) * width + part * local
            target = (part * 4 + block) * local
            up_ref[:, target : target + local] = ref[:, source : source + local].astype(WIDE_TYPE)
        source = (2 + block % 2) * width
        down_ref[block * local : (block + 1) * local] = ref[:, source : source + width].astype(WIDE_TYPE)


def expert_sums(early, late):
    local, hidden = early.shape
    width = hidden // 4
    return stepped(
        expert_sums_kernel,
        1,
        (early, late),
        [whole_block(early), whole_block(late)],
        [
            pl.BlockSpec((local, hidden), lambda step: (0, 0)),
            pl.BlockSpec((4 * local, width), lambda step: (0, 0)),
        ],
        [
            jax.ShapeDtypeStruct((local, hidden), WIDE_TYPE),
            jax.ShapeDtypeStruct((4 * local, width), WIDE_TYPE),
        ],
        (),
        "expert_sums",
    )


def slot_of_routes(route_rows, expert_count, capacity):
    pair_ids = route_rows.reshape(-1)
    onehot = (pair_ids[:, None] == jnp.arange(expert_count, dtype=jnp.int32)[None, :]).astype(
        jnp.int32
    )
    rank_values = jnp.cumsum(onehot, axis=0) - onehot
    slot_index = jnp.sum(rank_values * onehot, axis=1)
    return (pair_ids * capacity + slot_index).reshape(route_rows.shape)


def on_device(
    patches,
    cond,
    long_pack,
    routes,
    ada_weight,
    qkv_weight,
    out_weight,
    router_weight,
    shared_up,
    shared_down,
    expert_up,
    expert_down,
    out_grad,
):
    width = patches.shape[1]
    hidden = shared_up.shape[1]
    depth = lax.axis_size("dp")
    experts = lax.axis_size(PLANE)
    capacity = CAP
    slots = experts * capacity
    local = qkv_weight.shape[0]
    slice_rows = local // experts
    plane_index = lax.axis_index(PLANE)

    def blocked(columns):
        split = columns.reshape(columns.shape[0], depth, 4, local)
        return jnp.transpose(split, (0, 2, 1, 3)).reshape(columns.shape)

    def own(rows):
        return lax.dynamic_slice_in_dim(rows, plane_index * slice_rows, slice_rows, 0)

    places = slot_of_routes(routes, experts, capacity)
    columns, places = places, places.T
    expert_piece = expert_payload(expert_up[0], expert_down[0], ())

    cond_wide = cond.astype(WIDE_TYPE)
    cond_rows = cond.shape[0]
    if slice_rows % 8 == 0:
        first_stack = lax.all_to_all(
            first_payload(qkv_weight, out_weight, router_weight, cond, depth, slice_rows),
            "dp",
            split_axis=0,
            concat_axis=0,
            tiled=True,
        )
        first_end = 4 * width + 128
        silu_parts = first_stack[:, :cond_rows, first_end : first_end + local]
        rest_piece = rest_payload(
            shared_up, shared_down, slice_rows, (first_stack, places, expert_piece)
        )
    else:
        silu_cond = jax.nn.silu(cond_wide).astype(NARROW_TYPE)
        silu_parts = lax.all_to_all(
            jnp.transpose(silu_cond.reshape(cond_rows, depth, local), (1, 0, 2)),
            "dp",
            split_axis=0,
            concat_axis=0,
            tiled=True,
        )
        router_slice = jnp.pad(own(router_weight), ((0, 0), (0, 128 - router_weight.shape[1])))
        first_stack = depth_stack(
            jnp.concatenate([own(qkv_weight), own(out_weight), router_slice], axis=1)
        )
        down_slice = lax.dynamic_slice_in_dim(
            shared_down.reshape(4, local, width), plane_index * slice_rows, slice_rows, 1
        )
        rest_piece = jnp.concatenate(
            [
                blocked(own(shared_up)),
                jnp.transpose(down_slice, (1, 0, 2)).reshape(slice_rows, 4 * width),
            ],
            axis=1,
        )
    silu_parts = silu_parts.reshape(depth * cond_rows, local)
    partial = product_plain_operands(silu_parts, ada_weight)
    first_sides = side_gather(first_stack)
    rest_stack = lax.all_gather(rest_piece, "dp", axis=0)
    modulation = jnp.sum(
        lax.all_to_all(
            partial.reshape(depth, cond_rows, 6 * width), "dp", split_axis=0, concat_axis=0, tiled=True
        ),
        axis=0,
    )
    blocks = modulation.reshape(4, 6, width)
    is_long = long_pack[0] == 1
    mods = jnp.where(is_long, blocks[:1], blocks)

    def exchange(rows):
        return lax.all_to_all(rows, PLANE, split_axis=0, concat_axis=0, tiled=True)

    grad_shared, mixture_slots = spread_mixture(
        out_grad, mods, places, silu_parts.reshape(SPARE, -1), ()
    )
    first_near = near_slices(first_sides, (mixture_slots,))
    expert_piece, first_near = together(expert_piece, first_near)
    expert_weights = lax.all_gather(expert_piece, "dp", axis=0, tiled=True)
    mixture_slots = exchange(mixture_slots)
    first_full = plane_gather(first_near)
    rest_sides = side_gather(rest_stack)
    first_in, joined = first_half(patches, mods, first_full, ())
    attended, log_total = attend(long_pack, joined)
    attended, mixture_slots = together(attended, mixture_slots)
    attention, middle, second_in, gate_values, gate_rows = second_half(
        attended, patches, mods, routes, first_full, ()
    )
    slot_rows = spread_second(second_in, places, gate_rows, ())
    rest = plane_gather(near_slices(rest_sides, (attended, slot_rows)))
    slots_there = exchange(slot_rows)

    shared, grad_from_shared, kept, sent = shared_expert(
        second_in, grad_shared, rest, local, (slot_rows,)
    )
    sent, slots_there = together(sent, slots_there)
    gates_there = jnp.sum(slots_there[:, capacity : capacity + 3, :capacity].astype(WIDE_TYPE), axis=1)
    routed = (
        slots_there[:, :capacity].reshape(slots, width),
        mixture_slots[:, :capacity].reshape(slots, width),
        gates_there.reshape(slots, 1),
    )
    silu_all = mixture_slots[:, capacity:, : silu_parts.size // SPARE]
    silu_all = silu_all.reshape(experts, depth, cond_rows, local)
    silu_all = jnp.transpose(silu_all, (1, 0, 2, 3)).reshape(depth * experts * cond_rows, local)
    result_rows, grad_rows, gate_dots, units, grad_units = routed_expert(
        *routed, expert_weights, ()
    )
    grad_rows_back = exchange(grad_rows.reshape(experts, capacity, width)).reshape(slots, width)
    gate_dots_back = exchange(gate_dots.reshape(experts, 1, capacity)).reshape(1, slots)
    early_sums = routed_sums(*routed, units, grad_units, 0, ())
    early_sums, gate_dots_back = together(early_sums, gate_dots_back)
    early_final = lax.psum_scatter(early_sums, "dp", scatter_dimension=0, tiled=True)
    late_sums = routed_sums(*routed, units, grad_units, 1, (early_sums,))
    middle_own, *middle_sides = pair_sum(kept, flip(sent, CORE), (late_sums,))

    grad_middle, grad_attention, grad_attended, grad_logits, middle_sums = middle_back(
        grad_rows_back,
        gate_dots_back,
        columns,
        routes,
        gate_values,
        grad_from_shared,
        middle,
        attention,
        mods,
        out_grad,
        first_full,
        (silu_all,),
    )
    late_sums, *middle_sides, grad_attended = together(late_sums, *middle_sides, grad_attended)
    late_final = lax.psum_scatter(late_sums, "dp", scatter_dimension=0, tiled=True)
    result_back = exchange(result_rows.reshape(experts, capacity, width)).reshape(slots, width)
    grad_joined = attend_back(long_pack, joined, log_total, grad_attended, ())
    last_parts = last_gradients(
        grad_joined, first_in, grad_attention, attended, grad_logits, second_in
    )
    middle_sum = side_sum(middle_own, *middle_sides, after=(grad_joined,))
    block_out, output_sums = block_output(
        result_back,
        columns,
        shared,
        middle,
        mods,
        out_grad,
        (*last_parts, middle_sum, early_final),
    )
    middle_final = lax.psum_scatter(middle_sum, "dp", scatter_dimension=0, tiled=True)
    middle_final = middle_final.astype(WIDE_TYPE)
    shared_up_grad = middle_final[:, : hidden // experts]
    shared_down_grad = jnp.transpose(
        middle_final[:, hidden // experts :].reshape(local, 4, width // experts), (1, 0, 2)
    ).reshape(4 * local, width // experts)

    last_pair = pair_sum(last_parts[0], flip(last_parts[1], CORE))
    patches_grad, start_sums = start_back(
        grad_joined, first_full, patches, mods, grad_middle, tuple(last_pair)
    )
    last_sum = side_sum(*last_pair)
    grad_chosen = jnp.concatenate([start_sums, middle_sums, output_sums], axis=1)
    grad_chosen = grad_chosen.reshape(1, 4, 6 * width)
    long_total = jnp.sum(grad_chosen, axis=1, keepdims=True)
    first_slot = (jnp.arange(4, dtype=jnp.int32) == 0)[None, :, None]
    grad_blocks = jnp.where(is_long, jnp.where(first_slot, long_total, 0.0), grad_chosen)
    grad_modulation = grad_blocks.reshape(cond_rows, 6 * width).astype(NARROW_TYPE)
    everyone = ("dp",) + PLANE
    columns = 6 * width // experts
    grad_columns = jnp.transpose(grad_modulation.reshape(cond_rows, experts, columns), (1, 0, 2))
    grad_columns = jnp.broadcast_to(grad_columns[None], (depth, experts, cond_rows, columns))
    grad_columns = lax.all_to_all(
        grad_columns.reshape(depth * experts, cond_rows, columns),
        everyone,
        split_axis=0,
        concat_axis=0,
        tiled=True,
    ).reshape(depth * experts * cond_rows, columns)
    ada_weight_grad = product_left_operand(silu_all, grad_columns)
    own_ada = lax.dynamic_slice_in_dim(ada_weight, plane_index * columns, columns, 1)
    silu_back, last_sum = together(product_right_operand(grad_columns, own_ada), last_sum)
    silu_back = lax.all_to_all(
        silu_back.reshape(depth * experts, cond_rows, local),
        everyone,
        split_axis=0,
        concat_axis=0,
        tiled=True,
    )
    silu_back = jnp.sum(silu_back.reshape(depth, experts, cond_rows, local), axis=1)
    grad_silu = jnp.transpose(silu_back, (1, 0, 2)).reshape(cond_rows, width)
    cond_grad = jax.vjp(jax.nn.silu, cond_wide)[1](grad_silu)[0]
    last_final = depth_scatter(last_sum)
    edge_one, edge_two = 3 * width // experts, 4 * width // experts
    qkv_weight_grad = last_final[:, :edge_one]
    out_weight_grad = last_final[:, edge_one:edge_two]
    router_weight_grad = last_final[:, edge_two : edge_two + 1]

    expert_up_grad, expert_down_grad = expert_sums(early_final, late_final)
    return (
        block_out,
        patches_grad,
        cond_grad,
        ada_weight_grad,
        qkv_weight_grad,
        out_weight_grad,
        router_weight_grad,
        shared_up_grad,
        shared_down_grad,
        expert_up_grad[None],
        expert_down_grad[None],
    )


def solution(mesh):
    in_specs = (
        P(("dp", "expert", "stream"), None),
        P(("dp", "expert", "stream"), None),
        P(("dp", "expert", "stream")),
        P(("dp", "expert", "stream"), None),
        P("dp", None),
        P("dp", None),
        P("dp", None),
        P("dp", None),
        P("dp", None),
        P("dp", None),
        P(("expert", "stream"), "dp", None),
        P(("expert", "stream"), "dp", None),
        P(("dp", "expert", "stream"), None),
    )
    out_specs = (
        P(("dp", "expert", "stream"), None),
        P(("dp", "expert", "stream"), None),
        P(("dp", "expert", "stream"), None),
        P("dp", ("expert", "stream")),
        P("dp", ("expert", "stream")),
        P("dp", ("expert", "stream")),
        P("dp", ("expert", "stream")),
        P("dp", ("expert", "stream")),
        P("dp", ("expert", "stream")),
        P(("expert", "stream"), "dp", None),
        P(("expert", "stream"), "dp", None),
    )
    return jax.shard_map(
        on_device, mesh=mesh, in_specs=in_specs, out_specs=out_specs, check_vma=False
    )
```

```python
import functools
import math

import jax
import jax.numpy as jnp
from jax import lax
from jax.experimental import pallas as pl
from jax.experimental.pallas import tpu as pltpu
from jax.sharding import PartitionSpec as P

HEAD = 64
TOP = 2
CAP = 320
SPARE = 16


EPSILON = 1e-06
ROOT = math.sqrt(2.0 / math.pi)
CUBE = 0.044715 * ROOT
MEBI = 1 << 20
WIDE_TYPE = jnp.float32
NARROW_TYPE = jnp.bfloat16


def product_plain_operands(left_side, right_side):
    return jnp.dot(left_side, right_side, preferred_element_type=WIDE_TYPE)


def product_left_operand(left_side, right_side):
    return lax.dot_general(
        left_side, right_side, (((0,), (0,)), ((), ())), preferred_element_type=WIDE_TYPE
    )


def product_right_operand(left_side, right_side):
    return lax.dot_general(
        left_side, right_side, (((1,), (1,)), ((), ())), preferred_element_type=WIDE_TYPE
    )


def contract(left_side, right_side, left_dim, right_dim):
    return lax.dot_general(
        left_side, right_side, (((left_dim,), (right_dim,)), ((), ())), preferred_element_type=WIDE_TYPE
    )

def attend_rows(joined_ref, attended_ref, total_ref, head, rows, columns):
    lanes = slice(head * HEAD, (head + 1) * HEAD)
    queries = joined_ref[0, rows, lanes] * (1.0 / 8.0)
    keys = joined_ref[1, columns, lanes]
    values = joined_ref[2, columns, lanes]
    scores = contract(queries.astype(NARROW_TYPE), keys, 1, 1)
    summit = jnp.max(scores, axis=1, keepdims=True)
    weights = jnp.exp(scores - summit)
    row_total = jnp.sum(weights, axis=1, keepdims=True)
    probabilities = (weights * (1.0 / row_total)).astype(NARROW_TYPE)
    attended_ref[rows, lanes] = contract(probabilities, values, 1, 0).astype(NARROW_TYPE)
    total_ref[rows, lanes] = jnp.broadcast_to(summit + jnp.log(row_total), (scores.shape[0], HEAD))

def attend_kernel(long_ref, joined_ref, attended_ref, total_ref):
    length = joined_ref.shape[1]
    quarter = length // 4
    for whole in (True, False):
        @pl.when((long_ref[0] == 1) == whole)
        def _():
            block = 2 * quarter if whole else quarter
            for head in range(2):
                for start in range(0, length, block):
                    rows = slice(start, start + block)
                    attend_rows(joined_ref, attended_ref, total_ref, head, rows, slice(None) if whole else rows)

def attend(long_pack, joined):
    three, length, width = joined.shape
    return pl.pallas_call(
        attend_kernel,
        grid=(width // 128,),
        in_specs=[pl.BlockSpec(memory_space=pltpu.SMEM), pl.BlockSpec((3, length, 128), lambda pair: (0, 0, pair))],
        out_specs=[pl.BlockSpec((length, 128), lambda pair: (0, pair))] * 2,
        out_shape=[jax.ShapeDtypeStruct((length, width), NARROW_TYPE), jax.ShapeDtypeStruct((length, width), WIDE_TYPE)],
        compiler_params=pltpu.CompilerParams(vmem_limit_bytes=61 * MEBI),
        name="attend",
    )(long_pack, joined)

def attend_back_rows(joined_ref, total_ref, grad_ref, out_ref, keys_acc, values_acc, head, rows, columns):
    lanes = slice(head * HEAD, (head + 1) * HEAD)
    queries = joined_ref[0, rows, lanes]
    scaled = (queries * (1.0 / 8.0)).astype(NARROW_TYPE)
    keys = joined_ref[1, columns, lanes]
    values = joined_ref[2, columns, lanes]
    grads = grad_ref[rows, lanes]
    scores = contract(scaled, keys, 1, 1)
    probabilities = jnp.exp(scores - total_ref[rows, head * HEAD : head * HEAD + 1])
    grad_probs = contract(grads, values, 1, 1)
    product = probabilities * grad_probs
    centre = jnp.sum(product, axis=1, keepdims=True)
    grad_scores = (product - probabilities * centre).astype(NARROW_TYPE)
    out_ref[0, rows, lanes] = (contract(grad_scores, keys, 1, 0) * (1.0 / 8.0)).astype(NARROW_TYPE)
    keys_acc[lanes, columns] += contract(scaled.T, grad_scores, 1, 0)
    values_acc[lanes, columns] += contract(grads.T, probabilities.astype(NARROW_TYPE), 1, 0)

def attend_back_kernel(long_ref, joined_ref, total_ref, grad_ref, *refs):
    out_ref, keys_acc, values_acc = refs[-3:]
    length = joined_ref.shape[1]
    quarter = length // 4
    keys_acc[...] = jnp.zeros_like(keys_acc)
    values_acc[...] = jnp.zeros_like(values_acc)
    for whole in (True, False):
        @pl.when((long_ref[0] == 1) == whole)
        def _():
            block = 2 * quarter if whole else quarter
            for head in range(2):
                for start in range(0, length, block):
                    rows = slice(start, start + block)
                    attend_back_rows(joined_ref, total_ref, grad_ref, out_ref, keys_acc, values_acc, head, rows, slice(None) if whole else rows)
    out_ref[1] = keys_acc[...].T.astype(NARROW_TYPE)
    out_ref[2] = values_acc[...].T.astype(NARROW_TYPE)

def attend_back(long_pack, joined, total, grad, after):
    three, length, width = joined.shape
    wide = pl.BlockSpec((3, length, 128), lambda pair: (0, 0, pair))
    flat = pl.BlockSpec((length, 128), lambda pair: (0, pair))
    return pl.pallas_call(
        attend_back_kernel,
        grid=(width // 128,),
        in_specs=[pl.BlockSpec(memory_space=pltpu.SMEM), wide, flat, flat]
        + [pl.BlockSpec(memory_space=pl.ANY)] * len(after),
        out_specs=wide,
        out_shape=jax.ShapeDtypeStruct((3, length, width), NARROW_TYPE),
        scratch_shapes=[pltpu.VMEM((128, length), WIDE_TYPE)] * 2,
        compiler_params=pltpu.CompilerParams(vmem_limit_bytes=61 * MEBI),
        name="attend_back",
    )(long_pack, joined, total, grad, *after)


def gelu_pair(values):
    square = values * values
    half = 0.5 * jnp.tanh(values * (CUBE * square + ROOT)) + 0.5
    result = values * half
    slope = half + result * (1.0 - half) * (6.0 * CUBE * square + 2.0 * ROOT)
    return result, slope


def expert_block(rows, grads, up, down):
    hidden, slope = gelu_pair(contract(rows, up, 1, 0))
    grad_pre = slope * contract(grads, down, 1, 1)
    return hidden.astype(NARROW_TYPE), grad_pre.astype(NARROW_TYPE)


def slot_rows_of(ref):
    parts = [ref[part, :CAP] for part in range(ref.shape[0])]
    return jnp.concatenate(parts, axis=0)


def slot_gates_of(ref):
    columns = []
    for part in range(ref.shape[0]):
        terms = ref[part, CAP:, :].astype(WIDE_TYPE)
        gates = terms[0:1] + terms[1:2] + terms[2:3]
        columns.append(jnp.broadcast_to(gates, (128, gates.shape[1])).T[:CAP, 0:1])
    return jnp.concatenate(columns, axis=0)


def routed_kernel(
    rows_ref, grad_ref, weight_ref, out_ref, left_ref, right_ref, dots_ref, hidden_ref, grad_pre_ref
):
    width = rows_ref.shape[2]
    count = weight_ref.shape[1] // (2 * width)
    rows = slot_rows_of(rows_ref)
    gates = slot_gates_of(rows_ref)
    cotangent = slot_rows_of(grad_ref).astype(WIDE_TYPE)
    grads = (gates * cotangent).astype(NARROW_TYPE)
    out = jnp.zeros(rows.shape, WIDE_TYPE)
    back = jnp.zeros(rows.shape, WIDE_TYPE)
    for block in range(count):
        units = slice(block * width, (block + 1) * width)
        up = weight_ref[:, units]
        down = weight_ref[:, (count + block) * width : (count + block + 1) * width]
        hidden, grad_pre = expert_block(rows, grads, up, down)
        hidden_ref[:, units] = hidden
        grad_pre_ref[:, units] = grad_pre
        out += contract(hidden, down, 1, 0)
        back += contract(grad_pre, up, 1, 1)
    out = out.astype(NARROW_TYPE).astype(WIDE_TYPE)
    out_ref[...] = (gates * out).astype(NARROW_TYPE)
    left_ref[...] = back[:, : width // 2].astype(NARROW_TYPE)
    right_ref[...] = back[:, width // 2 :].astype(NARROW_TYPE)
    dots_ref[...] = jnp.sum(out * cotangent, axis=1, keepdims=True)


def routed_expert(rows, grads, weights, after, parts=2):
    sources, _, width = rows.shape
    count, block = sources * CAP, parts * CAP
    hidden = weights.shape[1] // 2
    narrow = jax.ShapeDtypeStruct((count, width), NARROW_TYPE)
    side = jax.ShapeDtypeStruct((count, width // 2), NARROW_TYPE)
    units = jax.ShapeDtypeStruct((count, hidden), NARROW_TYPE)
    slots = pl.BlockSpec((parts,) + rows.shape[1:], lambda step: (step, 0, 0))
    return stepped(
        routed_kernel,
        sources // parts,
        (rows, grads, weights),
        [slots, slots, whole_block(weights)],
        [row_block(block, width)]
        + [row_block(block, width // 2)] * 2
        + [row_block(block, 1)]
        + [row_block(block, hidden)] * 2,
        [narrow, side, side, jax.ShapeDtypeStruct((count, 1), WIDE_TYPE), units, units],
        after,
        "routed_expert",
    )


def sums_kernel(
    steps, rows_ref, grad_ref, hidden_ref, grad_pre_ref, *refs
):
    sums_ref, totals = refs[-2:]
    step = pl.program_id(0)
    width = rows_ref.shape[2]
    count = totals.shape[0] // 2

    @pl.when(step == 0)
    def _():
        totals[...] = jnp.zeros_like(totals)

    @pl.when(step < steps)
    def _():
        turned = slot_rows_of(rows_ref).T
        cotangent = slot_rows_of(grad_ref).astype(WIDE_TYPE)
        grads = (slot_gates_of(rows_ref) * cotangent).astype(NARROW_TYPE)
        for block in range(count):
            units = slice(block * width, (block + 1) * width)
            totals[block] += contract(turned, grad_pre_ref[:, units], 1, 0)
            totals[count + block] += contract(hidden_ref[:, units], grads, 0, 0)

    @pl.when(jnp.logical_and(step >= steps, step < steps + 2 * count))
    def _():
        sums_ref[...] = totals[jnp.clip(step - steps, 0, 2 * count - 1)].astype(NARROW_TYPE)

    if len(refs) == 3:

        @pl.when(step == steps + 2 * count)
        def _():
            sums_ref[...] = refs[0][...]


def routed_sums(rows, grads, hidden, grad_pre, side, after, extra=(), parts=4):
    sources, _, width = rows.shape
    half = hidden.shape[1] // 2
    count = half // width
    steps = sources // parts
    slots = pl.BlockSpec(
        (parts,) + rows.shape[1:], lambda step: (jnp.minimum(step, steps - 1), 0, 0)
    )
    units = pl.BlockSpec((parts * CAP, half), lambda step: (jnp.minimum(step, steps - 1), side))
    square = (width, width)
    return stepped(
        functools.partial(sums_kernel, steps),
        steps + 2 * count + len(extra),
        (rows, grads, hidden, grad_pre, *extra),
        [slots, slots, units, units] + [whole_block(block) for block in extra],
        pl.BlockSpec(square, lambda step: (0, jnp.maximum(step - steps, 0))),
        jax.ShapeDtypeStruct((width, 2 * half + len(extra) * width), NARROW_TYPE),
        after,
        "routed_sums",
        scratch_shapes=[pltpu.VMEM((2 * count,) + square, WIDE_TYPE)],
    )


def part_of_step(core, place):
    chip = lax.rem(place, 4)
    owner = jnp.where(place < 4, core, 1 - core)
    return 4 * (chip // 2) + 2 * owner + lax.rem(chip, 2)


def shared_kernel(
    local, steps, core_ref, rows_ref, grad_ref, up_ref, down_ref, out_ref, back_ref, kept_ref, sent_ref, totals
):
    step = pl.program_id(0)
    width = rows_ref.shape[1]
    count = totals.shape[0] // 2

    @pl.when(step == 0)
    def _():
        totals[...] = jnp.zeros_like(totals)

    @pl.when(step < steps)
    def _():
        rows, grads = rows_ref[...], grad_ref[...]
        turned = grads.T
        out = jnp.zeros(rows.shape, WIDE_TYPE)
        back = jnp.zeros(rows.shape, WIDE_TYPE)
        for block in range(count):
            units = slice(block * width, (block + 1) * width)
            up, down = up_ref[:, units], down_ref[:, units]
            hidden, grad_pre = expert_block(rows, grads, up, down)
            out += contract(hidden, down, 1, 0)
            back += contract(grad_pre, up, 1, 1)
            totals[block] += contract(grad_pre, rows, 0, 0)
            totals[count + block] += contract(turned, hidden, 1, 0)
        out_ref[...] = out
        back_ref[...] = back

    units = count * width // 8
    features = width // 8
    part = part_of_step(core_ref[0], jnp.maximum(step - steps, 0))

    def write(part_ref):
        for piece in range(units // local):
            number = part * (units // local) + piece
            start = pl.multiple_of((number // count) * local, 8)
            part_ref[0, piece * local : (piece + 1) * local] = totals[
                lax.rem(number, count), pl.ds(start, local)
            ].astype(NARROW_TYPE)
        for block in range(count):
            start = units + block * features
            part_ref[0, start : start + features] = totals[
                count + block, pl.ds(pl.multiple_of(part * features, 8), features)
            ].astype(NARROW_TYPE)

    @pl.when(jnp.logical_and(step >= steps, step < steps + 4))
    def _():
        write(kept_ref)

    @pl.when(step >= steps + 4)
    def _():
        write(sent_ref)


def part_specs(steps, rows, width):
    return [
        pl.BlockSpec((1, rows, width), lambda step, *_: (jnp.clip(step - steps, 0, 3), 0, 0)),
        pl.BlockSpec((1, rows, width), lambda step, *_: (jnp.clip(step - steps - 4, 0, 3), 0, 0)),
    ]


def own_core():
    return ((lax.axis_index(PLANE) // 2) % 2).reshape(1).astype(jnp.int32)


def shared_expert(rows, grads, weights, local, after, row_block=512):
    total_rows, width = rows.shape
    steps = total_rows // row_block
    count = 4
    row_spec = pl.BlockSpec((row_block, width), lambda step, core: (jnp.minimum(step, steps - 1), 0))

    def held(place):
        return pl.BlockSpec(
            (width, count * width), lambda step, core: (0, place), pipeline_mode=pl.Buffered(1)
        )

    def kernel(*refs):
        shared_kernel(local, steps, *refs[:5], *refs[5 + len(after) :])

    wide = jax.ShapeDtypeStruct((total_rows, width), WIDE_TYPE)
    return pl.pallas_call(
        kernel,
        grid_spec=pltpu.PrefetchScalarGridSpec(
            num_scalar_prefetch=1,
            grid=(steps + 8,),
            in_specs=[row_spec, row_spec, held(0), held(1)] + [ANYWHERE] * len(after),
            out_specs=[row_spec, row_spec] + part_specs(steps, width, width),
            scratch_shapes=[pltpu.VMEM((2 * count, width, width), WIDE_TYPE)],
        ),
        out_shape=[wide, wide] + [jax.ShapeDtypeStruct((4, width, width), NARROW_TYPE)] * 2,
        compiler_params=pltpu.CompilerParams(vmem_limit_bytes=61 * MEBI),
        name="shared_expert",
    )(own_core(), rows, grads, weights, weights, *after)


PLANE = ("expert", "stream")
CORE, SIDES = 2, (4, 1, 5)


def flip(value, mask):
    count = lax.axis_size(PLANE)
    return lax.ppermute(value, PLANE, [(index, index ^ mask) for index in range(count)])


def together(*values):
    return lax.optimization_barrier(values)


ANYWHERE = pl.BlockSpec(memory_space=pl.ANY)


def whole_block(operand):
    rank = len(operand.shape)
    return pl.BlockSpec(operand.shape, lambda *_: (0,) * rank, pipeline_mode=pl.Buffered(1))


def row_block(rows, columns):
    return pl.BlockSpec((rows, columns), lambda step, *_: (step, 0))


def column_block(operand, columns, place):
    return pl.BlockSpec(
        (operand.shape[0], columns), lambda step, *_: (0, place), pipeline_mode=pl.Buffered(1)
    )


def stepped(kernel, steps, operands, in_specs, out_specs, out_shape, after, name, **extra):
    given = len(operands)

    def body(*refs):
        kernel(*refs[:given], *refs[given + len(after) :])

    return pl.pallas_call(
        body,
        grid=(steps,),
        in_specs=list(in_specs) + [ANYWHERE] * len(after),
        out_specs=out_specs,
        out_shape=out_shape,
        compiler_params=pltpu.CompilerParams(vmem_limit_bytes=61 * MEBI),
        name=name,
        **extra,
    )(*operands, *after)


def depth_stack(piece):
    parts = jnp.broadcast_to(piece[None], (lax.axis_size("dp"),) + piece.shape)
    return lax.all_to_all(parts, "dp", split_axis=0, concat_axis=0, tiled=True)


def stack_kernel(*refs):
    for place, ref in enumerate(refs[:-1]):
        refs[-1][place] = ref[...]


def place_kernel(order_ref, near_ref, far_ref, out_ref):
    for place in range(4):
        chip = order_ref[place]
        first = 4 * (chip // 2) + lax.rem(chip, 2)
        out_ref[0, first + 2 * order_ref[4]] = near_ref[place, 0]
        out_ref[0, first + 2 * (1 - order_ref[4])] = far_ref[place, 0]


def side_gather(stacked):
    return [stacked] + [flip(stacked, mask) for mask in SIDES]


def near_slices(sides, after=()):
    depth, rows, columns = sides[0].shape
    slice_shape = (1, rows, columns)
    return stepped(
        stack_kernel,
        depth,
        sides,
        [pl.BlockSpec(slice_shape, lambda part: (part, 0, 0))] * 4,
        pl.BlockSpec((4,) + slice_shape, lambda part: (0, part, 0, 0)),
        jax.ShapeDtypeStruct((4, depth, rows, columns), sides[0].dtype),
        after,
        "stack_sides",
    )


def plane_gather(near):
    depth, rows, columns = near.shape[1:]
    slice_shape = (1, rows, columns)
    me = lax.axis_index(PLANE)
    chip = 2 * (me // 4) + me % 2
    far = flip(near, CORE)
    order = jnp.stack([chip, chip ^ 2, chip ^ 1, chip ^ 3, (me // 2) % 2]).astype(jnp.int32)
    source = pl.BlockSpec((4,) + slice_shape, lambda part, order: (0, part, 0, 0))
    placed = pl.pallas_call(
        place_kernel,
        grid_spec=pltpu.PrefetchScalarGridSpec(
            num_scalar_prefetch=1,
            grid=(depth,),
            in_specs=[source] * 2,
            out_specs=pl.BlockSpec((1, 8, rows, columns), lambda part, order: (part, 0, 0, 0)),
        ),
        out_shape=jax.ShapeDtypeStruct((depth, 8, rows, columns), near.dtype),
        compiler_params=pltpu.CompilerParams(vmem_limit_bytes=61 * MEBI),
        name="place_slices",
    )(order, near, far)
    return placed.reshape(depth * 8 * rows, columns)


def pair_kernel(place_ref, kept_ref, other_ref, *refs):
    own_ref, *side_refs = refs[-4:]
    place = place_ref[0]
    own_ref[...] = kept_ref[place].astype(WIDE_TYPE) + other_ref[place].astype(WIDE_TYPE)
    for side_ref, other in zip(side_refs, (2, 1, 3)):
        chip = place ^ other
        total = kept_ref[chip].astype(WIDE_TYPE) + other_ref[chip].astype(WIDE_TYPE)
        side_ref[...] = total.astype(NARROW_TYPE)


def finish_kernel(own_ref, *refs):
    total = own_ref[...]
    for ref in refs[:3]:
        total += ref[...].astype(WIDE_TYPE)
    refs[-1][...] = total.T.astype(NARROW_TYPE)


def pair_sum(kept, other, after=(), columns=256):
    me = lax.axis_index(PLANE)
    place = (2 * (me // 4) + me % 2).reshape(1).astype(jnp.int32)
    rows, width = kept.shape[1:]
    stack = pl.BlockSpec((4, rows, columns), lambda step, place: (0, 0, step))
    flat = pl.BlockSpec((rows, columns), lambda step, *_: (0, step))
    narrow = jax.ShapeDtypeStruct((rows, width), NARROW_TYPE)
    return pl.pallas_call(
        pair_kernel,
        grid_spec=pltpu.PrefetchScalarGridSpec(
            num_scalar_prefetch=1,
            grid=(width // columns,),
            in_specs=[stack, stack] + [ANYWHERE] * len(after),
            out_specs=[flat] * 4,
        ),
        out_shape=[jax.ShapeDtypeStruct((rows, width), WIDE_TYPE)] + [narrow] * 3,
        compiler_params=pltpu.CompilerParams(vmem_limit_bytes=61 * MEBI),
        name="pair_sum",
    )(place, kept, other, *after)


def side_flips(sides):
    return [flip(side, mask) for side, mask in zip(sides, SIDES)]


def side_sum(own, *sides, after=(), columns=256):
    rows, width = own.shape
    flat = pl.BlockSpec((rows, columns), lambda step, *_: (0, step))
    return pl.pallas_call(
        finish_kernel,
        grid=(width // columns,),
        in_specs=[flat] * 4 + [ANYWHERE] * len(after),
        out_specs=pl.BlockSpec((columns, rows), lambda step: (step, 0)),
        out_shape=jax.ShapeDtypeStruct((width, rows), NARROW_TYPE),
        compiler_params=pltpu.CompilerParams(vmem_limit_bytes=61 * MEBI),
        name="side_sum",
    )(own, *sides, *after)


def last_kernel(
    core_ref, joined_ref, first_ref, grad_ref, attended_ref, logits_ref, second_ref, kept_ref, sent_ref, totals, router
):
    step = pl.program_id(0)
    width = first_ref.shape[1]

    @pl.when(step < 3)
    def _():
        start = pl.multiple_of(step * width, 8)
        totals[pl.ds(start, width)] = contract(joined_ref[0], first_ref[...], 0, 0)

    @pl.when(step == 3)
    def _():
        totals[3 * width :] = contract(grad_ref[...], attended_ref[...], 0, 0)
        router[...] = contract(logits_ref[...], second_ref[...], 0, 0)

    part = part_of_step(core_ref[0], jnp.maximum(step - 4, 0))

    def write(part_ref):
        place = 0
        for start, rows in ((0, 3 * width // 8), (3 * width, width // 8)):
            first = pl.multiple_of(start + part * rows, 8)
            part_ref[0, place : place + rows] = totals[pl.ds(first, rows)].astype(NARROW_TYPE)
            place += rows
        number = lax.broadcasted_iota(jnp.int32, router.shape, 0)
        column = jnp.sum(jnp.where(number == part, router[...], 0.0), axis=0, keepdims=True)
        tail = part_ref.shape[1] - place
        row = lax.broadcasted_iota(jnp.int32, (tail, width), 0)
        part_ref[0, place:] = jnp.where(row == 0, column, 0.0).astype(NARROW_TYPE)

    @pl.when(jnp.logical_and(step >= 4, step < 8))
    def _():
        write(kept_ref)

    @pl.when(step >= 8)
    def _():
        write(sent_ref)


def last_gradients(grad_joined, first_in, grad_attention, attended, grad_logits, second_in, after):
    count, width = first_in.shape
    rows = width // 2 + 16
    flat = pl.BlockSpec((count, width), lambda step, core: (0, 0))
    thin = pl.BlockSpec((count, grad_logits.shape[1]), lambda step, core: (0, 0))
    def kernel(*refs):
        last_kernel(*refs[:7], *refs[7 + len(after) :])

    return pl.pallas_call(
        kernel,
        grid_spec=pltpu.PrefetchScalarGridSpec(
            num_scalar_prefetch=1,
            grid=(12,),
            in_specs=[
                pl.BlockSpec((1, count, width), lambda step, core: (jnp.minimum(step, 2), 0, 0)),
                flat,
                flat,
                flat,
                thin,
                flat,
            ]
            + [ANYWHERE] * len(after),
            out_specs=part_specs(4, rows, width),
            scratch_shapes=[
                pltpu.VMEM((4 * width, width), WIDE_TYPE),
                pltpu.VMEM((grad_logits.shape[1], width), WIDE_TYPE),
            ],
        ),
        out_shape=[jax.ShapeDtypeStruct((4, rows, width), NARROW_TYPE)] * 2,
        compiler_params=pltpu.CompilerParams(vmem_limit_bytes=61 * MEBI),
        name="last_gradients",
    )(own_core(), grad_joined, first_in, grad_attention, attended, grad_logits, second_in, *after)


def depth_shift(value, shift):
    depth = lax.axis_size("dp")
    return lax.ppermute(value, "dp", [(index, (index + shift) % depth) for index in range(depth)])


def depth_scatter(parts):
    depth = lax.axis_size("dp")
    blocks = parts.reshape(depth, parts.shape[0] // depth, parts.shape[1])
    if depth > 8:
        blocks = lax.all_to_all(blocks, "dp", split_axis=0, concat_axis=0, tiled=True)
        return jnp.sum(blocks.astype(WIDE_TYPE), axis=0)
    me = lax.axis_index("dp")
    total = lax.dynamic_index_in_dim(blocks, me, 0, keepdims=False).astype(WIDE_TYPE)
    for shift in range(1, depth):
        part = lax.dynamic_index_in_dim(blocks, (me + shift) % depth, 0, keepdims=False)
        total = total + depth_shift(part, shift).astype(WIDE_TYPE)
    return total


def first_payload_kernel(place_ref, qkv_ref, out_ref, router_ref, cond_ref, payload_ref):
    del place_ref
    depth, rows, columns = payload_ref.shape
    slots = cond_ref.shape[0]
    local = cond_ref.shape[1] // depth
    qkv_end = qkv_ref.shape[1]
    out_end = qkv_end + out_ref.shape[1]
    router_end = out_end + 128
    silu = cond_ref[...].astype(WIDE_TYPE)
    silu = silu * jax.nn.sigmoid(silu)
    router = jnp.concatenate(
        [router_ref[...].astype(WIDE_TYPE), jnp.zeros((rows, 128 - router_ref.shape[1]), WIDE_TYPE)],
        axis=1,
    ).astype(NARROW_TYPE)
    payload_ref[...] = jnp.zeros_like(payload_ref)
    for part in range(depth):
        payload_ref[part, :, :qkv_end] = qkv_ref[...]
        payload_ref[part, :, qkv_end:out_end] = out_ref[...]
        payload_ref[part, :, out_end:router_end] = router
        tail = jnp.concatenate(
            [silu[:, part * local : (part + 1) * local], jnp.zeros((slots, columns - router_end - local), WIDE_TYPE)],
            axis=1,
        )
        tail = jnp.concatenate([tail, jnp.zeros((rows - slots, columns - router_end), WIDE_TYPE)], axis=0)
        payload_ref[part, :, router_end:] = tail.astype(NARROW_TYPE)


def first_payload(qkv, out, router, cond, depth, rows):
    place = lax.axis_index(PLANE).reshape(1).astype(jnp.int32)
    local = cond.shape[1] // depth
    columns = qkv.shape[1] + out.shape[1] + 128 + local + -local % 128

    def slice_of(operand):
        return pl.BlockSpec((rows, operand.shape[1]), lambda step, place: (place[0], 0))

    return pl.pallas_call(
        first_payload_kernel,
        grid_spec=pltpu.PrefetchScalarGridSpec(
            num_scalar_prefetch=1,
            grid=(1,),
            in_specs=[slice_of(qkv), slice_of(out), slice_of(router), whole_block(cond)],
            out_specs=pl.BlockSpec((depth, rows, columns), lambda step, place: (0, 0, 0)),
        ),
        out_shape=jax.ShapeDtypeStruct((depth, rows, columns), NARROW_TYPE),
        compiler_params=pltpu.CompilerParams(vmem_limit_bytes=61 * MEBI),
        name="first_payload",
    )(place, qkv, out, router, cond)


def rest_payload_kernel(local, place_ref, up_ref, down_ref, *refs):
    del place_ref
    payload_ref = refs[-1]
    hidden = up_ref.shape[1]
    width = down_ref.shape[2]
    depth = hidden // (4 * local)
    for block in range(4):
        for part in range(depth):
            target = (block * depth + part) * local
            source = (part * 4 + block) * local
            payload_ref[:, target : target + local] = up_ref[:, source : source + local]
        start = hidden + block * width
        payload_ref[:, start : start + width] = down_ref[block]


def rest_payload(up, down, rows, after):
    place = lax.axis_index(PLANE).reshape(1).astype(jnp.int32)
    local, hidden = up.shape
    width = down.shape[1]
    shape = (rows, hidden + 4 * width)
    return pl.pallas_call(
        functools.partial(rest_payload_kernel, local),
        grid_spec=pltpu.PrefetchScalarGridSpec(
            num_scalar_prefetch=1,
            grid=(1,),
            in_specs=[
                pl.BlockSpec((rows, hidden), lambda step, place: (place[0], 0)),
                pl.BlockSpec((4, rows, width), lambda step, place: (0, place[0], 0)),
            ]
            + [ANYWHERE] * len(after),
            out_specs=pl.BlockSpec(shape, lambda step, place: (0, 0)),
        ),
        out_shape=jax.ShapeDtypeStruct(shape, NARROW_TYPE),
        compiler_params=pltpu.CompilerParams(vmem_limit_bytes=61 * MEBI),
        name="rest_payload",
    )(place, up, down.reshape(4, local, width), *after)


def expert_payload_kernel(up_ref, down_ref, *refs):
    payload_ref = refs[-1]
    local, hidden = up_ref.shape
    width = down_ref.shape[1]
    depth = hidden // (4 * local)
    for block in range(4):
        for part in range(depth):
            target = (block * depth + part) * local
            source = (part * 4 + block) * local
            payload_ref[:, target : target + local] = up_ref[:, source : source + local]
        start = hidden + block * width
        payload_ref[:, start : start + width] = down_ref[block * local : (block + 1) * local, :]


def expert_payload(up, down, after):
    local, hidden = up.shape
    whole = pl.BlockSpec(memory_space=pltpu.VMEM)
    return pl.pallas_call(
        expert_payload_kernel,
        in_specs=[whole, whole] + [ANYWHERE] * len(after),
        out_specs=whole,
        out_shape=jax.ShapeDtypeStruct((local, hidden + 4 * down.shape[1]), up.dtype),
        compiler_params=pltpu.CompilerParams(vmem_limit_bytes=61 * MEBI),
        name="expert_payload",
    )(up, down, *after)


def normalize_rows(values):
    centre = values - jnp.mean(values, axis=-1, keepdims=True)
    spread = jnp.mean(centre * centre, axis=-1, keepdims=True)
    reciprocal = lax.rsqrt(spread + EPSILON)
    return centre * reciprocal, reciprocal


def normalize_rows_back(gradient, normed, reciprocal):
    mean = jnp.mean(gradient, axis=-1, keepdims=True)
    along = jnp.mean(gradient * normed, axis=-1, keepdims=True)
    return reciprocal * (gradient - mean - normed * along)


def pick_slots(first, count, places_ref):
    patches = places_ref.shape[1]
    slot = first + lax.broadcasted_iota(jnp.int32, (count, patches), 0)
    return jnp.logical_or(slot == places_ref[0:1, :], slot == places_ref[1:2, :])


def one(mask):
    return jnp.where(mask, 1.0, 0.0).astype(NARROW_TYPE)


def mixture_kernel(grad_ref, mods_ref, places_ref, silu_ref, shared_ref, out_ref):
    step = pl.program_id(0)
    quarter = grad_ref.shape[0] // 4

    @pl.when(step == 0)
    def _():
        for part in range(4):
            rows = slice(part * quarter, (part + 1) * quarter)
            gradient = grad_ref[rows, :].astype(WIDE_TYPE) * mods_ref[part, 5:6, :]
            shared_ref[rows, :] = gradient.astype(NARROW_TYPE)

    parts = out_ref.shape[0]
    taken = one(pick_slots(step * parts * CAP, parts * CAP, places_ref))
    rows = contract(taken, shared_ref[...], 1, 0).astype(NARROW_TYPE)
    for part in range(parts):
        out_ref[part, :CAP] = rows[part * CAP : (part + 1) * CAP]
        out_ref[part, CAP:] = jnp.zeros((SPARE, out_ref.shape[2]), NARROW_TYPE)
        out_ref[part, CAP:, : silu_ref.shape[1]] = silu_ref[...]


def slot_block(width):
    return pl.BlockSpec((2, CAP + SPARE, width), lambda step: (step, 0, 0))


def spread_mixture(out_grad, mods, places, silu, after):
    count, width = out_grad.shape
    return stepped(
        mixture_kernel,
        4,
        (out_grad, mods, places, silu),
        [whole_block(operand) for operand in (out_grad, mods, places, silu)],
        [pl.BlockSpec((count, width), lambda step: (0, 0)), slot_block(width)],
        [
            jax.ShapeDtypeStruct((count, width), NARROW_TYPE),
            jax.ShapeDtypeStruct((8, CAP + SPARE, width), NARROW_TYPE),
        ],
        after,
        "spread_mixture",
    )


def first_kernel(patch_ref, mods_ref, weight_ref, first_ref, joined_ref):
    normed, _ = normalize_rows(patch_ref[...].astype(WIDE_TYPE))
    first = (normed * (1.0 + mods_ref[0, 1:2, :]) + mods_ref[0, 0:1, :]).astype(NARROW_TYPE)
    first_ref[...] = first
    width = first.shape[1]
    for part in range(3):
        columns = slice(part * width, (part + 1) * width)
        joined_ref[part] = contract(first, weight_ref[:, columns], 1, 0).astype(NARROW_TYPE)


def mods_block(mods, quarters=1):
    return pl.BlockSpec((quarters,) + mods.shape[1:], lambda step, *_: (step, 0, 0))


def first_half(patches, mods, weights, after):
    count, width = patches.shape
    quarter = count // 4
    rows = row_block(quarter, width)
    return stepped(
        first_kernel,
        4,
        (patches, mods, weights),
        [rows, mods_block(mods), column_block(weights, 3 * width, 0)],
        [rows, pl.BlockSpec((3, quarter, width), lambda step: (0, step, 0))],
        [
            jax.ShapeDtypeStruct((count, width), NARROW_TYPE),
            jax.ShapeDtypeStruct((3, count, width), NARROW_TYPE),
        ],
        after,
        "first_half",
    )


def second_kernel(
    attended_ref, patch_ref, mods_ref, routes_ref, out_ref, router_ref, attention_ref, middle_ref, second_ref, gates_ref, gate_rows_ref
):
    attention = contract(attended_ref[...], out_ref[...], 1, 0)
    attention_ref[...] = attention
    middle = patch_ref[...].astype(WIDE_TYPE) + mods_ref[0, 2:3, :] * attention
    middle_ref[...] = middle
    normed, _ = normalize_rows(middle)
    second = (normed * (1.0 + mods_ref[0, 4:5, :]) + mods_ref[0, 3:4, :]).astype(NARROW_TYPE)
    second_ref[...] = second
    logits = contract(second, router_ref[...], 1, 0)
    lane = lax.broadcasted_iota(jnp.int32, logits.shape, 1)
    picked = [
        jnp.sum(jnp.where(lane == routes_ref[:, k : k + 1], logits, 0.0), axis=1, keepdims=True)
        for k in range(TOP)
    ]
    summit = jnp.maximum(picked[0], picked[1])
    weights = [jnp.exp(value - summit) for value in picked]
    total = weights[0] + weights[1]
    gates = [weight / total for weight in weights]
    gates_ref[...] = jnp.concatenate(gates, axis=1)
    wide = jnp.where(lane == 0, gates[0], jnp.where(lane == 1, gates[1], 0.0))
    gate_rows_ref[...] = wide.T[0:TOP, :]


def second_half(attended, patches, mods, routes, weights, after):
    count, width = patches.shape
    quarter = count // 4
    rows = row_block(quarter, width)
    pair = row_block(quarter, TOP)
    wide = jax.ShapeDtypeStruct((count, width), WIDE_TYPE)
    return stepped(
        second_kernel,
        4,
        (attended, patches, mods, routes, weights, weights),
        [
            rows,
            rows,
            mods_block(mods),
            pair,
            column_block(weights, width, 3),
            column_block(weights, 128, 4 * width // 128),
        ],
        [rows, rows, rows, pair, pl.BlockSpec((TOP, quarter), lambda step: (0, step))],
        [
            wide,
            wide,
            jax.ShapeDtypeStruct((count, width), NARROW_TYPE),
            jax.ShapeDtypeStruct((count, TOP), WIDE_TYPE),
            jax.ShapeDtypeStruct((TOP, count), WIDE_TYPE),
        ],
        after,
        "second_half",
    )


def spread_kernel(second_ref, places_ref, gates_ref, rows_ref):
    parts = rows_ref.shape[0]
    first = pl.program_id(0) * parts * CAP
    slots = pick_slots(first, parts * CAP, places_ref)
    rows = contract(one(slots), second_ref[...], 1, 0).astype(NARROW_TYPE)
    slot = first + lax.broadcasted_iota(jnp.int32, slots.shape, 0)
    total = jnp.where(slot == places_ref[0:1, :], gates_ref[0:1, :], 0.0)
    total += jnp.where(slot == places_ref[1:2, :], gates_ref[1:2, :], 0.0)
    column = jnp.sum(total, axis=1, keepdims=True)
    gates = jnp.broadcast_to(column, (parts * CAP, 128)).T[0:SPARE, :]
    row = lax.broadcasted_iota(jnp.int32, gates.shape, 0)
    terms = jnp.zeros(gates.shape, WIDE_TYPE)
    for number in range(3):
        term = gates.astype(NARROW_TYPE).astype(WIDE_TYPE)
        terms = jnp.where(row == number, term, terms)
        gates = gates - term
    for part in range(parts):
        own = slice(part * CAP, (part + 1) * CAP)
        rows_ref[part, :CAP] = rows[own]
        rows_ref[part, CAP:] = jnp.zeros((SPARE, rows_ref.shape[2]), NARROW_TYPE)
        rows_ref[part, CAP:, :CAP] = terms[:, own].astype(NARROW_TYPE)


def spread_second(second_in, places, gates, after):
    width = second_in.shape[1]
    operands = (second_in, places, gates)
    return stepped(
        spread_kernel,
        4,
        operands,
        [whole_block(operand) for operand in operands],
        slot_block(width),
        jax.ShapeDtypeStruct((8, CAP + SPARE, width), NARROW_TYPE),
        after,
        "spread_second",
    )


def middle_kernel(
    left_ref,
    right_ref,
    dots_ref,
    columns_ref,
    routes_ref,
    gates_ref,
    shared_ref,
    middle_ref,
    attention_ref,
    mods_ref,
    grad_ref,
    out_ref,
    router_ref,
    grad_middle_ref,
    grad_attention_ref,
    grad_attended_ref,
    grad_logits_ref,
    sums_ref,
):
    count, width = middle_ref.shape
    quarters = mods_ref.shape[0]
    quarter = count // quarters
    slot = lax.broadcasted_iota(jnp.int32, (count, left_ref.shape[0]), 1)
    takes = [slot == columns_ref[:, k : k + 1] for k in range(TOP)]
    taken = one(jnp.logical_or(*takes))
    collected = [contract(taken, ref[...], 1, 0) for ref in (left_ref, right_ref)]
    collected = jnp.concatenate(collected, axis=1)
    gates = [gates_ref[:, k : k + 1] for k in range(TOP)]
    grad_gate = [
        jnp.sum(jnp.where(take, dots_ref[...], 0.0), axis=1, keepdims=True) for take in takes
    ]
    centre = gates[0] * grad_gate[0] + gates[1] * grad_gate[1]
    lane = lax.broadcasted_iota(jnp.int32, grad_logits_ref.shape, 1)
    grad_logits = jnp.zeros(grad_logits_ref.shape, WIDE_TYPE)
    for k in range(TOP):
        picked = gates[k] * (grad_gate[k] - centre)
        grad_logits += jnp.where(lane == routes_ref[:, k : k + 1], picked, 0.0)
    grad_logits = grad_logits.astype(NARROW_TYPE)
    grad_logits_ref[...] = grad_logits
    grad_second = shared_ref[...] + contract(grad_logits, router_ref[...], 1, 1) + collected
    normed, reciprocal = normalize_rows(middle_ref[...])
    grad_middle = grad_ref[...].astype(WIDE_TYPE) + normalize_rows_back(
        grad_second * (1.0 + mods_rows(mods_ref, 4, quarter)), normed, reciprocal
    )
    grad_middle_ref[...] = grad_middle
    grad_attention = (grad_middle * mods_rows(mods_ref, 2, quarter)).astype(NARROW_TYPE)
    grad_attention_ref[...] = grad_attention
    grad_attended_ref[...] = contract(grad_attention, out_ref[...], 1, 1).astype(NARROW_TYPE)
    totals = [grad_middle * attention_ref[...], grad_second, grad_second * normed]
    totals = [quarter_sums(total, quarters) for total in totals]
    for part in range(quarters):
        sums_ref[part] = jnp.concatenate([total[part] for total in totals], axis=0)


def sums_block(count, width, quarters=1):
    return pl.BlockSpec((quarters, count, width), lambda step: (step, 0, 0))


def mods_rows(mods_ref, piece, quarter):
    parts = [
        jnp.broadcast_to(mods_ref[part, piece : piece + 1, :], (quarter, mods_ref.shape[2]))
        for part in range(mods_ref.shape[0])
    ]
    return jnp.concatenate(parts, axis=0)


def quarter_sums(values, quarters):
    rows = values.shape[0] // quarters
    return [
        jnp.sum(values[part * rows : (part + 1) * rows], axis=0, keepdims=True)
        for part in range(quarters)
    ]


def middle_back(
    left, right, dots, columns, routes, gates, grad_shared, middle, attention, mods, out_grad, weights, after
):
    count, width = middle.shape
    half = count // 2
    rows, pair, lanes = row_block(half, width), row_block(half, TOP), row_block(half, 128)
    narrow = jax.ShapeDtypeStruct((count, width), NARROW_TYPE)
    return stepped(
        middle_kernel,
        2,
        (left, right, dots, columns, routes, gates, grad_shared, middle, attention, mods, out_grad, weights, weights),
        [whole_block(left), whole_block(right), whole_block(dots), pair, pair, pair, rows, rows, rows]
        + [mods_block(mods, 2), rows]
        + [column_block(weights, width, 3), column_block(weights, 128, 4 * width // 128)],
        [rows, rows, rows, lanes, sums_block(3, width, 2)],
        [
            jax.ShapeDtypeStruct((count, width), WIDE_TYPE),
            narrow,
            narrow,
            jax.ShapeDtypeStruct((count, 128), NARROW_TYPE),
            jax.ShapeDtypeStruct((4, 3, width), WIDE_TYPE),
        ],
        after,
        "middle_back",
    )


def output_kernel(
    result_ref, columns_ref, shared_ref, middle_ref, mods_ref, grad_ref, out_ref, sums_ref
):
    count = middle_ref.shape[0]
    quarters = mods_ref.shape[0]
    slot = lax.broadcasted_iota(jnp.int32, (count, result_ref.shape[0]), 1)
    takes = [slot == columns_ref[:, k : k + 1] for k in range(TOP)]
    mixture = shared_ref[...] + contract(one(jnp.logical_or(*takes)), result_ref[...], 1, 0)
    gate = mods_rows(mods_ref, 5, count // quarters)
    out_ref[...] = (middle_ref[...] + gate * mixture).astype(NARROW_TYPE)
    totals = quarter_sums(grad_ref[...].astype(WIDE_TYPE) * mixture, quarters)
    for part in range(quarters):
        sums_ref[part] = totals[part]


def block_output(result, columns, shared, middle, mods, out_grad, after):
    count, width = middle.shape
    half = count // 2
    rows, pair = row_block(half, width), row_block(half, TOP)
    return stepped(
        output_kernel,
        2,
        (result, columns, shared, middle, mods, out_grad),
        [whole_block(result), pair, rows, rows, mods_block(mods, 2), rows],
        [rows, sums_block(1, width, 2)],
        [
            jax.ShapeDtypeStruct((count, width), NARROW_TYPE),
            jax.ShapeDtypeStruct((4, 1, width), WIDE_TYPE),
        ],
        after,
        "block_output",
    )


def start_kernel(joined_ref, weight_ref, patch_ref, mods_ref, middle_ref, out_ref, sums_ref):
    width = patch_ref.shape[1]
    grad_first = jnp.zeros(patch_ref.shape, WIDE_TYPE)
    for part in range(3):
        columns = slice(part * width, (part + 1) * width)
        grad_first += contract(joined_ref[part], weight_ref[:, columns], 1, 1)
    normed, reciprocal = normalize_rows(patch_ref[...].astype(WIDE_TYPE))
    out_ref[...] = middle_ref[...] + normalize_rows_back(
        grad_first * (1.0 + mods_ref[0, 1:2, :]), normed, reciprocal
    )
    sums_ref[0] = jnp.concatenate(
        [
            jnp.sum(grad_first, axis=0, keepdims=True),
            jnp.sum(grad_first * normed, axis=0, keepdims=True),
        ],
        axis=0,
    )


def start_back(grad_joined, weights, patches, mods, grad_middle, after):
    count, width = patches.shape
    quarter = count // 4
    rows = row_block(quarter, width)
    return stepped(
        start_kernel,
        4,
        (grad_joined, weights, patches, mods, grad_middle),
        [
            pl.BlockSpec((3, quarter, width), lambda step: (0, step, 0)),
            column_block(weights, 3 * width, 0),
            rows,
            mods_block(mods),
            rows,
        ],
        [rows, sums_block(2, width)],
        [
            jax.ShapeDtypeStruct((count, width), WIDE_TYPE),
            jax.ShapeDtypeStruct((4, 2, width), WIDE_TYPE),
        ],
        after,
        "start_back",
    )


def expert_sums_kernel(early_ref, late_ref, up_ref, down_ref):
    local, hidden = up_ref.shape
    width = down_ref.shape[1]
    depth = hidden // (4 * local)
    for block in range(4):
        ref = (early_ref, late_ref)[block // 2]
        for part in range(depth):
            source = (block % 2) * width + part * local
            target = (part * 4 + block) * local
            up_ref[:, target : target + local] = ref[:, source : source + local].astype(WIDE_TYPE)
        source = (2 + block % 2) * width
        down_ref[block * local : (block + 1) * local] = ref[:, source : source + width].astype(WIDE_TYPE)


def expert_sums(early, late):
    local, hidden = early.shape
    width = hidden // 4
    return stepped(
        expert_sums_kernel,
        1,
        (early, late),
        [whole_block(early), column_block(late, hidden, 0)],
        [
            pl.BlockSpec((local, hidden), lambda step: (0, 0)),
            pl.BlockSpec((4 * local, width), lambda step: (0, 0)),
        ],
        [
            jax.ShapeDtypeStruct((local, hidden), WIDE_TYPE),
            jax.ShapeDtypeStruct((4 * local, width), WIDE_TYPE),
        ],
        (),
        "expert_sums",
    )


def slot_of_routes(route_rows, expert_count, capacity):
    pair_ids = route_rows.reshape(-1)
    onehot = (pair_ids[:, None] == jnp.arange(expert_count, dtype=jnp.int32)[None, :]).astype(
        jnp.int32
    )
    rank_values = jnp.cumsum(onehot, axis=0) - onehot
    slot_index = jnp.sum(rank_values * onehot, axis=1)
    return (pair_ids * capacity + slot_index).reshape(route_rows.shape)


def on_device(
    patches,
    cond,
    long_pack,
    routes,
    ada_weight,
    qkv_weight,
    out_weight,
    router_weight,
    shared_up,
    shared_down,
    expert_up,
    expert_down,
    out_grad,
):
    width = patches.shape[1]
    hidden = shared_up.shape[1]
    depth = lax.axis_size("dp")
    experts = lax.axis_size(PLANE)
    capacity = CAP
    slots = experts * capacity
    local = qkv_weight.shape[0]
    slice_rows = local // experts
    plane_index = lax.axis_index(PLANE)

    def blocked(columns):
        split = columns.reshape(columns.shape[0], depth, 4, local)
        return jnp.transpose(split, (0, 2, 1, 3)).reshape(columns.shape)

    def own(rows):
        return lax.dynamic_slice_in_dim(rows, plane_index * slice_rows, slice_rows, 0)

    places = slot_of_routes(routes, experts, capacity)
    columns, places = places, places.T
    expert_piece = expert_payload(expert_up[0], expert_down[0], ())

    cond_wide = cond.astype(WIDE_TYPE)
    cond_rows = cond.shape[0]
    if slice_rows % 8 == 0:
        first_stack = lax.all_to_all(
            first_payload(qkv_weight, out_weight, router_weight, cond, depth, slice_rows),
            "dp",
            split_axis=0,
            concat_axis=0,
            tiled=True,
        )
        first_end = 4 * width + 128
        silu_parts = first_stack[:, :cond_rows, first_end : first_end + local]
        rest_piece = rest_payload(
            shared_up, shared_down, slice_rows, (first_stack, places, expert_piece)
        )
    else:
        silu_cond = jax.nn.silu(cond_wide).astype(NARROW_TYPE)
        silu_parts = lax.all_to_all(
            jnp.transpose(silu_cond.reshape(cond_rows, depth, local), (1, 0, 2)),
            "dp",
            split_axis=0,
            concat_axis=0,
            tiled=True,
        )
        router_slice = jnp.pad(own(router_weight), ((0, 0), (0, 128 - router_weight.shape[1])))
        first_stack = depth_stack(
            jnp.concatenate([own(qkv_weight), own(out_weight), router_slice], axis=1)
        )
        down_slice = lax.dynamic_slice_in_dim(
            shared_down.reshape(4, local, width), plane_index * slice_rows, slice_rows, 1
        )
        rest_piece = jnp.concatenate(
            [
                blocked(own(shared_up)),
                jnp.transpose(down_slice, (1, 0, 2)).reshape(slice_rows, 4 * width),
            ],
            axis=1,
        )
    silu_parts = silu_parts.reshape(depth * cond_rows, local)
    partial = product_plain_operands(silu_parts, ada_weight)
    first_sides = side_gather(first_stack)
    rest_stack = lax.all_gather(rest_piece, "dp", axis=0)
    modulation = jnp.sum(
        lax.all_to_all(
            partial.reshape(depth, cond_rows, 6 * width), "dp", split_axis=0, concat_axis=0, tiled=True
        ),
        axis=0,
    )
    blocks = modulation.reshape(4, 6, width)
    is_long = long_pack[0] == 1
    mods = jnp.where(is_long, blocks[:1], blocks)

    def exchange(rows):
        return lax.all_to_all(rows, PLANE, split_axis=0, concat_axis=0, tiled=True)

    grad_shared, mixture_slots = spread_mixture(
        out_grad, mods, places, silu_parts.reshape(SPARE, -1), ()
    )
    first_near = near_slices(first_sides, (mixture_slots,))
    expert_piece, first_near = together(expert_piece, first_near)
    expert_weights = lax.all_gather(expert_piece, "dp", axis=0, tiled=True)
    mixture_slots = exchange(mixture_slots)
    first_full = plane_gather(first_near)
    rest_sides = side_gather(rest_stack)
    first_in, joined = first_half(patches, mods, first_full, ())
    attended, log_total = attend(long_pack, joined)
    attended, mixture_slots = together(attended, mixture_slots)
    attention, middle, second_in, gate_values, gate_rows = second_half(
        attended, patches, mods, routes, first_full, ()
    )
    slot_rows = spread_second(second_in, places, gate_rows, ())
    rest = plane_gather(near_slices(rest_sides, (attended, slot_rows)))
    slots_there = exchange(slot_rows)

    shared, grad_from_shared, kept, sent = shared_expert(
        second_in, grad_shared, rest, local, (slot_rows,)
    )
    sent, slots_there = together(sent, slots_there)
    routed = (slots_there, mixture_slots)
    silu_all = mixture_slots[:, capacity:, : silu_parts.size // SPARE]
    silu_all = silu_all.reshape(experts, depth, cond_rows, local)
    silu_all = jnp.transpose(silu_all, (1, 0, 2, 3)).reshape(depth * experts * cond_rows, local)
    middle_own, *middle_sides = pair_sum(kept, flip(sent, CORE))
    middle_sides = side_flips(middle_sides)
    result_rows, *grad_rows, gate_dots, units, grad_units = routed_expert(
        *routed, expert_weights, (middle_own,)
    )
    *middle_sides, left, right = together(*middle_sides, *grad_rows)
    left_back = exchange(left.reshape(experts, capacity, width // 2))
    left_back, gate_dots = together(left_back, gate_dots)
    left_back = left_back.reshape(slots, width // 2)
    gate_dots_back = exchange(gate_dots.reshape(experts, 1, capacity)).reshape(1, slots)
    early_sums = routed_sums(*routed, units, grad_units, 0, ())
    early_sums, left_back = together(early_sums, left_back)
    early_final = lax.psum_scatter(early_sums, "dp", scatter_dimension=0, tiled=True)
    middle_sum = side_sum(middle_own, *middle_sides, after=(early_sums,))
    right, middle_sum = together(right, middle_sum)
    right_back = exchange(right.reshape(experts, capacity, width // 2)).reshape(slots, width // 2)
    late_sums = routed_sums(*routed, units, grad_units, 1, (early_sums,), (middle_sum,))

    grad_middle, grad_attention, grad_attended, grad_logits, middle_sums = middle_back(
        left_back,
        right_back,
        gate_dots_back,
        columns,
        routes,
        gate_values,
        grad_from_shared,
        middle,
        attention,
        mods,
        out_grad,
        first_full,
        (silu_all,),
    )
    late_sums, grad_attended = together(late_sums, grad_attended)
    late_final = lax.psum_scatter(late_sums, "dp", scatter_dimension=0, tiled=True)
    result_back = exchange(result_rows.reshape(experts, capacity, width)).reshape(slots, width)
    grad_joined = attend_back(long_pack, joined, log_total, grad_attended, ())
    last_parts = last_gradients(
        grad_joined, first_in, grad_attention, attended, grad_logits, second_in, (result_back,)
    )
    block_out, output_sums = block_output(
        result_back,
        columns,
        shared,
        middle,
        mods,
        out_grad,
        (*last_parts, early_final),
    )
    last_pair = pair_sum(last_parts[0], flip(last_parts[1], CORE), (output_sums,))
    patches_grad, start_sums = start_back(
        grad_joined, first_full, patches, mods, grad_middle, tuple(last_pair)
    )
    last_sides = side_flips(last_pair[1:])
    grad_chosen = jnp.concatenate([start_sums, middle_sums, output_sums], axis=1)
    grad_chosen = grad_chosen.reshape(1, 4, 6 * width)
    long_total = jnp.sum(grad_chosen, axis=1, keepdims=True)
    first_slot = (jnp.arange(4, dtype=jnp.int32) == 0)[None, :, None]
    grad_blocks = jnp.where(is_long, jnp.where(first_slot, long_total, 0.0), grad_chosen)
    grad_modulation = grad_blocks.reshape(cond_rows, 6 * width).astype(NARROW_TYPE)
    everyone = ("dp",) + PLANE
    columns = 6 * width // experts
    grad_columns = jnp.transpose(grad_modulation.reshape(cond_rows, experts, columns), (1, 0, 2))
    *last_sides, grad_columns = together(*last_sides, grad_columns)
    last_sum = side_sum(last_pair[0], *last_sides)
    grad_columns = jnp.broadcast_to(grad_columns[None], (depth, experts, cond_rows, columns))
    grad_columns = lax.all_to_all(
        grad_columns.reshape(depth * experts, cond_rows, columns),
        everyone,
        split_axis=0,
        concat_axis=0,
        tiled=True,
    ).reshape(depth * experts * cond_rows, columns)
    grad_columns, last_sum = together(grad_columns, last_sum)
    ada_weight_grad = product_left_operand(silu_all, grad_columns)
    own_ada = lax.dynamic_slice_in_dim(ada_weight, plane_index * columns, columns, 1)
    silu_back = product_right_operand(grad_columns, own_ada)
    silu_back = lax.all_to_all(
        silu_back.reshape(depth * experts, cond_rows, local),
        everyone,
        split_axis=0,
        concat_axis=0,
        tiled=True,
    )
    silu_back, late_final = together(silu_back, late_final)
    silu_back = jnp.sum(silu_back.reshape(depth, experts, cond_rows, local), axis=1)
    grad_silu = jnp.transpose(silu_back, (1, 0, 2)).reshape(cond_rows, width)
    cond_grad = jax.vjp(jax.nn.silu, cond_wide)[1](grad_silu)[0]
    last_final = depth_scatter(last_sum)
    edge_one, edge_two = 3 * width // experts, 4 * width // experts
    qkv_weight_grad = last_final[:, :edge_one]
    out_weight_grad = last_final[:, edge_one:edge_two]
    router_weight_grad = last_final[:, edge_two : edge_two + 1]

    middle_final = late_final[:, hidden:].astype(WIDE_TYPE)
    shared_up_grad = middle_final[:, : hidden // experts]
    shared_down_grad = jnp.transpose(
        middle_final[:, hidden // experts :].reshape(local, 4, width // experts), (1, 0, 2)
    ).reshape(4 * local, width // experts)
    expert_up_grad, expert_down_grad = expert_sums(early_final, late_final)
    return (
        block_out,
        patches_grad,
        cond_grad,
        ada_weight_grad,
        qkv_weight_grad,
        out_weight_grad,
        router_weight_grad,
        shared_up_grad,
        shared_down_grad,
        expert_up_grad[None],
        expert_down_grad[None],
    )


def solution(mesh):
    in_specs = (
        P(("dp", "expert", "stream"), None),
        P(("dp", "expert", "stream"), None),
        P(("dp", "expert", "stream")),
        P(("dp", "expert", "stream"), None),
        P("dp", None),
        P("dp", None),
        P("dp", None),
        P("dp", None),
        P("dp", None),
        P("dp", None),
        P(("expert", "stream"), "dp", None),
        P(("expert", "stream"), "dp", None),
        P(("dp", "expert", "stream"), None),
    )
    out_specs = (
        P(("dp", "expert", "stream"), None),
        P(("dp", "expert", "stream"), None),
        P(("dp", "expert", "stream"), None),
        P("dp", ("expert", "stream")),
        P("dp", ("expert", "stream")),
        P("dp", ("expert", "stream")),
        P("dp", ("expert", "stream")),
        P("dp", ("expert", "stream")),
        P("dp", ("expert", "stream")),
        P(("expert", "stream"), "dp", None),
        P(("expert", "stream"), "dp", None),
    )
    return jax.shard_map(
        on_device, mesh=mesh, in_specs=in_specs, out_specs=out_specs, check_vma=False
    )
```

```python
import functools
import math

import jax
import jax.numpy as jnp
from jax import lax
from jax.experimental import pallas as pl
from jax.experimental.pallas import tpu as pltpu
from jax.sharding import PartitionSpec as P

HEAD = 64
TOP = 2
CAP = 320
SPARE = 16


EPSILON = 1e-06
ROOT = math.sqrt(2.0 / math.pi)
CUBE = 0.044715 * ROOT
MEBI = 1 << 20
WIDE_TYPE = jnp.float32
NARROW_TYPE = jnp.bfloat16


def product_plain_operands(left_side, right_side):
    return jnp.dot(left_side, right_side, preferred_element_type=WIDE_TYPE)


def product_left_operand(left_side, right_side):
    return lax.dot_general(
        left_side, right_side, (((0,), (0,)), ((), ())), preferred_element_type=WIDE_TYPE
    )


def product_right_operand(left_side, right_side):
    return lax.dot_general(
        left_side, right_side, (((1,), (1,)), ((), ())), preferred_element_type=WIDE_TYPE
    )


def contract(left_side, right_side, left_dim, right_dim):
    return lax.dot_general(
        left_side, right_side, (((left_dim,), (right_dim,)), ((), ())), preferred_element_type=WIDE_TYPE
    )

def attend_rows(joined_ref, attended_ref, total_ref, head, rows, columns):
    lanes = slice(head * HEAD, (head + 1) * HEAD)
    queries = joined_ref[0, rows, lanes] * (1.0 / 8.0)
    keys = joined_ref[1, columns, lanes]
    values = joined_ref[2, columns, lanes]
    scores = contract(queries.astype(NARROW_TYPE), keys, 1, 1)
    summit = jnp.max(scores, axis=1, keepdims=True)
    weights = jnp.exp(scores - summit)
    row_total = jnp.sum(weights, axis=1, keepdims=True)
    probabilities = (weights * (1.0 / row_total)).astype(NARROW_TYPE)
    attended_ref[rows, lanes] = contract(probabilities, values, 1, 0).astype(NARROW_TYPE)
    total_ref[rows, lanes] = jnp.broadcast_to(summit + jnp.log(row_total), (scores.shape[0], HEAD))

def attend_kernel(long_ref, joined_ref, attended_ref, total_ref):
    length = joined_ref.shape[1]
    quarter = length // 4
    for whole in (True, False):
        @pl.when((long_ref[0] == 1) == whole)
        def _():
            block = 2 * quarter if whole else quarter
            for head in range(2):
                for start in range(0, length, block):
                    rows = slice(start, start + block)
                    attend_rows(joined_ref, attended_ref, total_ref, head, rows, slice(None) if whole else rows)

def attend(long_pack, joined):
    three, length, width = joined.shape
    return pl.pallas_call(
        attend_kernel,
        grid=(width // 128,),
        in_specs=[pl.BlockSpec(memory_space=pltpu.SMEM), pl.BlockSpec((3, length, 128), lambda pair: (0, 0, pair))],
        out_specs=[pl.BlockSpec((length, 128), lambda pair: (0, pair))] * 2,
        out_shape=[jax.ShapeDtypeStruct((length, width), NARROW_TYPE), jax.ShapeDtypeStruct((length, width), WIDE_TYPE)],
        compiler_params=pltpu.CompilerParams(vmem_limit_bytes=61 * MEBI),
        name="attend",
    )(long_pack, joined)

def attend_back_rows(joined_ref, total_ref, grad_ref, out_ref, keys_acc, values_acc, head, rows, columns):
    lanes = slice(head * HEAD, (head + 1) * HEAD)
    queries = joined_ref[0, rows, lanes]
    scaled = (queries * (1.0 / 8.0)).astype(NARROW_TYPE)
    keys = joined_ref[1, columns, lanes]
    values = joined_ref[2, columns, lanes]
    grads = grad_ref[rows, lanes]
    scores = contract(scaled, keys, 1, 1)
    probabilities = jnp.exp(scores - total_ref[rows, head * HEAD : head * HEAD + 1])
    grad_probs = contract(grads, values, 1, 1)
    product = probabilities * grad_probs
    centre = jnp.sum(product, axis=1, keepdims=True)
    grad_scores = (product - probabilities * centre).astype(NARROW_TYPE)
    out_ref[0, rows, lanes] = (contract(grad_scores, keys, 1, 0) * (1.0 / 8.0)).astype(NARROW_TYPE)
    keys_acc[lanes, columns] += contract(scaled.T, grad_scores, 1, 0)
    values_acc[lanes, columns] += contract(grads.T, probabilities.astype(NARROW_TYPE), 1, 0)

def attend_back_kernel(long_ref, joined_ref, total_ref, grad_ref, *refs):
    out_ref, keys_acc, values_acc = refs[-3:]
    length = joined_ref.shape[1]
    quarter = length // 4
    keys_acc[...] = jnp.zeros_like(keys_acc)
    values_acc[...] = jnp.zeros_like(values_acc)
    for whole in (True, False):
        @pl.when((long_ref[0] == 1) == whole)
        def _():
            block = 2 * quarter if whole else quarter
            for head in range(2):
                for start in range(0, length, block):
                    rows = slice(start, start + block)
                    attend_back_rows(joined_ref, total_ref, grad_ref, out_ref, keys_acc, values_acc, head, rows, slice(None) if whole else rows)
    out_ref[1] = keys_acc[...].T.astype(NARROW_TYPE)
    out_ref[2] = values_acc[...].T.astype(NARROW_TYPE)

def attend_back(long_pack, joined, total, grad, after):
    three, length, width = joined.shape
    wide = pl.BlockSpec((3, length, 128), lambda pair: (0, 0, pair))
    flat = pl.BlockSpec((length, 128), lambda pair: (0, pair))
    return pl.pallas_call(
        attend_back_kernel,
        grid=(width // 128,),
        in_specs=[pl.BlockSpec(memory_space=pltpu.SMEM), wide, flat, flat]
        + [pl.BlockSpec(memory_space=pl.ANY)] * len(after),
        out_specs=wide,
        out_shape=jax.ShapeDtypeStruct((3, length, width), NARROW_TYPE),
        scratch_shapes=[pltpu.VMEM((128, length), WIDE_TYPE)] * 2,
        compiler_params=pltpu.CompilerParams(vmem_limit_bytes=61 * MEBI),
        name="attend_back",
    )(long_pack, joined, total, grad, *after)


def gelu_pair(values):
    square = values * values
    half = 0.5 * jnp.tanh(values * (CUBE * square + ROOT)) + 0.5
    result = values * half
    slope = half + result * (1.0 - half) * (6.0 * CUBE * square + 2.0 * ROOT)
    return result, slope


def expert_block(rows, grads, up, down):
    hidden, slope = gelu_pair(contract(rows, up, 1, 0))
    grad_pre = slope * contract(grads, down, 1, 1)
    return hidden.astype(NARROW_TYPE), grad_pre.astype(NARROW_TYPE)


def slot_rows_of(ref):
    parts = [ref[part, :CAP] for part in range(ref.shape[0])]
    return jnp.concatenate(parts, axis=0)


def slot_gates_of(ref):
    columns = []
    for part in range(ref.shape[0]):
        terms = ref[part, CAP:, :].astype(WIDE_TYPE)
        gates = terms[0:1] + terms[1:2] + terms[2:3]
        columns.append(jnp.broadcast_to(gates, (128, gates.shape[1])).T[:CAP, 0:1])
    return jnp.concatenate(columns, axis=0)


def routed_kernel(
    rows_ref, grad_ref, weight_ref, out_ref, left_ref, right_ref, dots_ref, hidden_ref, grad_pre_ref
):
    width = rows_ref.shape[2]
    count = weight_ref.shape[1] // (2 * width)
    rows = slot_rows_of(rows_ref)
    gates = slot_gates_of(rows_ref)
    cotangent = slot_rows_of(grad_ref).astype(WIDE_TYPE)
    grads = (gates * cotangent).astype(NARROW_TYPE)
    out = jnp.zeros(rows.shape, WIDE_TYPE)
    back = jnp.zeros(rows.shape, WIDE_TYPE)
    for block in range(count):
        units = slice(block * width, (block + 1) * width)
        up = weight_ref[:, units]
        down = weight_ref[:, (count + block) * width : (count + block + 1) * width]
        hidden, grad_pre = expert_block(rows, grads, up, down)
        hidden_ref[:, units] = hidden
        grad_pre_ref[:, units] = grad_pre
        out += contract(hidden, down, 1, 0)
        back += contract(grad_pre, up, 1, 1)
    out = out.astype(NARROW_TYPE).astype(WIDE_TYPE)
    out_ref[...] = (gates * out).astype(NARROW_TYPE)
    left_ref[...] = back[:, : width // 2].astype(NARROW_TYPE)
    right_ref[...] = back[:, width // 2 :].astype(NARROW_TYPE)
    dots_ref[...] = jnp.sum(out * cotangent, axis=1, keepdims=True)


def routed_expert(rows, grads, weights, after, parts=2):
    sources, _, width = rows.shape
    count, block = sources * CAP, parts * CAP
    hidden = weights.shape[1] // 2
    narrow = jax.ShapeDtypeStruct((count, width), NARROW_TYPE)
    side = jax.ShapeDtypeStruct((count, width // 2), NARROW_TYPE)
    units = jax.ShapeDtypeStruct((count, hidden), NARROW_TYPE)
    slots = pl.BlockSpec((parts,) + rows.shape[1:], lambda step: (step, 0, 0))
    return stepped(
        routed_kernel,
        sources // parts,
        (rows, grads, weights),
        [slots, slots, whole_block(weights)],
        [row_block(block, width)]
        + [row_block(block, width // 2)] * 2
        + [row_block(block, 1)]
        + [row_block(block, hidden)] * 2,
        [narrow, side, side, jax.ShapeDtypeStruct((count, 1), WIDE_TYPE), units, units],
        after,
        "routed_expert",
    )


def sums_kernel(
    steps, rows_ref, grad_ref, hidden_ref, grad_pre_ref, *refs
):
    sums_ref, totals = refs[-2:]
    step = pl.program_id(0)
    width = rows_ref.shape[2]
    count = totals.shape[0] // 2

    @pl.when(step == 0)
    def _():
        totals[...] = jnp.zeros_like(totals)

    @pl.when(step < steps)
    def _():
        turned = slot_rows_of(rows_ref).T
        cotangent = slot_rows_of(grad_ref).astype(WIDE_TYPE)
        grads = (slot_gates_of(rows_ref) * cotangent).astype(NARROW_TYPE)
        for block in range(count):
            units = slice(block * width, (block + 1) * width)
            totals[block] += contract(turned, grad_pre_ref[:, units], 1, 0)
            totals[count + block] += contract(hidden_ref[:, units], grads, 0, 0)

    @pl.when(jnp.logical_and(step >= steps, step < steps + 2 * count))
    def _():
        sums_ref[...] = totals[jnp.clip(step - steps, 0, 2 * count - 1)].astype(NARROW_TYPE)

    if len(refs) == 3:

        @pl.when(step == steps + 2 * count)
        def _():
            sums_ref[...] = refs[0][...]


def routed_sums(rows, grads, hidden, grad_pre, side, after, extra=(), parts=4):
    sources, _, width = rows.shape
    half = hidden.shape[1] // 2
    count = half // width
    steps = sources // parts
    slots = pl.BlockSpec(
        (parts,) + rows.shape[1:], lambda step: (jnp.minimum(step, steps - 1), 0, 0)
    )
    units = pl.BlockSpec((parts * CAP, half), lambda step: (jnp.minimum(step, steps - 1), side))
    square = (width, width)
    return stepped(
        functools.partial(sums_kernel, steps),
        steps + 2 * count + len(extra),
        (rows, grads, hidden, grad_pre, *extra),
        [slots, slots, units, units] + [whole_block(block) for block in extra],
        pl.BlockSpec(square, lambda step: (0, jnp.maximum(step - steps, 0))),
        jax.ShapeDtypeStruct((width, 2 * half + len(extra) * width), NARROW_TYPE),
        after,
        "routed_sums",
        scratch_shapes=[pltpu.VMEM((2 * count,) + square, WIDE_TYPE)],
    )


def part_of_step(core, place):
    chip = lax.rem(place, 4)
    owner = jnp.where(place < 4, core, 1 - core)
    return 4 * (chip // 2) + 2 * owner + lax.rem(chip, 2)


def shared_kernel(
    local, steps, core_ref, rows_ref, grad_ref, up_ref, down_ref, out_ref, back_ref, kept_ref, sent_ref, totals
):
    step = pl.program_id(0)
    width = rows_ref.shape[1]
    count = totals.shape[0] // 2

    @pl.when(step == 0)
    def _():
        totals[...] = jnp.zeros_like(totals)

    @pl.when(step < steps)
    def _():
        rows, grads = rows_ref[...], grad_ref[...]
        turned = grads.T
        out = jnp.zeros(rows.shape, WIDE_TYPE)
        back = jnp.zeros(rows.shape, WIDE_TYPE)
        for block in range(count):
            units = slice(block * width, (block + 1) * width)
            up, down = up_ref[:, units], down_ref[:, units]
            hidden, grad_pre = expert_block(rows, grads, up, down)
            out += contract(hidden, down, 1, 0)
            back += contract(grad_pre, up, 1, 1)
            totals[block] += contract(grad_pre, rows, 0, 0)
            totals[count + block] += contract(turned, hidden, 1, 0)
        out_ref[...] = out
        back_ref[...] = back

    units = count * width // 8
    features = width // 8
    part = part_of_step(core_ref[0], jnp.maximum(step - steps, 0))

    def write(part_ref):
        for piece in range(units // local):
            number = part * (units // local) + piece
            start = pl.multiple_of((number // count) * local, 8)
            part_ref[0, piece * local : (piece + 1) * local] = totals[
                lax.rem(number, count), pl.ds(start, local)
            ].astype(NARROW_TYPE)
        for block in range(count):
            start = units + block * features
            part_ref[0, start : start + features] = totals[
                count + block, pl.ds(pl.multiple_of(part * features, 8), features)
            ].astype(NARROW_TYPE)

    @pl.when(jnp.logical_and(step >= steps, step < steps + 4))
    def _():
        write(kept_ref)

    @pl.when(step >= steps + 4)
    def _():
        write(sent_ref)


def part_specs(steps, rows, width):
    return [
        pl.BlockSpec((1, rows, width), lambda step, *_: (jnp.clip(step - steps, 0, 3), 0, 0)),
        pl.BlockSpec((1, rows, width), lambda step, *_: (jnp.clip(step - steps - 4, 0, 3), 0, 0)),
    ]


def own_core():
    return ((lax.axis_index(PLANE) // 2) % 2).reshape(1).astype(jnp.int32)


def shared_expert(rows, grads, weights, local, after, row_block=512):
    total_rows, width = rows.shape
    steps = total_rows // row_block
    count = 4
    row_spec = pl.BlockSpec((row_block, width), lambda step, core: (jnp.minimum(step, steps - 1), 0))

    def held(place):
        return pl.BlockSpec(
            (width, count * width), lambda step, core: (0, place), pipeline_mode=pl.Buffered(1)
        )

    def kernel(*refs):
        shared_kernel(local, steps, *refs[:5], *refs[5 + len(after) :])

    wide = jax.ShapeDtypeStruct((total_rows, width), WIDE_TYPE)
    return pl.pallas_call(
        kernel,
        grid_spec=pltpu.PrefetchScalarGridSpec(
            num_scalar_prefetch=1,
            grid=(steps + 8,),
            in_specs=[row_spec, row_spec, held(0), held(1)] + [ANYWHERE] * len(after),
            out_specs=[row_spec, row_spec] + part_specs(steps, width, width),
            scratch_shapes=[pltpu.VMEM((2 * count, width, width), WIDE_TYPE)],
        ),
        out_shape=[wide, wide] + [jax.ShapeDtypeStruct((4, width, width), NARROW_TYPE)] * 2,
        compiler_params=pltpu.CompilerParams(vmem_limit_bytes=61 * MEBI),
        name="shared_expert",
    )(own_core(), rows, grads, weights, weights, *after)


PLANE = ("expert", "stream")
CORE, SIDES = 2, (4, 1, 5)


def flip(value, mask):
    count = lax.axis_size(PLANE)
    return lax.ppermute(value, PLANE, [(index, index ^ mask) for index in range(count)])


def together(*values):
    return lax.optimization_barrier(values)


ANYWHERE = pl.BlockSpec(memory_space=pl.ANY)


def whole_block(operand):
    rank = len(operand.shape)
    return pl.BlockSpec(operand.shape, lambda *_: (0,) * rank, pipeline_mode=pl.Buffered(1))


def row_block(rows, columns):
    return pl.BlockSpec((rows, columns), lambda step, *_: (step, 0))


def column_block(operand, columns, place):
    return pl.BlockSpec(
        (operand.shape[0], columns), lambda step, *_: (0, place), pipeline_mode=pl.Buffered(1)
    )


def stepped(kernel, steps, operands, in_specs, out_specs, out_shape, after, name, **extra):
    given = len(operands)

    def body(*refs):
        kernel(*refs[:given], *refs[given + len(after) :])

    return pl.pallas_call(
        body,
        grid=(steps,),
        in_specs=list(in_specs) + [ANYWHERE] * len(after),
        out_specs=out_specs,
        out_shape=out_shape,
        compiler_params=pltpu.CompilerParams(vmem_limit_bytes=61 * MEBI),
        name=name,
        **extra,
    )(*operands, *after)


def depth_stack(piece):
    parts = jnp.broadcast_to(piece[None], (lax.axis_size("dp"),) + piece.shape)
    return lax.all_to_all(parts, "dp", split_axis=0, concat_axis=0, tiled=True)


def stack_kernel(*refs):
    for place, ref in enumerate(refs[:-1]):
        refs[-1][place] = ref[...]


def place_kernel(order_ref, near_ref, far_ref, out_ref):
    for place in range(4):
        chip = order_ref[place]
        first = 4 * (chip // 2) + lax.rem(chip, 2)
        out_ref[0, first + 2 * order_ref[4]] = near_ref[place, 0]
        out_ref[0, first + 2 * (1 - order_ref[4])] = far_ref[place, 0]


def side_gather(stacked):
    return [stacked] + [flip(stacked, mask) for mask in SIDES]


def near_slices(sides, after=()):
    depth, rows, columns = sides[0].shape
    slice_shape = (1, rows, columns)
    return stepped(
        stack_kernel,
        depth,
        sides,
        [pl.BlockSpec(slice_shape, lambda part: (part, 0, 0))] * 4,
        pl.BlockSpec((4,) + slice_shape, lambda part: (0, part, 0, 0)),
        jax.ShapeDtypeStruct((4, depth, rows, columns), sides[0].dtype),
        after,
        "stack_sides",
    )


def plane_gather(near):
    depth, rows, columns = near.shape[1:]
    slice_shape = (1, rows, columns)
    me = lax.axis_index(PLANE)
    chip = 2 * (me // 4) + me % 2
    far = flip(near, CORE)
    order = jnp.stack([chip, chip ^ 2, chip ^ 1, chip ^ 3, (me // 2) % 2]).astype(jnp.int32)
    source = pl.BlockSpec((4,) + slice_shape, lambda part, order: (0, part, 0, 0))
    placed = pl.pallas_call(
        place_kernel,
        grid_spec=pltpu.PrefetchScalarGridSpec(
            num_scalar_prefetch=1,
            grid=(depth,),
            in_specs=[source] * 2,
            out_specs=pl.BlockSpec((1, 8, rows, columns), lambda part, order: (part, 0, 0, 0)),
        ),
        out_shape=jax.ShapeDtypeStruct((depth, 8, rows, columns), near.dtype),
        compiler_params=pltpu.CompilerParams(vmem_limit_bytes=61 * MEBI),
        name="place_slices",
    )(order, near, far)
    return placed.reshape(depth * 8 * rows, columns)


def pair_kernel(place_ref, kept_ref, other_ref, *refs):
    own_ref, *side_refs = refs[-4:]
    place = place_ref[0]
    own_ref[...] = kept_ref[place].astype(WIDE_TYPE) + other_ref[place].astype(WIDE_TYPE)
    for side_ref, other in zip(side_refs, (2, 1, 3)):
        chip = place ^ other
        total = kept_ref[chip].astype(WIDE_TYPE) + other_ref[chip].astype(WIDE_TYPE)
        side_ref[...] = total.astype(NARROW_TYPE)


def finish_kernel(own_ref, *refs):
    total = own_ref[...]
    for ref in refs[:3]:
        total += ref[...].astype(WIDE_TYPE)
    refs[-1][...] = total.T.astype(NARROW_TYPE)


def pair_sum(kept, other, after=(), columns=256):
    me = lax.axis_index(PLANE)
    place = (2 * (me // 4) + me % 2).reshape(1).astype(jnp.int32)
    rows, width = kept.shape[1:]
    stack = pl.BlockSpec((4, rows, columns), lambda step, place: (0, 0, step))
    flat = pl.BlockSpec((rows, columns), lambda step, *_: (0, step))
    narrow = jax.ShapeDtypeStruct((rows, width), NARROW_TYPE)
    return pl.pallas_call(
        pair_kernel,
        grid_spec=pltpu.PrefetchScalarGridSpec(
            num_scalar_prefetch=1,
            grid=(width // columns,),
            in_specs=[stack, stack] + [ANYWHERE] * len(after),
            out_specs=[flat] * 4,
        ),
        out_shape=[jax.ShapeDtypeStruct((rows, width), WIDE_TYPE)] + [narrow] * 3,
        compiler_params=pltpu.CompilerParams(vmem_limit_bytes=61 * MEBI),
        name="pair_sum",
    )(place, kept, other, *after)


def side_flips(sides):
    return [flip(side, mask) for side, mask in zip(sides, SIDES)]


def side_sum(own, *sides, after=(), columns=256):
    rows, width = own.shape
    flat = pl.BlockSpec((rows, columns), lambda step, *_: (0, step))
    return pl.pallas_call(
        finish_kernel,
        grid=(width // columns,),
        in_specs=[flat] * 4 + [ANYWHERE] * len(after),
        out_specs=pl.BlockSpec((columns, rows), lambda step: (step, 0)),
        out_shape=jax.ShapeDtypeStruct((width, rows), NARROW_TYPE),
        compiler_params=pltpu.CompilerParams(vmem_limit_bytes=61 * MEBI),
        name="side_sum",
    )(own, *sides, *after)


def last_kernel(
    core_ref, joined_ref, first_ref, grad_ref, attended_ref, logits_ref, second_ref, kept_ref, sent_ref, totals, router
):
    step = pl.program_id(0)
    width = first_ref.shape[1]

    @pl.when(step < 3)
    def _():
        start = pl.multiple_of(step * width, 8)
        totals[pl.ds(start, width)] = contract(joined_ref[0], first_ref[...], 0, 0)

    @pl.when(step == 3)
    def _():
        totals[3 * width :] = contract(grad_ref[...], attended_ref[...], 0, 0)
        router[...] = contract(logits_ref[...], second_ref[...], 0, 0)

    part = part_of_step(core_ref[0], jnp.maximum(step - 4, 0))

    def write(part_ref):
        place = 0
        for start, rows in ((0, 3 * width // 8), (3 * width, width // 8)):
            first = pl.multiple_of(start + part * rows, 8)
            part_ref[0, place : place + rows] = totals[pl.ds(first, rows)].astype(NARROW_TYPE)
            place += rows
        number = lax.broadcasted_iota(jnp.int32, router.shape, 0)
        column = jnp.sum(jnp.where(number == part, router[...], 0.0), axis=0, keepdims=True)
        tail = part_ref.shape[1] - place
        row = lax.broadcasted_iota(jnp.int32, (tail, width), 0)
        part_ref[0, place:] = jnp.where(row == 0, column, 0.0).astype(NARROW_TYPE)

    @pl.when(jnp.logical_and(step >= 4, step < 8))
    def _():
        write(kept_ref)

    @pl.when(step >= 8)
    def _():
        write(sent_ref)


def last_gradients(grad_joined, first_in, grad_attention, attended, grad_logits, second_in, after):
    count, width = first_in.shape
    rows = width // 2 + 16
    flat = pl.BlockSpec((count, width), lambda step, core: (0, 0))
    thin = pl.BlockSpec((count, grad_logits.shape[1]), lambda step, core: (0, 0))
    def kernel(*refs):
        last_kernel(*refs[:7], *refs[7 + len(after) :])

    return pl.pallas_call(
        kernel,
        grid_spec=pltpu.PrefetchScalarGridSpec(
            num_scalar_prefetch=1,
            grid=(12,),
            in_specs=[
                pl.BlockSpec((1, count, width), lambda step, core: (jnp.minimum(step, 2), 0, 0)),
                flat,
                flat,
                flat,
                thin,
                flat,
            ]
            + [ANYWHERE] * len(after),
            out_specs=part_specs(4, rows, width),
            scratch_shapes=[
                pltpu.VMEM((4 * width, width), WIDE_TYPE),
                pltpu.VMEM((grad_logits.shape[1], width), WIDE_TYPE),
            ],
        ),
        out_shape=[jax.ShapeDtypeStruct((4, rows, width), NARROW_TYPE)] * 2,
        compiler_params=pltpu.CompilerParams(vmem_limit_bytes=61 * MEBI),
        name="last_gradients",
    )(own_core(), grad_joined, first_in, grad_attention, attended, grad_logits, second_in, *after)


def depth_shift(value, shift):
    depth = lax.axis_size("dp")
    return lax.ppermute(value, "dp", [(index, (index + shift) % depth) for index in range(depth)])


def depth_scatter(parts):
    depth = lax.axis_size("dp")
    blocks = parts.reshape(depth, parts.shape[0] // depth, parts.shape[1])
    if depth > 8:
        blocks = lax.all_to_all(blocks, "dp", split_axis=0, concat_axis=0, tiled=True)
        return jnp.sum(blocks.astype(WIDE_TYPE), axis=0)
    me = lax.axis_index("dp")
    total = lax.dynamic_index_in_dim(blocks, me, 0, keepdims=False).astype(WIDE_TYPE)
    for shift in range(1, depth):
        part = lax.dynamic_index_in_dim(blocks, (me + shift) % depth, 0, keepdims=False)
        total = total + depth_shift(part, shift).astype(WIDE_TYPE)
    return total


def first_payload_kernel(place_ref, qkv_ref, out_ref, router_ref, cond_ref, payload_ref):
    del place_ref
    depth, rows, columns = payload_ref.shape
    slots = cond_ref.shape[0]
    local = cond_ref.shape[1] // depth
    qkv_end = qkv_ref.shape[1]
    out_end = qkv_end + out_ref.shape[1]
    router_end = out_end + 128
    silu = cond_ref[...].astype(WIDE_TYPE)
    silu = silu * jax.nn.sigmoid(silu)
    router = jnp.concatenate(
        [router_ref[...].astype(WIDE_TYPE), jnp.zeros((rows, 128 - router_ref.shape[1]), WIDE_TYPE)],
        axis=1,
    ).astype(NARROW_TYPE)
    payload_ref[...] = jnp.zeros_like(payload_ref)
    for part in range(depth):
        payload_ref[part, :, :qkv_end] = qkv_ref[...]
        payload_ref[part, :, qkv_end:out_end] = out_ref[...]
        payload_ref[part, :, out_end:router_end] = router
        tail = jnp.concatenate(
            [silu[:, part * local : (part + 1) * local], jnp.zeros((slots, columns - router_end - local), WIDE_TYPE)],
            axis=1,
        )
        tail = jnp.concatenate([tail, jnp.zeros((rows - slots, columns - router_end), WIDE_TYPE)], axis=0)
        payload_ref[part, :, router_end:] = tail.astype(NARROW_TYPE)


def first_payload(qkv, out, router, cond, depth, rows):
    place = lax.axis_index(PLANE).reshape(1).astype(jnp.int32)
    local = cond.shape[1] // depth
    columns = qkv.shape[1] + out.shape[1] + 128 + local + -local % 128

    def slice_of(operand):
        return pl.BlockSpec((rows, operand.shape[1]), lambda step, place: (place[0], 0))

    return pl.pallas_call(
        first_payload_kernel,
        grid_spec=pltpu.PrefetchScalarGridSpec(
            num_scalar_prefetch=1,
            grid=(1,),
            in_specs=[slice_of(qkv), slice_of(out), slice_of(router), whole_block(cond)],
            out_specs=pl.BlockSpec((depth, rows, columns), lambda step, place: (0, 0, 0)),
        ),
        out_shape=jax.ShapeDtypeStruct((depth, rows, columns), NARROW_TYPE),
        compiler_params=pltpu.CompilerParams(vmem_limit_bytes=61 * MEBI),
        name="first_payload",
    )(place, qkv, out, router, cond)


def rest_payload_kernel(local, place_ref, up_ref, down_ref, *refs):
    del place_ref
    payload_ref = refs[-1]
    hidden = up_ref.shape[1]
    width = down_ref.shape[2]
    depth = hidden // (4 * local)
    for block in range(4):
        for part in range(depth):
            target = (block * depth + part) * local
            source = (part * 4 + block) * local
            payload_ref[:, target : target + local] = up_ref[:, source : source + local]
        start = hidden + block * width
        payload_ref[:, start : start + width] = down_ref[block]


def rest_payload(up, down, rows, after):
    place = lax.axis_index(PLANE).reshape(1).astype(jnp.int32)
    local, hidden = up.shape
    width = down.shape[1]
    shape = (rows, hidden + 4 * width)
    return pl.pallas_call(
        functools.partial(rest_payload_kernel, local),
        grid_spec=pltpu.PrefetchScalarGridSpec(
            num_scalar_prefetch=1,
            grid=(1,),
            in_specs=[
                pl.BlockSpec((rows, hidden), lambda step, place: (place[0], 0)),
                pl.BlockSpec((4, rows, width), lambda step, place: (0, place[0], 0)),
            ]
            + [ANYWHERE] * len(after),
            out_specs=pl.BlockSpec(shape, lambda step, place: (0, 0)),
        ),
        out_shape=jax.ShapeDtypeStruct(shape, NARROW_TYPE),
        compiler_params=pltpu.CompilerParams(vmem_limit_bytes=61 * MEBI),
        name="rest_payload",
    )(place, up, down.reshape(4, local, width), *after)


def expert_payload_kernel(up_ref, down_ref, *refs):
    payload_ref = refs[-1]
    local, hidden = up_ref.shape
    width = down_ref.shape[1]
    depth = hidden // (4 * local)
    for block in range(4):
        for part in range(depth):
            target = (block * depth + part) * local
            source = (part * 4 + block) * local
            payload_ref[:, target : target + local] = up_ref[:, source : source + local]
        start = hidden + block * width
        payload_ref[:, start : start + width] = down_ref[block * local : (block + 1) * local, :]


def expert_payload(up, down, after):
    local, hidden = up.shape
    whole = pl.BlockSpec(memory_space=pltpu.VMEM)
    return pl.pallas_call(
        expert_payload_kernel,
        in_specs=[whole, whole] + [ANYWHERE] * len(after),
        out_specs=whole,
        out_shape=jax.ShapeDtypeStruct((local, hidden + 4 * down.shape[1]), up.dtype),
        compiler_params=pltpu.CompilerParams(vmem_limit_bytes=61 * MEBI),
        name="expert_payload",
    )(up, down, *after)


def normalize_rows(values):
    centre = values - jnp.mean(values, axis=-1, keepdims=True)
    spread = jnp.mean(centre * centre, axis=-1, keepdims=True)
    reciprocal = lax.rsqrt(spread + EPSILON)
    return centre * reciprocal, reciprocal


def normalize_rows_back(gradient, normed, reciprocal):
    mean = jnp.mean(gradient, axis=-1, keepdims=True)
    along = jnp.mean(gradient * normed, axis=-1, keepdims=True)
    return reciprocal * (gradient - mean - normed * along)


def pick_slots(first, count, places_ref):
    patches = places_ref.shape[1]
    slot = first + lax.broadcasted_iota(jnp.int32, (count, patches), 0)
    return jnp.logical_or(slot == places_ref[0:1, :], slot == places_ref[1:2, :])


def one(mask):
    return jnp.where(mask, 1.0, 0.0).astype(NARROW_TYPE)


def mixture_kernel(grad_ref, mods_ref, places_ref, silu_ref, shared_ref, out_ref):
    step = pl.program_id(0)
    quarter = grad_ref.shape[0] // 4

    @pl.when(step == 0)
    def _():
        for part in range(4):
            rows = slice(part * quarter, (part + 1) * quarter)
            gradient = grad_ref[rows, :].astype(WIDE_TYPE) * mods_ref[part, 5:6, :]
            shared_ref[rows, :] = gradient.astype(NARROW_TYPE)

    parts = out_ref.shape[0]
    taken = one(pick_slots(step * parts * CAP, parts * CAP, places_ref))
    rows = contract(taken, shared_ref[...], 1, 0).astype(NARROW_TYPE)
    for part in range(parts):
        out_ref[part, :CAP] = rows[part * CAP : (part + 1) * CAP]
        out_ref[part, CAP:] = jnp.zeros((SPARE, out_ref.shape[2]), NARROW_TYPE)
        out_ref[part, CAP:, : silu_ref.shape[1]] = silu_ref[...]


def slot_block(width):
    return pl.BlockSpec((2, CAP + SPARE, width), lambda step: (step, 0, 0))


def spread_mixture(out_grad, mods, places, silu, after):
    count, width = out_grad.shape
    return stepped(
        mixture_kernel,
        4,
        (out_grad, mods, places, silu),
        [whole_block(operand) for operand in (out_grad, mods, places, silu)],
        [pl.BlockSpec((count, width), lambda step: (0, 0)), slot_block(width)],
        [
            jax.ShapeDtypeStruct((count, width), NARROW_TYPE),
            jax.ShapeDtypeStruct((8, CAP + SPARE, width), NARROW_TYPE),
        ],
        after,
        "spread_mixture",
    )


def first_kernel(patch_ref, mods_ref, weight_ref, first_ref, joined_ref):
    normed, _ = normalize_rows(patch_ref[...].astype(WIDE_TYPE))
    first = (normed * (1.0 + mods_ref[0, 1:2, :]) + mods_ref[0, 0:1, :]).astype(NARROW_TYPE)
    first_ref[...] = first
    width = first.shape[1]
    for part in range(3):
        columns = slice(part * width, (part + 1) * width)
        joined_ref[part] = contract(first, weight_ref[:, columns], 1, 0).astype(NARROW_TYPE)


def mods_block(mods, quarters=1):
    return pl.BlockSpec((quarters,) + mods.shape[1:], lambda step, *_: (step, 0, 0))


def first_half(patches, mods, weights, after):
    count, width = patches.shape
    quarter = count // 4
    rows = row_block(quarter, width)
    return stepped(
        first_kernel,
        4,
        (patches, mods, weights),
        [rows, mods_block(mods), column_block(weights, 3 * width, 0)],
        [rows, pl.BlockSpec((3, quarter, width), lambda step: (0, step, 0))],
        [
            jax.ShapeDtypeStruct((count, width), NARROW_TYPE),
            jax.ShapeDtypeStruct((3, count, width), NARROW_TYPE),
        ],
        after,
        "first_half",
    )


def second_kernel(
    attended_ref, patch_ref, mods_ref, routes_ref, out_ref, router_ref, attention_ref, middle_ref, second_ref, gates_ref, gate_rows_ref
):
    attention = contract(attended_ref[...], out_ref[...], 1, 0)
    attention_ref[...] = attention
    middle = patch_ref[...].astype(WIDE_TYPE) + mods_ref[0, 2:3, :] * attention
    middle_ref[...] = middle
    normed, _ = normalize_rows(middle)
    second = (normed * (1.0 + mods_ref[0, 4:5, :]) + mods_ref[0, 3:4, :]).astype(NARROW_TYPE)
    second_ref[...] = second
    logits = contract(second, router_ref[...], 1, 0)
    lane = lax.broadcasted_iota(jnp.int32, logits.shape, 1)
    picked = [
        jnp.sum(jnp.where(lane == routes_ref[:, k : k + 1], logits, 0.0), axis=1, keepdims=True)
        for k in range(TOP)
    ]
    summit = jnp.maximum(picked[0], picked[1])
    weights = [jnp.exp(value - summit) for value in picked]
    total = weights[0] + weights[1]
    gates = [weight / total for weight in weights]
    gates_ref[...] = jnp.concatenate(gates, axis=1)
    wide = jnp.where(lane == 0, gates[0], jnp.where(lane == 1, gates[1], 0.0))
    gate_rows_ref[...] = wide.T[0:TOP, :]


def second_half(attended, patches, mods, routes, weights, after):
    count, width = patches.shape
    quarter = count // 4
    rows = row_block(quarter, width)
    pair = row_block(quarter, TOP)
    wide = jax.ShapeDtypeStruct((count, width), WIDE_TYPE)
    return stepped(
        second_kernel,
        4,
        (attended, patches, mods, routes, weights, weights),
        [
            rows,
            rows,
            mods_block(mods),
            pair,
            column_block(weights, width, 3),
            column_block(weights, 128, 4 * width // 128),
        ],
        [rows, rows, rows, pair, pl.BlockSpec((TOP, quarter), lambda step: (0, step))],
        [
            wide,
            wide,
            jax.ShapeDtypeStruct((count, width), NARROW_TYPE),
            jax.ShapeDtypeStruct((count, TOP), WIDE_TYPE),
            jax.ShapeDtypeStruct((TOP, count), WIDE_TYPE),
        ],
        after,
        "second_half",
    )


def spread_kernel(second_ref, places_ref, gates_ref, rows_ref):
    parts = rows_ref.shape[0]
    first = pl.program_id(0) * parts * CAP
    slots = pick_slots(first, parts * CAP, places_ref)
    rows = contract(one(slots), second_ref[...], 1, 0).astype(NARROW_TYPE)
    slot = first + lax.broadcasted_iota(jnp.int32, slots.shape, 0)
    total = jnp.where(slot == places_ref[0:1, :], gates_ref[0:1, :], 0.0)
    total += jnp.where(slot == places_ref[1:2, :], gates_ref[1:2, :], 0.0)
    column = jnp.sum(total, axis=1, keepdims=True)
    gates = jnp.broadcast_to(column, (parts * CAP, 128)).T[0:SPARE, :]
    row = lax.broadcasted_iota(jnp.int32, gates.shape, 0)
    terms = jnp.zeros(gates.shape, WIDE_TYPE)
    for number in range(3):
        term = gates.astype(NARROW_TYPE).astype(WIDE_TYPE)
        terms = jnp.where(row == number, term, terms)
        gates = gates - term
    for part in range(parts):
        own = slice(part * CAP, (part + 1) * CAP)
        rows_ref[part, :CAP] = rows[own]
        rows_ref[part, CAP:] = jnp.zeros((SPARE, rows_ref.shape[2]), NARROW_TYPE)
        rows_ref[part, CAP:, :CAP] = terms[:, own].astype(NARROW_TYPE)


def spread_second(second_in, places, gates, after):
    width = second_in.shape[1]
    operands = (second_in, places, gates)
    return stepped(
        spread_kernel,
        4,
        operands,
        [whole_block(operand) for operand in operands],
        slot_block(width),
        jax.ShapeDtypeStruct((8, CAP + SPARE, width), NARROW_TYPE),
        after,
        "spread_second",
    )


def middle_kernel(
    left_ref,
    right_ref,
    dots_ref,
    columns_ref,
    routes_ref,
    gates_ref,
    shared_ref,
    middle_ref,
    attention_ref,
    mods_ref,
    grad_ref,
    out_ref,
    router_ref,
    grad_middle_ref,
    grad_attention_ref,
    grad_attended_ref,
    grad_logits_ref,
    sums_ref,
):
    count, width = middle_ref.shape
    quarters = mods_ref.shape[0]
    quarter = count // quarters
    slot = lax.broadcasted_iota(jnp.int32, (count, left_ref.shape[0]), 1)
    takes = [slot == columns_ref[:, k : k + 1] for k in range(TOP)]
    taken = one(jnp.logical_or(*takes))
    collected = [contract(taken, ref[...], 1, 0) for ref in (left_ref, right_ref)]
    collected = jnp.concatenate(collected, axis=1)
    gates = [gates_ref[:, k : k + 1] for k in range(TOP)]
    grad_gate = [
        jnp.sum(jnp.where(take, dots_ref[...], 0.0), axis=1, keepdims=True) for take in takes
    ]
    centre = gates[0] * grad_gate[0] + gates[1] * grad_gate[1]
    lane = lax.broadcasted_iota(jnp.int32, grad_logits_ref.shape, 1)
    grad_logits = jnp.zeros(grad_logits_ref.shape, WIDE_TYPE)
    for k in range(TOP):
        picked = gates[k] * (grad_gate[k] - centre)
        grad_logits += jnp.where(lane == routes_ref[:, k : k + 1], picked, 0.0)
    grad_logits = grad_logits.astype(NARROW_TYPE)
    grad_logits_ref[...] = grad_logits
    grad_second = shared_ref[...] + contract(grad_logits, router_ref[...], 1, 1) + collected
    normed, reciprocal = normalize_rows(middle_ref[...])
    grad_middle = grad_ref[...].astype(WIDE_TYPE) + normalize_rows_back(
        grad_second * (1.0 + mods_rows(mods_ref, 4, quarter)), normed, reciprocal
    )
    grad_middle_ref[...] = grad_middle
    grad_attention = (grad_middle * mods_rows(mods_ref, 2, quarter)).astype(NARROW_TYPE)
    grad_attention_ref[...] = grad_attention
    grad_attended_ref[...] = contract(grad_attention, out_ref[...], 1, 1).astype(NARROW_TYPE)
    totals = [grad_middle * attention_ref[...], grad_second, grad_second * normed]
    totals = [quarter_sums(total, quarters) for total in totals]
    for part in range(quarters):
        sums_ref[part] = jnp.concatenate([total[part] for total in totals], axis=0)


def sums_block(count, width, quarters=1):
    return pl.BlockSpec((quarters, count, width), lambda step: (step, 0, 0))


def mods_rows(mods_ref, piece, quarter):
    parts = [
        jnp.broadcast_to(mods_ref[part, piece : piece + 1, :], (quarter, mods_ref.shape[2]))
        for part in range(mods_ref.shape[0])
    ]
    return jnp.concatenate(parts, axis=0)


def quarter_sums(values, quarters):
    rows = values.shape[0] // quarters
    return [
        jnp.sum(values[part * rows : (part + 1) * rows], axis=0, keepdims=True)
        for part in range(quarters)
    ]


def middle_back(
    left, right, dots, columns, routes, gates, grad_shared, middle, attention, mods, out_grad, weights, after
):
    count, width = middle.shape
    half = count // 2
    rows, pair, lanes = row_block(half, width), row_block(half, TOP), row_block(half, 128)
    narrow = jax.ShapeDtypeStruct((count, width), NARROW_TYPE)
    return stepped(
        middle_kernel,
        2,
        (left, right, dots, columns, routes, gates, grad_shared, middle, attention, mods, out_grad, weights, weights),
        [whole_block(left), whole_block(right), whole_block(dots), pair, pair, pair, rows, rows, rows]
        + [mods_block(mods, 2), rows]
        + [column_block(weights, width, 3), column_block(weights, 128, 4 * width // 128)],
        [rows, rows, rows, lanes, sums_block(3, width, 2)],
        [
            jax.ShapeDtypeStruct((count, width), WIDE_TYPE),
            narrow,
            narrow,
            jax.ShapeDtypeStruct((count, 128), NARROW_TYPE),
            jax.ShapeDtypeStruct((4, 3, width), WIDE_TYPE),
        ],
        after,
        "middle_back",
    )


def output_kernel(
    result_ref, columns_ref, shared_ref, middle_ref, mods_ref, grad_ref, out_ref, sums_ref
):
    count = middle_ref.shape[0]
    quarters = mods_ref.shape[0]
    slot = lax.broadcasted_iota(jnp.int32, (count, result_ref.shape[0]), 1)
    takes = [slot == columns_ref[:, k : k + 1] for k in range(TOP)]
    mixture = shared_ref[...] + contract(one(jnp.logical_or(*takes)), result_ref[...], 1, 0)
    gate = mods_rows(mods_ref, 5, count // quarters)
    out_ref[...] = (middle_ref[...] + gate * mixture).astype(NARROW_TYPE)
    totals = quarter_sums(grad_ref[...].astype(WIDE_TYPE) * mixture, quarters)
    for part in range(quarters):
        sums_ref[part] = totals[part]


def block_output(result, columns, shared, middle, mods, out_grad, after):
    count, width = middle.shape
    half = count // 2
    rows, pair = row_block(half, width), row_block(half, TOP)
    return stepped(
        output_kernel,
        2,
        (result, columns, shared, middle, mods, out_grad),
        [whole_block(result), pair, rows, rows, mods_block(mods, 2), rows],
        [rows, sums_block(1, width, 2)],
        [
            jax.ShapeDtypeStruct((count, width), NARROW_TYPE),
            jax.ShapeDtypeStruct((4, 1, width), WIDE_TYPE),
        ],
        after,
        "block_output",
    )


def start_kernel(joined_ref, weight_ref, patch_ref, mods_ref, middle_ref, out_ref, sums_ref):
    width = patch_ref.shape[1]
    grad_first = jnp.zeros(patch_ref.shape, WIDE_TYPE)
    for part in range(3):
        columns = slice(part * width, (part + 1) * width)
        grad_first += contract(joined_ref[part], weight_ref[:, columns], 1, 1)
    normed, reciprocal = normalize_rows(patch_ref[...].astype(WIDE_TYPE))
    out_ref[...] = middle_ref[...] + normalize_rows_back(
        grad_first * (1.0 + mods_ref[0, 1:2, :]), normed, reciprocal
    )
    sums_ref[0] = jnp.concatenate(
        [
            jnp.sum(grad_first, axis=0, keepdims=True),
            jnp.sum(grad_first * normed, axis=0, keepdims=True),
        ],
        axis=0,
    )


def start_back(grad_joined, weights, patches, mods, grad_middle, after):
    count, width = patches.shape
    quarter = count // 4
    rows = row_block(quarter, width)
    return stepped(
        start_kernel,
        4,
        (grad_joined, weights, patches, mods, grad_middle),
        [
            pl.BlockSpec((3, quarter, width), lambda step: (0, step, 0)),
            column_block(weights, 3 * width, 0),
            rows,
            mods_block(mods),
            rows,
        ],
        [rows, sums_block(2, width)],
        [
            jax.ShapeDtypeStruct((count, width), WIDE_TYPE),
            jax.ShapeDtypeStruct((4, 2, width), WIDE_TYPE),
        ],
        after,
        "start_back",
    )


def expert_sums_kernel(early_ref, late_ref, up_ref, down_ref):
    local, hidden = up_ref.shape
    width = down_ref.shape[1]
    depth = hidden // (4 * local)
    for block in range(4):
        ref = (early_ref, late_ref)[block // 2]
        for part in range(depth):
            source = (block % 2) * width + part * local
            target = (part * 4 + block) * local
            up_ref[:, target : target + local] = ref[:, source : source + local].astype(WIDE_TYPE)
        source = (2 + block % 2) * width
        down_ref[block * local : (block + 1) * local] = ref[:, source : source + width].astype(WIDE_TYPE)


def expert_sums(early, late):
    local, hidden = early.shape
    width = hidden // 4
    return stepped(
        expert_sums_kernel,
        1,
        (early, late),
        [whole_block(early), column_block(late, hidden, 0)],
        [
            pl.BlockSpec((local, hidden), lambda step: (0, 0)),
            pl.BlockSpec((4 * local, width), lambda step: (0, 0)),
        ],
        [
            jax.ShapeDtypeStruct((local, hidden), WIDE_TYPE),
            jax.ShapeDtypeStruct((4 * local, width), WIDE_TYPE),
        ],
        (),
        "expert_sums",
    )


def slot_of_routes(route_rows, expert_count, capacity):
    pair_ids = route_rows.reshape(-1)
    onehot = (pair_ids[:, None] == jnp.arange(expert_count, dtype=jnp.int32)[None, :]).astype(
        jnp.int32
    )
    rank_values = jnp.cumsum(onehot, axis=0) - onehot
    slot_index = jnp.sum(rank_values * onehot, axis=1)
    return (pair_ids * capacity + slot_index).reshape(route_rows.shape)


def on_device(
    patches,
    cond,
    long_pack,
    routes,
    ada_weight,
    qkv_weight,
    out_weight,
    router_weight,
    shared_up,
    shared_down,
    expert_up,
    expert_down,
    out_grad,
):
    width = patches.shape[1]
    hidden = shared_up.shape[1]
    depth = lax.axis_size("dp")
    experts = lax.axis_size(PLANE)
    capacity = CAP
    slots = experts * capacity
    local = qkv_weight.shape[0]
    slice_rows = local // experts
    plane_index = lax.axis_index(PLANE)

    def blocked(columns):
        split = columns.reshape(columns.shape[0], depth, 4, local)
        return jnp.transpose(split, (0, 2, 1, 3)).reshape(columns.shape)

    def own(rows):
        return lax.dynamic_slice_in_dim(rows, plane_index * slice_rows, slice_rows, 0)

    places = slot_of_routes(routes, experts, capacity)
    columns, places = places, places.T
    expert_piece = expert_payload(expert_up[0], expert_down[0], ())

    cond_wide = cond.astype(WIDE_TYPE)
    cond_rows = cond.shape[0]
    if slice_rows % 8 == 0:
        first_stack = lax.all_to_all(
            first_payload(qkv_weight, out_weight, router_weight, cond, depth, slice_rows),
            "dp",
            split_axis=0,
            concat_axis=0,
            tiled=True,
        )
        first_end = 4 * width + 128
        silu_parts = first_stack[:, :cond_rows, first_end : first_end + local]
        rest_piece = rest_payload(
            shared_up, shared_down, slice_rows, (first_stack, places, expert_piece)
        )
    else:
        silu_cond = jax.nn.silu(cond_wide).astype(NARROW_TYPE)
        silu_parts = lax.all_to_all(
            jnp.transpose(silu_cond.reshape(cond_rows, depth, local), (1, 0, 2)),
            "dp",
            split_axis=0,
            concat_axis=0,
            tiled=True,
        )
        router_slice = jnp.pad(own(router_weight), ((0, 0), (0, 128 - router_weight.shape[1])))
        first_stack = depth_stack(
            jnp.concatenate([own(qkv_weight), own(out_weight), router_slice], axis=1)
        )
        down_slice = lax.dynamic_slice_in_dim(
            shared_down.reshape(4, local, width), plane_index * slice_rows, slice_rows, 1
        )
        rest_piece = jnp.concatenate(
            [
                blocked(own(shared_up)),
                jnp.transpose(down_slice, (1, 0, 2)).reshape(slice_rows, 4 * width),
            ],
            axis=1,
        )
    silu_parts = silu_parts.reshape(depth * cond_rows, local)
    partial = product_plain_operands(silu_parts, ada_weight)
    first_sides = side_gather(first_stack)
    rest_stack = lax.all_gather(rest_piece, "dp", axis=0)
    modulation = jnp.sum(
        lax.all_to_all(
            partial.reshape(depth, cond_rows, 6 * width), "dp", split_axis=0, concat_axis=0, tiled=True
        ),
        axis=0,
    )
    blocks = modulation.reshape(4, 6, width)
    is_long = long_pack[0] == 1
    mods = jnp.where(is_long, blocks[:1], blocks)

    def exchange(rows):
        return lax.all_to_all(rows, PLANE, split_axis=0, concat_axis=0, tiled=True)

    grad_shared, mixture_slots = spread_mixture(
        out_grad, mods, places, silu_parts.reshape(SPARE, -1), ()
    )
    first_near = near_slices(first_sides, (mixture_slots,))
    expert_piece, first_near = together(expert_piece, first_near)
    expert_weights = lax.all_gather(expert_piece, "dp", axis=0, tiled=True)
    mixture_slots = exchange(mixture_slots)
    first_full = plane_gather(first_near)
    rest_sides = side_gather(rest_stack)
    first_in, joined = first_half(patches, mods, first_full, ())
    attended, log_total = attend(long_pack, joined)
    attended, mixture_slots = together(attended, mixture_slots)
    attention, middle, second_in, gate_values, gate_rows = second_half(
        attended, patches, mods, routes, first_full, ()
    )
    slot_rows = spread_second(second_in, places, gate_rows, ())
    rest = plane_gather(near_slices(rest_sides, (attended, slot_rows)))
    slots_there = exchange(slot_rows)

    shared, grad_from_shared, kept, sent = shared_expert(
        second_in, grad_shared, rest, local, (slot_rows,)
    )
    sent, slots_there = together(sent, slots_there)
    routed = (slots_there, mixture_slots)
    silu_all = mixture_slots[:, capacity:, : silu_parts.size // SPARE]
    silu_all = silu_all.reshape(experts, depth, cond_rows, local)
    silu_all = jnp.transpose(silu_all, (1, 0, 2, 3)).reshape(depth * experts * cond_rows, local)
    middle_own, *middle_sides = pair_sum(kept, flip(sent, CORE))
    middle_sides = side_flips(middle_sides)
    result_rows, *grad_rows, gate_dots, units, grad_units = routed_expert(
        *routed, expert_weights, (middle_own,)
    )
    *middle_sides, left, right = together(*middle_sides, *grad_rows)
    left_back = exchange(left.reshape(experts, capacity, width // 2))
    left_back, gate_dots = together(left_back, gate_dots)
    left_back = left_back.reshape(slots, width // 2)
    gate_dots_back = exchange(gate_dots.reshape(experts, 1, capacity)).reshape(1, slots)
    early_sums = routed_sums(*routed, units, grad_units, 0, ())
    early_sums, left_back = together(early_sums, left_back)
    early_final = lax.psum_scatter(early_sums, "dp", scatter_dimension=0, tiled=True)
    middle_sum = side_sum(middle_own, *middle_sides, after=(early_sums,))
    right, middle_sum = together(right, middle_sum)
    right_back = exchange(right.reshape(experts, capacity, width // 2)).reshape(slots, width // 2)
    late_sums = routed_sums(*routed, units, grad_units, 1, (early_sums,), (middle_sum,))

    grad_middle, grad_attention, grad_attended, grad_logits, middle_sums = middle_back(
        left_back,
        right_back,
        gate_dots_back,
        columns,
        routes,
        gate_values,
        grad_from_shared,
        middle,
        attention,
        mods,
        out_grad,
        first_full,
        (silu_all,),
    )
    late_sums, grad_attended = together(late_sums, grad_attended)
    late_final = lax.psum_scatter(late_sums, "dp", scatter_dimension=0, tiled=True)
    result_back = exchange(result_rows.reshape(experts, capacity, width)).reshape(slots, width)
    grad_joined = attend_back(long_pack, joined, log_total, grad_attended, ())
    last_parts = last_gradients(
        grad_joined, first_in, grad_attention, attended, grad_logits, second_in, (result_back,)
    )
    block_out, output_sums = block_output(
        result_back,
        columns,
        shared,
        middle,
        mods,
        out_grad,
        (*last_parts, early_final),
    )
    last_pair = pair_sum(last_parts[0], flip(last_parts[1], CORE), (output_sums,))
    patches_grad, start_sums = start_back(
        grad_joined, first_full, patches, mods, grad_middle, tuple(last_pair)
    )
    last_sides = side_flips(last_pair[1:])
    grad_chosen = jnp.concatenate([start_sums, middle_sums, output_sums], axis=1)
    grad_chosen = grad_chosen.reshape(1, 4, 6 * width)
    long_total = jnp.sum(grad_chosen, axis=1, keepdims=True)
    first_slot = (jnp.arange(4, dtype=jnp.int32) == 0)[None, :, None]
    grad_blocks = jnp.where(is_long, jnp.where(first_slot, long_total, 0.0), grad_chosen)
    grad_modulation = grad_blocks.reshape(cond_rows, 6 * width).astype(NARROW_TYPE)
    everyone = ("dp",) + PLANE
    columns = 6 * width // experts
    grad_columns = jnp.transpose(grad_modulation.reshape(cond_rows, experts, columns), (1, 0, 2))
    *last_sides, grad_columns = together(*last_sides, grad_columns)
    last_sum = side_sum(last_pair[0], *last_sides)
    grad_columns = jnp.broadcast_to(grad_columns[None], (depth, experts, cond_rows, columns))
    grad_columns = lax.all_to_all(
        grad_columns.reshape(depth * experts, cond_rows, columns),
        everyone,
        split_axis=0,
        concat_axis=0,
        tiled=True,
    ).reshape(depth * experts * cond_rows, columns)
    grad_columns, last_sum = together(grad_columns, last_sum)
    ada_weight_grad = product_left_operand(silu_all, grad_columns)
    own_ada = lax.dynamic_slice_in_dim(ada_weight, plane_index * columns, columns, 1)
    silu_back, late_final = together(product_right_operand(grad_columns, own_ada), late_final)
    silu_back = lax.all_to_all(
        silu_back.reshape(depth * experts, cond_rows, local),
        everyone,
        split_axis=0,
        concat_axis=0,
        tiled=True,
    )
    silu_back = jnp.sum(silu_back.reshape(depth, experts, cond_rows, local), axis=1)
    grad_silu = jnp.transpose(silu_back, (1, 0, 2)).reshape(cond_rows, width)
    cond_grad = jax.vjp(jax.nn.silu, cond_wide)[1](grad_silu)[0]
    last_final = depth_scatter(last_sum)
    edge_one, edge_two = 3 * width // experts, 4 * width // experts
    qkv_weight_grad = last_final[:, :edge_one]
    out_weight_grad = last_final[:, edge_one:edge_two]
    router_weight_grad = last_final[:, edge_two : edge_two + 1]

    middle_final = late_final[:, hidden:].astype(WIDE_TYPE)
    shared_up_grad = middle_final[:, : hidden // experts]
    shared_down_grad = jnp.transpose(
        middle_final[:, hidden // experts :].reshape(local, 4, width // experts), (1, 0, 2)
    ).reshape(4 * local, width // experts)
    expert_up_grad, expert_down_grad = expert_sums(early_final, late_final)
    return (
        block_out,
        patches_grad,
        cond_grad,
        ada_weight_grad,
        qkv_weight_grad,
        out_weight_grad,
        router_weight_grad,
        shared_up_grad,
        shared_down_grad,
        expert_up_grad[None],
        expert_down_grad[None],
    )


def solution(mesh):
    in_specs = (
        P(("dp", "expert", "stream"), None),
        P(("dp", "expert", "stream"), None),
        P(("dp", "expert", "stream")),
        P(("dp", "expert", "stream"), None),
        P("dp", None),
        P("dp", None),
        P("dp", None),
        P("dp", None),
        P("dp", None),
        P("dp", None),
        P(("expert", "stream"), "dp", None),
        P(("expert", "stream"), "dp", None),
        P(("dp", "expert", "stream"), None),
    )
    out_specs = (
        P(("dp", "expert", "stream"), None),
        P(("dp", "expert", "stream"), None),
        P(("dp", "expert", "stream"), None),
        P("dp", ("expert", "stream")),
        P("dp", ("expert", "stream")),
        P("dp", ("expert", "stream")),
        P("dp", ("expert", "stream")),
        P("dp", ("expert", "stream")),
        P("dp", ("expert", "stream")),
        P(("expert", "stream"), "dp", None),
        P(("expert", "stream"), "dp", None),
    )
    return jax.shard_map(
        on_device, mesh=mesh, in_specs=in_specs, out_specs=out_specs, check_vma=False
    )
```

```python
import functools
import math

import jax
import jax.numpy as jnp
from jax import lax
from jax.experimental import pallas as pl
from jax.experimental.pallas import tpu as pltpu
from jax.sharding import PartitionSpec as P

HEAD = 64
TOP = 2
CAP = 320
SPARE = 16


EPSILON = 1e-06
ROOT = math.sqrt(2.0 / math.pi)
CUBE = 0.044715 * ROOT
MEBI = 1 << 20
WIDE_TYPE = jnp.float32
NARROW_TYPE = jnp.bfloat16


def product_plain_operands(left_side, right_side):
    return jnp.dot(left_side, right_side, preferred_element_type=WIDE_TYPE)


def product_left_operand(left_side, right_side):
    return lax.dot_general(
        left_side, right_side, (((0,), (0,)), ((), ())), preferred_element_type=WIDE_TYPE
    )


def product_right_operand(left_side, right_side):
    return lax.dot_general(
        left_side, right_side, (((1,), (1,)), ((), ())), preferred_element_type=WIDE_TYPE
    )


def contract(left_side, right_side, left_dim, right_dim):
    return lax.dot_general(
        left_side, right_side, (((left_dim,), (right_dim,)), ((), ())), preferred_element_type=WIDE_TYPE
    )

def attend_rows(joined_ref, attended_ref, total_ref, head, rows, columns):
    lanes = slice(head * HEAD, (head + 1) * HEAD)
    queries = joined_ref[0, rows, lanes] * (1.0 / 8.0)
    keys = joined_ref[1, columns, lanes]
    values = joined_ref[2, columns, lanes]
    scores = contract(queries.astype(NARROW_TYPE), keys, 1, 1)
    summit = jnp.max(scores, axis=1, keepdims=True)
    weights = jnp.exp(scores - summit)
    row_total = jnp.sum(weights, axis=1, keepdims=True)
    probabilities = (weights * (1.0 / row_total)).astype(NARROW_TYPE)
    attended_ref[rows, lanes] = contract(probabilities, values, 1, 0).astype(NARROW_TYPE)
    total_ref[rows, lanes] = jnp.broadcast_to(summit + jnp.log(row_total), (scores.shape[0], HEAD))

def attend_kernel(long_ref, joined_ref, attended_ref, total_ref):
    length = joined_ref.shape[1]
    quarter = length // 4
    for whole in (True, False):
        @pl.when((long_ref[0] == 1) == whole)
        def _():
            block = 2 * quarter if whole else quarter
            for head in range(2):
                for start in range(0, length, block):
                    rows = slice(start, start + block)
                    attend_rows(joined_ref, attended_ref, total_ref, head, rows, slice(None) if whole else rows)

def attend(long_pack, joined):
    three, length, width = joined.shape
    return pl.pallas_call(
        attend_kernel,
        grid=(width // 128,),
        in_specs=[pl.BlockSpec(memory_space=pltpu.SMEM), pl.BlockSpec((3, length, 128), lambda pair: (0, 0, pair))],
        out_specs=[pl.BlockSpec((length, 128), lambda pair: (0, pair))] * 2,
        out_shape=[jax.ShapeDtypeStruct((length, width), NARROW_TYPE), jax.ShapeDtypeStruct((length, width), WIDE_TYPE)],
        compiler_params=pltpu.CompilerParams(vmem_limit_bytes=61 * MEBI),
        name="attend",
    )(long_pack, joined)

def attend_back_rows(joined_ref, total_ref, grad_ref, out_ref, keys_acc, values_acc, head, rows, columns):
    lanes = slice(head * HEAD, (head + 1) * HEAD)
    queries = joined_ref[0, rows, lanes]
    scaled = (queries * (1.0 / 8.0)).astype(NARROW_TYPE)
    keys = joined_ref[1, columns, lanes]
    values = joined_ref[2, columns, lanes]
    grads = grad_ref[rows, lanes]
    scores = contract(scaled, keys, 1, 1)
    probabilities = jnp.exp(scores - total_ref[rows, head * HEAD : head * HEAD + 1])
    grad_probs = contract(grads, values, 1, 1)
    product = probabilities * grad_probs
    centre = jnp.sum(product, axis=1, keepdims=True)
    grad_scores = (product - probabilities * centre).astype(NARROW_TYPE)
    out_ref[0, rows, lanes] = (contract(grad_scores, keys, 1, 0) * (1.0 / 8.0)).astype(NARROW_TYPE)
    keys_acc[lanes, columns] += contract(scaled.T, grad_scores, 1, 0)
    values_acc[lanes, columns] += contract(grads.T, probabilities.astype(NARROW_TYPE), 1, 0)

def attend_back_kernel(long_ref, joined_ref, total_ref, grad_ref, *refs):
    out_ref, keys_acc, values_acc = refs[-3:]
    length = joined_ref.shape[1]
    quarter = length // 4
    keys_acc[...] = jnp.zeros_like(keys_acc)
    values_acc[...] = jnp.zeros_like(values_acc)
    for whole in (True, False):
        @pl.when((long_ref[0] == 1) == whole)
        def _():
            block = 2 * quarter if whole else quarter
            for head in range(2):
                for start in range(0, length, block):
                    rows = slice(start, start + block)
                    attend_back_rows(joined_ref, total_ref, grad_ref, out_ref, keys_acc, values_acc, head, rows, slice(None) if whole else rows)
    out_ref[1] = keys_acc[...].T.astype(NARROW_TYPE)
    out_ref[2] = values_acc[...].T.astype(NARROW_TYPE)

def attend_back(long_pack, joined, total, grad, after):
    three, length, width = joined.shape
    wide = pl.BlockSpec((3, length, 128), lambda pair: (0, 0, pair))
    flat = pl.BlockSpec((length, 128), lambda pair: (0, pair))
    return pl.pallas_call(
        attend_back_kernel,
        grid=(width // 128,),
        in_specs=[pl.BlockSpec(memory_space=pltpu.SMEM), wide, flat, flat]
        + [pl.BlockSpec(memory_space=pl.ANY)] * len(after),
        out_specs=wide,
        out_shape=jax.ShapeDtypeStruct((3, length, width), NARROW_TYPE),
        scratch_shapes=[pltpu.VMEM((128, length), WIDE_TYPE)] * 2,
        compiler_params=pltpu.CompilerParams(vmem_limit_bytes=61 * MEBI),
        name="attend_back",
    )(long_pack, joined, total, grad, *after)


def gelu_pair(values):
    square = values * values
    half = 0.5 * jnp.tanh(values * (CUBE * square + ROOT)) + 0.5
    result = values * half
    slope = half + result * (1.0 - half) * (6.0 * CUBE * square + 2.0 * ROOT)
    return result, slope


def expert_block(rows, grads, up, down):
    hidden, slope = gelu_pair(contract(rows, up, 1, 0))
    grad_pre = slope * contract(grads, down, 1, 1)
    return hidden.astype(NARROW_TYPE), grad_pre.astype(NARROW_TYPE)


def slot_rows_of(ref):
    parts = [ref[part, :CAP] for part in range(ref.shape[0])]
    return jnp.concatenate(parts, axis=0)


def slot_gates_of(ref):
    columns = []
    for part in range(ref.shape[0]):
        terms = ref[part, CAP:, :].astype(WIDE_TYPE)
        gates = terms[0:1] + terms[1:2] + terms[2:3]
        columns.append(jnp.broadcast_to(gates, (128, gates.shape[1])).T[:CAP, 0:1])
    return jnp.concatenate(columns, axis=0)


def routed_kernel(
    rows_ref, grad_ref, weight_ref, out_ref, left_ref, right_ref, dots_ref, hidden_ref, grad_pre_ref
):
    width = rows_ref.shape[2]
    count = weight_ref.shape[1] // (2 * width)
    rows = slot_rows_of(rows_ref)
    gates = slot_gates_of(rows_ref)
    cotangent = slot_rows_of(grad_ref).astype(WIDE_TYPE)
    grads = (gates * cotangent).astype(NARROW_TYPE)
    out = jnp.zeros(rows.shape, WIDE_TYPE)
    back = jnp.zeros(rows.shape, WIDE_TYPE)
    for block in range(count):
        units = slice(block * width, (block + 1) * width)
        up = weight_ref[:, units]
        down = weight_ref[:, (count + block) * width : (count + block + 1) * width]
        hidden, grad_pre = expert_block(rows, grads, up, down)
        hidden_ref[:, units] = hidden
        grad_pre_ref[:, units] = grad_pre
        out += contract(hidden, down, 1, 0)
        back += contract(grad_pre, up, 1, 1)
    out = out.astype(NARROW_TYPE).astype(WIDE_TYPE)
    out_ref[...] = (gates * out).astype(NARROW_TYPE)
    left_ref[...] = back[:, : width // 2].astype(NARROW_TYPE)
    right_ref[...] = back[:, width // 2 :].astype(NARROW_TYPE)
    dots_ref[...] = jnp.sum(out * cotangent, axis=1, keepdims=True)


def routed_expert(rows, grads, weights, after, parts=2):
    sources, _, width = rows.shape
    count, block = sources * CAP, parts * CAP
    hidden = weights.shape[1] // 2
    narrow = jax.ShapeDtypeStruct((count, width), NARROW_TYPE)
    side = jax.ShapeDtypeStruct((count, width // 2), NARROW_TYPE)
    units = jax.ShapeDtypeStruct((count, hidden), NARROW_TYPE)
    slots = pl.BlockSpec((parts,) + rows.shape[1:], lambda step: (step, 0, 0))
    return stepped(
        routed_kernel,
        sources // parts,
        (rows, grads, weights),
        [slots, slots, whole_block(weights)],
        [row_block(block, width)]
        + [row_block(block, width // 2)] * 2
        + [row_block(block, 1)]
        + [row_block(block, hidden)] * 2,
        [narrow, side, side, jax.ShapeDtypeStruct((count, 1), WIDE_TYPE), units, units],
        after,
        "routed_expert",
    )


def sums_kernel(
    steps, rows_ref, grad_ref, hidden_ref, grad_pre_ref, *refs
):
    sums_ref, totals = refs[-2:]
    step = pl.program_id(0)
    width = rows_ref.shape[2]
    count = totals.shape[0] // 2

    @pl.when(step == 0)
    def _():
        totals[...] = jnp.zeros_like(totals)

    @pl.when(step < steps)
    def _():
        turned = slot_rows_of(rows_ref).T
        cotangent = slot_rows_of(grad_ref).astype(WIDE_TYPE)
        grads = (slot_gates_of(rows_ref) * cotangent).astype(NARROW_TYPE)
        for block in range(count):
            units = slice(block * width, (block + 1) * width)
            totals[block] += contract(turned, grad_pre_ref[:, units], 1, 0)
            totals[count + block] += contract(hidden_ref[:, units], grads, 0, 0)

    @pl.when(jnp.logical_and(step >= steps, step < steps + 2 * count))
    def _():
        sums_ref[...] = totals[jnp.clip(step - steps, 0, 2 * count - 1)].astype(NARROW_TYPE)

    if len(refs) == 3:

        @pl.when(step == steps + 2 * count)
        def _():
            sums_ref[...] = refs[0][...]


def routed_sums(rows, grads, hidden, grad_pre, side, after, extra=(), parts=4):
    sources, _, width = rows.shape
    half = hidden.shape[1] // 2
    count = half // width
    steps = sources // parts
    slots = pl.BlockSpec(
        (parts,) + rows.shape[1:], lambda step: (jnp.minimum(step, steps - 1), 0, 0)
    )
    units = pl.BlockSpec((parts * CAP, half), lambda step: (jnp.minimum(step, steps - 1), side))
    square = (width, width)
    return stepped(
        functools.partial(sums_kernel, steps),
        steps + 2 * count + len(extra),
        (rows, grads, hidden, grad_pre, *extra),
        [slots, slots, units, units] + [whole_block(block) for block in extra],
        pl.BlockSpec(square, lambda step: (0, jnp.maximum(step - steps, 0))),
        jax.ShapeDtypeStruct((width, 2 * half + len(extra) * width), NARROW_TYPE),
        after,
        "routed_sums",
        scratch_shapes=[pltpu.VMEM((2 * count,) + square, WIDE_TYPE)],
    )


def part_of_step(core, place):
    chip = lax.rem(place, 4)
    owner = jnp.where(place < 4, core, 1 - core)
    return 4 * (chip // 2) + 2 * owner + lax.rem(chip, 2)


def shared_kernel(
    local, steps, core_ref, rows_ref, grad_ref, up_ref, down_ref, out_ref, back_ref, kept_ref, sent_ref, totals
):
    step = pl.program_id(0)
    width = rows_ref.shape[1]
    count = totals.shape[0] // 2

    @pl.when(step == 0)
    def _():
        totals[...] = jnp.zeros_like(totals)

    @pl.when(step < steps)
    def _():
        rows, grads = rows_ref[...], grad_ref[...]
        turned = grads.T
        out = jnp.zeros(rows.shape, WIDE_TYPE)
        back = jnp.zeros(rows.shape, WIDE_TYPE)
        for block in range(count):
            units = slice(block * width, (block + 1) * width)
            up, down = up_ref[:, units], down_ref[:, units]
            hidden, grad_pre = expert_block(rows, grads, up, down)
            out += contract(hidden, down, 1, 0)
            back += contract(grad_pre, up, 1, 1)
            totals[block] += contract(grad_pre, rows, 0, 0)
            totals[count + block] += contract(turned, hidden, 1, 0)
        out_ref[...] = out
        back_ref[...] = back

    units = count * width // 8
    features = width // 8
    part = part_of_step(core_ref[0], jnp.maximum(step - steps, 0))

    def write(part_ref):
        for piece in range(units // local):
            number = part * (units // local) + piece
            start = pl.multiple_of((number // count) * local, 8)
            part_ref[0, piece * local : (piece + 1) * local] = totals[
                lax.rem(number, count), pl.ds(start, local)
            ].astype(NARROW_TYPE)
        for block in range(count):
            start = units + block * features
            part_ref[0, start : start + features] = totals[
                count + block, pl.ds(pl.multiple_of(part * features, 8), features)
            ].astype(NARROW_TYPE)

    @pl.when(jnp.logical_and(step >= steps, step < steps + 4))
    def _():
        write(kept_ref)

    @pl.when(step >= steps + 4)
    def _():
        write(sent_ref)


def part_specs(steps, rows, width):
    return [
        pl.BlockSpec((1, rows, width), lambda step, *_: (jnp.clip(step - steps, 0, 3), 0, 0)),
        pl.BlockSpec((1, rows, width), lambda step, *_: (jnp.clip(step - steps - 4, 0, 3), 0, 0)),
    ]


def own_core():
    return ((lax.axis_index(PLANE) // 2) % 2).reshape(1).astype(jnp.int32)


def shared_expert(rows, grads, weights, local, after, row_block=512):
    total_rows, width = rows.shape
    steps = total_rows // row_block
    count = 4
    row_spec = pl.BlockSpec((row_block, width), lambda step, core: (jnp.minimum(step, steps - 1), 0))

    def held(place):
        return pl.BlockSpec(
            (width, count * width), lambda step, core: (0, place), pipeline_mode=pl.Buffered(1)
        )

    def kernel(*refs):
        shared_kernel(local, steps, *refs[:5], *refs[5 + len(after) :])

    wide = jax.ShapeDtypeStruct((total_rows, width), WIDE_TYPE)
    return pl.pallas_call(
        kernel,
        grid_spec=pltpu.PrefetchScalarGridSpec(
            num_scalar_prefetch=1,
            grid=(steps + 8,),
            in_specs=[row_spec, row_spec, held(0), held(1)] + [ANYWHERE] * len(after),
            out_specs=[row_spec, row_spec] + part_specs(steps, width, width),
            scratch_shapes=[pltpu.VMEM((2 * count, width, width), WIDE_TYPE)],
        ),
        out_shape=[wide, wide] + [jax.ShapeDtypeStruct((4, width, width), NARROW_TYPE)] * 2,
        compiler_params=pltpu.CompilerParams(vmem_limit_bytes=61 * MEBI),
        name="shared_expert",
    )(own_core(), rows, grads, weights, weights, *after)


PLANE = ("expert", "stream")
CORE, SIDES = 2, (4, 1, 5)


def flip(value, mask):
    count = lax.axis_size(PLANE)
    return lax.ppermute(value, PLANE, [(index, index ^ mask) for index in range(count)])


def together(*values):
    return lax.optimization_barrier(values)


ANYWHERE = pl.BlockSpec(memory_space=pl.ANY)


def whole_block(operand):
    rank = len(operand.shape)
    return pl.BlockSpec(operand.shape, lambda *_: (0,) * rank, pipeline_mode=pl.Buffered(1))


def row_block(rows, columns):
    return pl.BlockSpec((rows, columns), lambda step, *_: (step, 0))


def column_block(operand, columns, place):
    return pl.BlockSpec(
        (operand.shape[0], columns), lambda step, *_: (0, place), pipeline_mode=pl.Buffered(1)
    )


def stepped(kernel, steps, operands, in_specs, out_specs, out_shape, after, name, **extra):
    given = len(operands)

    def body(*refs):
        kernel(*refs[:given], *refs[given + len(after) :])

    return pl.pallas_call(
        body,
        grid=(steps,),
        in_specs=list(in_specs) + [ANYWHERE] * len(after),
        out_specs=out_specs,
        out_shape=out_shape,
        compiler_params=pltpu.CompilerParams(vmem_limit_bytes=61 * MEBI),
        name=name,
        **extra,
    )(*operands, *after)


def depth_stack(piece):
    parts = jnp.broadcast_to(piece[None], (lax.axis_size("dp"),) + piece.shape)
    return lax.all_to_all(parts, "dp", split_axis=0, concat_axis=0, tiled=True)


def stack_kernel(*refs):
    for place, ref in enumerate(refs[:-1]):
        refs[-1][place] = ref[...]


def place_kernel(order_ref, near_ref, far_ref, out_ref):
    for place in range(4):
        chip = order_ref[place]
        first = 4 * (chip // 2) + lax.rem(chip, 2)
        out_ref[0, first + 2 * order_ref[4]] = near_ref[place, 0]
        out_ref[0, first + 2 * (1 - order_ref[4])] = far_ref[place, 0]


def side_gather(stacked):
    return [stacked] + [flip(stacked, mask) for mask in SIDES]


def near_slices(sides, after=()):
    depth, rows, columns = sides[0].shape
    slice_shape = (1, rows, columns)
    return stepped(
        stack_kernel,
        depth,
        sides,
        [pl.BlockSpec(slice_shape, lambda part: (part, 0, 0))] * 4,
        pl.BlockSpec((4,) + slice_shape, lambda part: (0, part, 0, 0)),
        jax.ShapeDtypeStruct((4, depth, rows, columns), sides[0].dtype),
        after,
        "stack_sides",
    )


def plane_gather(near):
    depth, rows, columns = near.shape[1:]
    slice_shape = (1, rows, columns)
    me = lax.axis_index(PLANE)
    chip = 2 * (me // 4) + me % 2
    far = flip(near, CORE)
    order = jnp.stack([chip, chip ^ 2, chip ^ 1, chip ^ 3, (me // 2) % 2]).astype(jnp.int32)
    source = pl.BlockSpec((4,) + slice_shape, lambda part, order: (0, part, 0, 0))
    placed = pl.pallas_call(
        place_kernel,
        grid_spec=pltpu.PrefetchScalarGridSpec(
            num_scalar_prefetch=1,
            grid=(depth,),
            in_specs=[source] * 2,
            out_specs=pl.BlockSpec((1, 8, rows, columns), lambda part, order: (part, 0, 0, 0)),
        ),
        out_shape=jax.ShapeDtypeStruct((depth, 8, rows, columns), near.dtype),
        compiler_params=pltpu.CompilerParams(vmem_limit_bytes=61 * MEBI),
        name="place_slices",
    )(order, near, far)
    return placed.reshape(depth * 8 * rows, columns)


def pair_kernel(place_ref, kept_ref, other_ref, *refs):
    own_ref, *side_refs = refs[-4:]
    place = place_ref[0]
    own_ref[...] = kept_ref[place].astype(WIDE_TYPE) + other_ref[place].astype(WIDE_TYPE)
    for side_ref, other in zip(side_refs, (2, 1, 3)):
        chip = place ^ other
        total = kept_ref[chip].astype(WIDE_TYPE) + other_ref[chip].astype(WIDE_TYPE)
        side_ref[...] = total.astype(NARROW_TYPE)


def finish_kernel(own_ref, *refs):
    total = own_ref[...]
    for ref in refs[:3]:
        total += ref[...].astype(WIDE_TYPE)
    refs[-1][...] = total.T.astype(NARROW_TYPE)


def pair_sum(kept, other, after=(), columns=256):
    me = lax.axis_index(PLANE)
    place = (2 * (me // 4) + me % 2).reshape(1).astype(jnp.int32)
    rows, width = kept.shape[1:]
    stack = pl.BlockSpec((4, rows, columns), lambda step, place: (0, 0, step))
    flat = pl.BlockSpec((rows, columns), lambda step, *_: (0, step))
    narrow = jax.ShapeDtypeStruct((rows, width), NARROW_TYPE)
    return pl.pallas_call(
        pair_kernel,
        grid_spec=pltpu.PrefetchScalarGridSpec(
            num_scalar_prefetch=1,
            grid=(width // columns,),
            in_specs=[stack, stack] + [ANYWHERE] * len(after),
            out_specs=[flat] * 4,
        ),
        out_shape=[jax.ShapeDtypeStruct((rows, width), WIDE_TYPE)] + [narrow] * 3,
        compiler_params=pltpu.CompilerParams(vmem_limit_bytes=61 * MEBI),
        name="pair_sum",
    )(place, kept, other, *after)


def side_flips(sides):
    return [flip(side, mask) for side, mask in zip(sides, SIDES)]


def side_sum(own, *sides, after=(), columns=256):
    rows, width = own.shape
    flat = pl.BlockSpec((rows, columns), lambda step, *_: (0, step))
    return pl.pallas_call(
        finish_kernel,
        grid=(width // columns,),
        in_specs=[flat] * 4 + [ANYWHERE] * len(after),
        out_specs=pl.BlockSpec((columns, rows), lambda step: (step, 0)),
        out_shape=jax.ShapeDtypeStruct((width, rows), NARROW_TYPE),
        compiler_params=pltpu.CompilerParams(vmem_limit_bytes=61 * MEBI),
        name="side_sum",
    )(own, *sides, *after)


def last_kernel(
    core_ref, joined_ref, first_ref, grad_ref, attended_ref, logits_ref, second_ref, kept_ref, sent_ref, totals, router
):
    step = pl.program_id(0)
    width = first_ref.shape[1]

    @pl.when(step < 3)
    def _():
        start = pl.multiple_of(step * width, 8)
        totals[pl.ds(start, width)] = contract(joined_ref[0], first_ref[...], 0, 0)

    @pl.when(step == 3)
    def _():
        totals[3 * width :] = contract(grad_ref[...], attended_ref[...], 0, 0)
        router[...] = contract(logits_ref[...], second_ref[...], 0, 0)

    part = part_of_step(core_ref[0], jnp.maximum(step - 4, 0))

    def write(part_ref):
        place = 0
        for start, rows in ((0, 3 * width // 8), (3 * width, width // 8)):
            first = pl.multiple_of(start + part * rows, 8)
            part_ref[0, place : place + rows] = totals[pl.ds(first, rows)].astype(NARROW_TYPE)
            place += rows
        number = lax.broadcasted_iota(jnp.int32, router.shape, 0)
        column = jnp.sum(jnp.where(number == part, router[...], 0.0), axis=0, keepdims=True)
        tail = part_ref.shape[1] - place
        row = lax.broadcasted_iota(jnp.int32, (tail, width), 0)
        part_ref[0, place:] = jnp.where(row == 0, column, 0.0).astype(NARROW_TYPE)

    @pl.when(jnp.logical_and(step >= 4, step < 8))
    def _():
        write(kept_ref)

    @pl.when(step >= 8)
    def _():
        write(sent_ref)


def last_gradients(grad_joined, first_in, grad_attention, attended, grad_logits, second_in, after):
    count, width = first_in.shape
    rows = width // 2 + 16
    flat = pl.BlockSpec((count, width), lambda step, core: (0, 0))
    thin = pl.BlockSpec((count, grad_logits.shape[1]), lambda step, core: (0, 0))
    def kernel(*refs):
        last_kernel(*refs[:7], *refs[7 + len(after) :])

    return pl.pallas_call(
        kernel,
        grid_spec=pltpu.PrefetchScalarGridSpec(
            num_scalar_prefetch=1,
            grid=(12,),
            in_specs=[
                pl.BlockSpec((1, count, width), lambda step, core: (jnp.minimum(step, 2), 0, 0)),
                flat,
                flat,
                flat,
                thin,
                flat,
            ]
            + [ANYWHERE] * len(after),
            out_specs=part_specs(4, rows, width),
            scratch_shapes=[
                pltpu.VMEM((4 * width, width), WIDE_TYPE),
                pltpu.VMEM((grad_logits.shape[1], width), WIDE_TYPE),
            ],
        ),
        out_shape=[jax.ShapeDtypeStruct((4, rows, width), NARROW_TYPE)] * 2,
        compiler_params=pltpu.CompilerParams(vmem_limit_bytes=61 * MEBI),
        name="last_gradients",
    )(own_core(), grad_joined, first_in, grad_attention, attended, grad_logits, second_in, *after)


def depth_shift(value, shift):
    depth = lax.axis_size("dp")
    return lax.ppermute(value, "dp", [(index, (index + shift) % depth) for index in range(depth)])


def depth_scatter(parts):
    depth = lax.axis_size("dp")
    blocks = parts.reshape(depth, parts.shape[0] // depth, parts.shape[1])
    if depth > 8:
        blocks = lax.all_to_all(blocks, "dp", split_axis=0, concat_axis=0, tiled=True)
        return jnp.sum(blocks.astype(WIDE_TYPE), axis=0)
    me = lax.axis_index("dp")
    total = lax.dynamic_index_in_dim(blocks, me, 0, keepdims=False).astype(WIDE_TYPE)
    for shift in range(1, depth):
        part = lax.dynamic_index_in_dim(blocks, (me + shift) % depth, 0, keepdims=False)
        total = total + depth_shift(part, shift).astype(WIDE_TYPE)
    return total


def first_payload_kernel(place_ref, qkv_ref, out_ref, router_ref, cond_ref, payload_ref):
    del place_ref
    depth, rows, columns = payload_ref.shape
    slots = cond_ref.shape[0]
    local = cond_ref.shape[1] // depth
    qkv_end = qkv_ref.shape[1]
    out_end = qkv_end + out_ref.shape[1]
    router_end = out_end + 128
    silu = cond_ref[...].astype(WIDE_TYPE)
    silu = silu * jax.nn.sigmoid(silu)
    router = jnp.concatenate(
        [router_ref[...].astype(WIDE_TYPE), jnp.zeros((rows, 128 - router_ref.shape[1]), WIDE_TYPE)],
        axis=1,
    ).astype(NARROW_TYPE)
    payload_ref[...] = jnp.zeros_like(payload_ref)
    for part in range(depth):
        payload_ref[part, :, :qkv_end] = qkv_ref[...]
        payload_ref[part, :, qkv_end:out_end] = out_ref[...]
        payload_ref[part, :, out_end:router_end] = router
        tail = jnp.concatenate(
            [silu[:, part * local : (part + 1) * local], jnp.zeros((slots, columns - router_end - local), WIDE_TYPE)],
            axis=1,
        )
        tail = jnp.concatenate([tail, jnp.zeros((rows - slots, columns - router_end), WIDE_TYPE)], axis=0)
        payload_ref[part, :, router_end:] = tail.astype(NARROW_TYPE)


def first_payload(qkv, out, router, cond, depth, rows):
    place = lax.axis_index(PLANE).reshape(1).astype(jnp.int32)
    local = cond.shape[1] // depth
    columns = qkv.shape[1] + out.shape[1] + 128 + local + -local % 128

    def slice_of(operand):
        return pl.BlockSpec((rows, operand.shape[1]), lambda step, place: (place[0], 0))

    return pl.pallas_call(
        first_payload_kernel,
        grid_spec=pltpu.PrefetchScalarGridSpec(
            num_scalar_prefetch=1,
            grid=(1,),
            in_specs=[slice_of(qkv), slice_of(out), slice_of(router), whole_block(cond)],
            out_specs=pl.BlockSpec((depth, rows, columns), lambda step, place: (0, 0, 0)),
        ),
        out_shape=jax.ShapeDtypeStruct((depth, rows, columns), NARROW_TYPE),
        compiler_params=pltpu.CompilerParams(vmem_limit_bytes=61 * MEBI),
        name="first_payload",
    )(place, qkv, out, router, cond)


def rest_payload_kernel(local, place_ref, up_ref, down_ref, *refs):
    del place_ref
    payload_ref = refs[-1]
    hidden = up_ref.shape[1]
    width = down_ref.shape[2]
    depth = hidden // (4 * local)
    for block in range(4):
        for part in range(depth):
            target = (block * depth + part) * local
            source = (part * 4 + block) * local
            payload_ref[:, target : target + local] = up_ref[:, source : source + local]
        start = hidden + block * width
        payload_ref[:, start : start + width] = down_ref[block]


def rest_payload(up, down, rows, after):
    place = lax.axis_index(PLANE).reshape(1).astype(jnp.int32)
    local, hidden = up.shape
    width = down.shape[1]
    shape = (rows, hidden + 4 * width)
    return pl.pallas_call(
        functools.partial(rest_payload_kernel, local),
        grid_spec=pltpu.PrefetchScalarGridSpec(
            num_scalar_prefetch=1,
            grid=(1,),
            in_specs=[
                pl.BlockSpec((rows, hidden), lambda step, place: (place[0], 0)),
                pl.BlockSpec((4, rows, width), lambda step, place: (0, place[0], 0)),
            ]
            + [ANYWHERE] * len(after),
            out_specs=pl.BlockSpec(shape, lambda step, place: (0, 0)),
        ),
        out_shape=jax.ShapeDtypeStruct(shape, NARROW_TYPE),
        compiler_params=pltpu.CompilerParams(vmem_limit_bytes=61 * MEBI),
        name="rest_payload",
    )(place, up, down.reshape(4, local, width), *after)


def expert_payload_kernel(up_ref, down_ref, *refs):
    payload_ref = refs[-1]
    local, hidden = up_ref.shape
    width = down_ref.shape[1]
    depth = hidden // (4 * local)
    for block in range(4):
        for part in range(depth):
            target = (block * depth + part) * local
            source = (part * 4 + block) * local
            payload_ref[:, target : target + local] = up_ref[:, source : source + local]
        start = hidden + block * width
        payload_ref[:, start : start + width] = down_ref[block * local : (block + 1) * local, :]


def expert_payload(up, down, after):
    local, hidden = up.shape
    whole = pl.BlockSpec(memory_space=pltpu.VMEM)
    return pl.pallas_call(
        expert_payload_kernel,
        in_specs=[whole, whole] + [ANYWHERE] * len(after),
        out_specs=whole,
        out_shape=jax.ShapeDtypeStruct((local, hidden + 4 * down.shape[1]), up.dtype),
        compiler_params=pltpu.CompilerParams(vmem_limit_bytes=61 * MEBI),
        name="expert_payload",
    )(up, down, *after)


def normalize_rows(values):
    centre = values - jnp.mean(values, axis=-1, keepdims=True)
    spread = jnp.mean(centre * centre, axis=-1, keepdims=True)
    reciprocal = lax.rsqrt(spread + EPSILON)
    return centre * reciprocal, reciprocal


def normalize_rows_back(gradient, normed, reciprocal):
    mean = jnp.mean(gradient, axis=-1, keepdims=True)
    along = jnp.mean(gradient * normed, axis=-1, keepdims=True)
    return reciprocal * (gradient - mean - normed * along)


def pick_slots(first, count, places_ref):
    patches = places_ref.shape[1]
    slot = first + lax.broadcasted_iota(jnp.int32, (count, patches), 0)
    return jnp.logical_or(slot == places_ref[0:1, :], slot == places_ref[1:2, :])


def one(mask):
    return jnp.where(mask, 1.0, 0.0).astype(NARROW_TYPE)


def mixture_kernel(grad_ref, mods_ref, places_ref, silu_ref, shared_ref, out_ref):
    step = pl.program_id(0)
    quarter = grad_ref.shape[0] // 4

    @pl.when(step == 0)
    def _():
        for part in range(4):
            rows = slice(part * quarter, (part + 1) * quarter)
            gradient = grad_ref[rows, :].astype(WIDE_TYPE) * mods_ref[part, 5:6, :]
            shared_ref[rows, :] = gradient.astype(NARROW_TYPE)

    parts = out_ref.shape[0]
    taken = one(pick_slots(step * parts * CAP, parts * CAP, places_ref))
    rows = contract(taken, shared_ref[...], 1, 0).astype(NARROW_TYPE)
    for part in range(parts):
        out_ref[part, :CAP] = rows[part * CAP : (part + 1) * CAP]
        out_ref[part, CAP:] = jnp.zeros((SPARE, out_ref.shape[2]), NARROW_TYPE)
        out_ref[part, CAP:, : silu_ref.shape[1]] = silu_ref[...]


def slot_block(width):
    return pl.BlockSpec((2, CAP + SPARE, width), lambda step: (step, 0, 0))


def spread_mixture(out_grad, mods, places, silu, after):
    count, width = out_grad.shape
    return stepped(
        mixture_kernel,
        4,
        (out_grad, mods, places, silu),
        [whole_block(operand) for operand in (out_grad, mods, places, silu)],
        [pl.BlockSpec((count, width), lambda step: (0, 0)), slot_block(width)],
        [
            jax.ShapeDtypeStruct((count, width), NARROW_TYPE),
            jax.ShapeDtypeStruct((8, CAP + SPARE, width), NARROW_TYPE),
        ],
        after,
        "spread_mixture",
    )


def first_kernel(patch_ref, mods_ref, weight_ref, first_ref, joined_ref):
    normed, _ = normalize_rows(patch_ref[...].astype(WIDE_TYPE))
    first = (normed * (1.0 + mods_ref[0, 1:2, :]) + mods_ref[0, 0:1, :]).astype(NARROW_TYPE)
    first_ref[...] = first
    width = first.shape[1]
    for part in range(3):
        columns = slice(part * width, (part + 1) * width)
        joined_ref[part] = contract(first, weight_ref[:, columns], 1, 0).astype(NARROW_TYPE)


def mods_block(mods, quarters=1):
    return pl.BlockSpec((quarters,) + mods.shape[1:], lambda step, *_: (step, 0, 0))


def first_half(patches, mods, weights, after):
    count, width = patches.shape
    quarter = count // 4
    rows = row_block(quarter, width)
    return stepped(
        first_kernel,
        4,
        (patches, mods, weights),
        [rows, mods_block(mods), column_block(weights, 3 * width, 0)],
        [rows, pl.BlockSpec((3, quarter, width), lambda step: (0, step, 0))],
        [
            jax.ShapeDtypeStruct((count, width), NARROW_TYPE),
            jax.ShapeDtypeStruct((3, count, width), NARROW_TYPE),
        ],
        after,
        "first_half",
    )


def second_kernel(
    attended_ref, patch_ref, mods_ref, routes_ref, out_ref, router_ref, attention_ref, middle_ref, second_ref, gates_ref, gate_rows_ref
):
    attention = contract(attended_ref[...], out_ref[...], 1, 0)
    attention_ref[...] = attention
    middle = patch_ref[...].astype(WIDE_TYPE) + mods_ref[0, 2:3, :] * attention
    middle_ref[...] = middle
    normed, _ = normalize_rows(middle)
    second = (normed * (1.0 + mods_ref[0, 4:5, :]) + mods_ref[0, 3:4, :]).astype(NARROW_TYPE)
    second_ref[...] = second
    logits = contract(second, router_ref[...], 1, 0)
    lane = lax.broadcasted_iota(jnp.int32, logits.shape, 1)
    picked = [
        jnp.sum(jnp.where(lane == routes_ref[:, k : k + 1], logits, 0.0), axis=1, keepdims=True)
        for k in range(TOP)
    ]
    summit = jnp.maximum(picked[0], picked[1])
    weights = [jnp.exp(value - summit) for value in picked]
    total = weights[0] + weights[1]
    gates = [weight / total for weight in weights]
    gates_ref[...] = jnp.concatenate(gates, axis=1)
    wide = jnp.where(lane == 0, gates[0], jnp.where(lane == 1, gates[1], 0.0))
    gate_rows_ref[...] = wide.T[0:TOP, :]


def second_half(attended, patches, mods, routes, weights, after):
    count, width = patches.shape
    quarter = count // 4
    rows = row_block(quarter, width)
    pair = row_block(quarter, TOP)
    wide = jax.ShapeDtypeStruct((count, width), WIDE_TYPE)
    return stepped(
        second_kernel,
        4,
        (attended, patches, mods, routes, weights, weights),
        [
            rows,
            rows,
            mods_block(mods),
            pair,
            column_block(weights, width, 3),
            column_block(weights, 128, 4 * width // 128),
        ],
        [rows, rows, rows, pair, pl.BlockSpec((TOP, quarter), lambda step: (0, step))],
        [
            wide,
            wide,
            jax.ShapeDtypeStruct((count, width), NARROW_TYPE),
            jax.ShapeDtypeStruct((count, TOP), WIDE_TYPE),
            jax.ShapeDtypeStruct((TOP, count), WIDE_TYPE),
        ],
        after,
        "second_half",
    )


def spread_kernel(second_ref, places_ref, gates_ref, rows_ref):
    parts = rows_ref.shape[0]
    first = pl.program_id(0) * parts * CAP
    slots = pick_slots(first, parts * CAP, places_ref)
    rows = contract(one(slots), second_ref[...], 1, 0).astype(NARROW_TYPE)
    slot = first + lax.broadcasted_iota(jnp.int32, slots.shape, 0)
    total = jnp.where(slot == places_ref[0:1, :], gates_ref[0:1, :], 0.0)
    total += jnp.where(slot == places_ref[1:2, :], gates_ref[1:2, :], 0.0)
    column = jnp.sum(total, axis=1, keepdims=True)
    gates = jnp.broadcast_to(column, (parts * CAP, 128)).T[0:SPARE, :]
    row = lax.broadcasted_iota(jnp.int32, gates.shape, 0)
    terms = jnp.zeros(gates.shape, WIDE_TYPE)
    for number in range(3):
        term = gates.astype(NARROW_TYPE).astype(WIDE_TYPE)
        terms = jnp.where(row == number, term, terms)
        gates = gates - term
    for part in range(parts):
        own = slice(part * CAP, (part + 1) * CAP)
        rows_ref[part, :CAP] = rows[own]
        rows_ref[part, CAP:] = jnp.zeros((SPARE, rows_ref.shape[2]), NARROW_TYPE)
        rows_ref[part, CAP:, :CAP] = terms[:, own].astype(NARROW_TYPE)


def spread_second(second_in, places, gates, after):
    width = second_in.shape[1]
    operands = (second_in, places, gates)
    return stepped(
        spread_kernel,
        4,
        operands,
        [whole_block(operand) for operand in operands],
        slot_block(width),
        jax.ShapeDtypeStruct((8, CAP + SPARE, width), NARROW_TYPE),
        after,
        "spread_second",
    )


def middle_kernel(
    left_ref,
    right_ref,
    dots_ref,
    columns_ref,
    routes_ref,
    gates_ref,
    shared_ref,
    middle_ref,
    attention_ref,
    mods_ref,
    grad_ref,
    out_ref,
    router_ref,
    grad_middle_ref,
    grad_attention_ref,
    grad_attended_ref,
    grad_logits_ref,
    sums_ref,
):
    count, width = middle_ref.shape
    quarters = mods_ref.shape[0]
    quarter = count // quarters
    slot = lax.broadcasted_iota(jnp.int32, (count, left_ref.shape[0]), 1)
    takes = [slot == columns_ref[:, k : k + 1] for k in range(TOP)]
    taken = one(jnp.logical_or(*takes))
    collected = [contract(taken, ref[...], 1, 0) for ref in (left_ref, right_ref)]
    collected = jnp.concatenate(collected, axis=1)
    gates = [gates_ref[:, k : k + 1] for k in range(TOP)]
    grad_gate = [
        jnp.sum(jnp.where(take, dots_ref[...], 0.0), axis=1, keepdims=True) for take in takes
    ]
    centre = gates[0] * grad_gate[0] + gates[1] * grad_gate[1]
    lane = lax.broadcasted_iota(jnp.int32, grad_logits_ref.shape, 1)
    grad_logits = jnp.zeros(grad_logits_ref.shape, WIDE_TYPE)
    for k in range(TOP):
        picked = gates[k] * (grad_gate[k] - centre)
        grad_logits += jnp.where(lane == routes_ref[:, k : k + 1], picked, 0.0)
    grad_logits = grad_logits.astype(NARROW_TYPE)
    grad_logits_ref[...] = grad_logits
    grad_second = shared_ref[...] + contract(grad_logits, router_ref[...], 1, 1) + collected
    normed, reciprocal = normalize_rows(middle_ref[...])
    grad_middle = grad_ref[...].astype(WIDE_TYPE) + normalize_rows_back(
        grad_second * (1.0 + mods_rows(mods_ref, 4, quarter)), normed, reciprocal
    )
    grad_middle_ref[...] = grad_middle
    grad_attention = (grad_middle * mods_rows(mods_ref, 2, quarter)).astype(NARROW_TYPE)
    grad_attention_ref[...] = grad_attention
    grad_attended_ref[...] = contract(grad_attention, out_ref[...], 1, 1).astype(NARROW_TYPE)
    totals = [grad_middle * attention_ref[...], grad_second, grad_second * normed]
    totals = [quarter_sums(total, quarters) for total in totals]
    for part in range(quarters):
        sums_ref[part] = jnp.concatenate([total[part] for total in totals], axis=0)


def sums_block(count, width, quarters=1):
    return pl.BlockSpec((quarters, count, width), lambda step: (step, 0, 0))


def mods_rows(mods_ref, piece, quarter):
    parts = [
        jnp.broadcast_to(mods_ref[part, piece : piece + 1, :], (quarter, mods_ref.shape[2]))
        for part in range(mods_ref.shape[0])
    ]
    return jnp.concatenate(parts, axis=0)


def quarter_sums(values, quarters):
    rows = values.shape[0] // quarters
    return [
        jnp.sum(values[part * rows : (part + 1) * rows], axis=0, keepdims=True)
        for part in range(quarters)
    ]


def middle_back(
    left, right, dots, columns, routes, gates, grad_shared, middle, attention, mods, out_grad, weights, after
):
    count, width = middle.shape
    half = count // 2
    rows, pair, lanes = row_block(half, width), row_block(half, TOP), row_block(half, 128)
    narrow = jax.ShapeDtypeStruct((count, width), NARROW_TYPE)
    return stepped(
        middle_kernel,
        2,
        (left, right, dots, columns, routes, gates, grad_shared, middle, attention, mods, out_grad, weights, weights),
        [whole_block(left), whole_block(right), whole_block(dots), pair, pair, pair, rows, rows, rows]
        + [mods_block(mods, 2), rows]
        + [column_block(weights, width, 3), column_block(weights, 128, 4 * width // 128)],
        [rows, rows, rows, lanes, sums_block(3, width, 2)],
        [
            jax.ShapeDtypeStruct((count, width), WIDE_TYPE),
            narrow,
            narrow,
            jax.ShapeDtypeStruct((count, 128), NARROW_TYPE),
            jax.ShapeDtypeStruct((4, 3, width), WIDE_TYPE),
        ],
        after,
        "middle_back",
    )


def output_kernel(
    result_ref, columns_ref, shared_ref, middle_ref, mods_ref, grad_ref, out_ref, sums_ref
):
    count = middle_ref.shape[0]
    quarters = mods_ref.shape[0]
    slot = lax.broadcasted_iota(jnp.int32, (count, result_ref.shape[0]), 1)
    takes = [slot == columns_ref[:, k : k + 1] for k in range(TOP)]
    mixture = shared_ref[...] + contract(one(jnp.logical_or(*takes)), result_ref[...], 1, 0)
    gate = mods_rows(mods_ref, 5, count // quarters)
    out_ref[...] = (middle_ref[...] + gate * mixture).astype(NARROW_TYPE)
    totals = quarter_sums(grad_ref[...].astype(WIDE_TYPE) * mixture, quarters)
    for part in range(quarters):
        sums_ref[part] = totals[part]


def block_output(result, columns, shared, middle, mods, out_grad, after):
    count, width = middle.shape
    half = count // 2
    rows, pair = row_block(half, width), row_block(half, TOP)
    return stepped(
        output_kernel,
        2,
        (result, columns, shared, middle, mods, out_grad),
        [whole_block(result), pair, rows, rows, mods_block(mods, 2), rows],
        [rows, sums_block(1, width, 2)],
        [
            jax.ShapeDtypeStruct((count, width), NARROW_TYPE),
            jax.ShapeDtypeStruct((4, 1, width), WIDE_TYPE),
        ],
        after,
        "block_output",
    )


def start_kernel(joined_ref, weight_ref, patch_ref, mods_ref, middle_ref, out_ref, sums_ref):
    width = patch_ref.shape[1]
    grad_first = jnp.zeros(patch_ref.shape, WIDE_TYPE)
    for part in range(3):
        columns = slice(part * width, (part + 1) * width)
        grad_first += contract(joined_ref[part], weight_ref[:, columns], 1, 1)
    normed, reciprocal = normalize_rows(patch_ref[...].astype(WIDE_TYPE))
    out_ref[...] = middle_ref[...] + normalize_rows_back(
        grad_first * (1.0 + mods_ref[0, 1:2, :]), normed, reciprocal
    )
    sums_ref[0] = jnp.concatenate(
        [
            jnp.sum(grad_first, axis=0, keepdims=True),
            jnp.sum(grad_first * normed, axis=0, keepdims=True),
        ],
        axis=0,
    )


def start_back(grad_joined, weights, patches, mods, grad_middle, after):
    count, width = patches.shape
    quarter = count // 4
    rows = row_block(quarter, width)
    return stepped(
        start_kernel,
        4,
        (grad_joined, weights, patches, mods, grad_middle),
        [
            pl.BlockSpec((3, quarter, width), lambda step: (0, step, 0)),
            column_block(weights, 3 * width, 0),
            rows,
            mods_block(mods),
            rows,
        ],
        [rows, sums_block(2, width)],
        [
            jax.ShapeDtypeStruct((count, width), WIDE_TYPE),
            jax.ShapeDtypeStruct((4, 2, width), WIDE_TYPE),
        ],
        after,
        "start_back",
    )


def expert_sums_kernel(early_ref, late_ref, up_ref, down_ref):
    local, hidden = up_ref.shape
    width = down_ref.shape[1]
    depth = hidden // (4 * local)
    for block in range(4):
        ref = (early_ref, late_ref)[block // 2]
        for part in range(depth):
            source = (block % 2) * width + part * local
            target = (part * 4 + block) * local
            up_ref[:, target : target + local] = ref[:, source : source + local].astype(WIDE_TYPE)
        source = (2 + block % 2) * width
        down_ref[block * local : (block + 1) * local] = ref[:, source : source + width].astype(WIDE_TYPE)


def expert_sums(early, late):
    local, hidden = early.shape
    width = hidden // 4
    return stepped(
        expert_sums_kernel,
        1,
        (early, late),
        [whole_block(early), column_block(late, hidden, 0)],
        [
            pl.BlockSpec((local, hidden), lambda step: (0, 0)),
            pl.BlockSpec((4 * local, width), lambda step: (0, 0)),
        ],
        [
            jax.ShapeDtypeStruct((local, hidden), WIDE_TYPE),
            jax.ShapeDtypeStruct((4 * local, width), WIDE_TYPE),
        ],
        (),
        "expert_sums",
    )


def slot_of_routes(route_rows, expert_count, capacity):
    pair_ids = route_rows.reshape(-1)
    onehot = (pair_ids[:, None] == jnp.arange(expert_count, dtype=jnp.int32)[None, :]).astype(
        jnp.int32
    )
    rank_values = jnp.cumsum(onehot, axis=0) - onehot
    slot_index = jnp.sum(rank_values * onehot, axis=1)
    return (pair_ids * capacity + slot_index).reshape(route_rows.shape)


def on_device(
    patches,
    cond,
    long_pack,
    routes,
    ada_weight,
    qkv_weight,
    out_weight,
    router_weight,
    shared_up,
    shared_down,
    expert_up,
    expert_down,
    out_grad,
):
    width = patches.shape[1]
    hidden = shared_up.shape[1]
    depth = lax.axis_size("dp")
    experts = lax.axis_size(PLANE)
    capacity = CAP
    slots = experts * capacity
    local = qkv_weight.shape[0]
    slice_rows = local // experts
    plane_index = lax.axis_index(PLANE)

    def blocked(columns):
        split = columns.reshape(columns.shape[0], depth, 4, local)
        return jnp.transpose(split, (0, 2, 1, 3)).reshape(columns.shape)

    def own(rows):
        return lax.dynamic_slice_in_dim(rows, plane_index * slice_rows, slice_rows, 0)

    places = slot_of_routes(routes, experts, capacity)
    columns, places = places, places.T
    expert_piece = expert_payload(expert_up[0], expert_down[0], ())

    cond_wide = cond.astype(WIDE_TYPE)
    cond_rows = cond.shape[0]
    if slice_rows % 8 == 0:
        first_stack = lax.all_to_all(
            first_payload(qkv_weight, out_weight, router_weight, cond, depth, slice_rows),
            "dp",
            split_axis=0,
            concat_axis=0,
            tiled=True,
        )
        first_end = 4 * width + 128
        silu_parts = first_stack[:, :cond_rows, first_end : first_end + local]
        rest_piece = rest_payload(
            shared_up, shared_down, slice_rows, (places, expert_piece)
        )
        rest_piece, first_stack = together(rest_piece, first_stack)
    else:
        silu_cond = jax.nn.silu(cond_wide).astype(NARROW_TYPE)
        silu_parts = lax.all_to_all(
            jnp.transpose(silu_cond.reshape(cond_rows, depth, local), (1, 0, 2)),
            "dp",
            split_axis=0,
            concat_axis=0,
            tiled=True,
        )
        router_slice = jnp.pad(own(router_weight), ((0, 0), (0, 128 - router_weight.shape[1])))
        first_stack = depth_stack(
            jnp.concatenate([own(qkv_weight), own(out_weight), router_slice], axis=1)
        )
        down_slice = lax.dynamic_slice_in_dim(
            shared_down.reshape(4, local, width), plane_index * slice_rows, slice_rows, 1
        )
        rest_piece = jnp.concatenate(
            [
                blocked(own(shared_up)),
                jnp.transpose(down_slice, (1, 0, 2)).reshape(slice_rows, 4 * width),
            ],
            axis=1,
        )
    silu_parts = silu_parts.reshape(depth * cond_rows, local)
    partial = product_plain_operands(silu_parts, ada_weight)
    first_sides = side_gather(first_stack)
    rest_stack = lax.all_gather(rest_piece, "dp", axis=0)
    modulation = jnp.sum(
        lax.all_to_all(
            partial.reshape(depth, cond_rows, 6 * width), "dp", split_axis=0, concat_axis=0, tiled=True
        ),
        axis=0,
    )
    blocks = modulation.reshape(4, 6, width)
    is_long = long_pack[0] == 1
    mods = jnp.where(is_long, blocks[:1], blocks)

    def exchange(rows):
        return lax.all_to_all(rows, PLANE, split_axis=0, concat_axis=0, tiled=True)

    grad_shared, mixture_slots = spread_mixture(
        out_grad, mods, places, silu_parts.reshape(SPARE, -1), ()
    )
    expert_piece, *first_sides = together(expert_piece, *first_sides)
    first_near = near_slices(first_sides, (mixture_slots,))
    expert_weights = lax.all_gather(expert_piece, "dp", axis=0, tiled=True)
    mixture_slots = exchange(mixture_slots)
    first_full = plane_gather(first_near)
    rest_sides = side_gather(rest_stack)
    first_in, joined = first_half(patches, mods, first_full, ())
    attended, log_total = attend(long_pack, joined)
    attended, mixture_slots = together(attended, mixture_slots)
    attention, middle, second_in, gate_values, gate_rows = second_half(
        attended, patches, mods, routes, first_full, ()
    )
    slot_rows = spread_second(second_in, places, gate_rows, ())
    rest = plane_gather(near_slices(rest_sides, (attended, slot_rows)))
    slots_there = exchange(slot_rows)

    shared, grad_from_shared, kept, sent = shared_expert(
        second_in, grad_shared, rest, local, (slot_rows,)
    )
    sent, slots_there = together(sent, slots_there)
    routed = (slots_there, mixture_slots)
    silu_all = mixture_slots[:, capacity:, : silu_parts.size // SPARE]
    silu_all = silu_all.reshape(experts, depth, cond_rows, local)
    silu_all = jnp.transpose(silu_all, (1, 0, 2, 3)).reshape(depth * experts * cond_rows, local)
    middle_own, *middle_sides = pair_sum(kept, flip(sent, CORE))
    middle_sides = side_flips(middle_sides)
    result_rows, *grad_rows, gate_dots, units, grad_units = routed_expert(
        *routed, expert_weights, (middle_own,)
    )
    *middle_sides, left, right = together(*middle_sides, *grad_rows)
    left_back = exchange(left.reshape(experts, capacity, width // 2))
    left_back, gate_dots = together(left_back, gate_dots)
    left_back = left_back.reshape(slots, width // 2)
    gate_dots_back = exchange(gate_dots.reshape(experts, 1, capacity)).reshape(1, slots)
    early_sums = routed_sums(*routed, units, grad_units, 0, ())
    early_sums, left_back = together(early_sums, left_back)
    early_final = lax.psum_scatter(early_sums, "dp", scatter_dimension=0, tiled=True)
    middle_sum = side_sum(middle_own, *middle_sides, after=(early_sums,))
    right, middle_sum = together(right, middle_sum)
    right_back = exchange(right.reshape(experts, capacity, width // 2)).reshape(slots, width // 2)
    late_sums = routed_sums(*routed, units, grad_units, 1, (early_sums,), (middle_sum,))

    grad_middle, grad_attention, grad_attended, grad_logits, middle_sums = middle_back(
        left_back,
        right_back,
        gate_dots_back,
        columns,
        routes,
        gate_values,
        grad_from_shared,
        middle,
        attention,
        mods,
        out_grad,
        first_full,
        (silu_all,),
    )
    late_sums, grad_attended = together(late_sums, grad_attended)
    late_final = lax.psum_scatter(late_sums, "dp", scatter_dimension=0, tiled=True)
    result_back = exchange(result_rows.reshape(experts, capacity, width)).reshape(slots, width)
    grad_joined = attend_back(long_pack, joined, log_total, grad_attended, ())
    last_parts = last_gradients(
        grad_joined, first_in, grad_attention, attended, grad_logits, second_in, (result_back,)
    )
    block_out, output_sums = block_output(
        result_back,
        columns,
        shared,
        middle,
        mods,
        out_grad,
        (*last_parts, early_final),
    )
    last_pair = pair_sum(last_parts[0], flip(last_parts[1], CORE), (output_sums,))
    patches_grad, start_sums = start_back(
        grad_joined, first_full, patches, mods, grad_middle, tuple(last_pair)
    )
    last_sides = side_flips(last_pair[1:])
    grad_chosen = jnp.concatenate([start_sums, middle_sums, output_sums], axis=1)
    grad_chosen = grad_chosen.reshape(1, 4, 6 * width)
    long_total = jnp.sum(grad_chosen, axis=1, keepdims=True)
    first_slot = (jnp.arange(4, dtype=jnp.int32) == 0)[None, :, None]
    grad_blocks = jnp.where(is_long, jnp.where(first_slot, long_total, 0.0), grad_chosen)
    grad_modulation = grad_blocks.reshape(cond_rows, 6 * width).astype(NARROW_TYPE)
    everyone = ("dp",) + PLANE
    columns = 6 * width // experts
    grad_columns = jnp.transpose(grad_modulation.reshape(cond_rows, experts, columns), (1, 0, 2))
    *last_sides, grad_columns = together(*last_sides, grad_columns)
    last_sum = side_sum(last_pair[0], *last_sides)
    grad_columns = jnp.broadcast_to(grad_columns[None], (depth, experts, cond_rows, columns))
    grad_columns = lax.all_to_all(
        grad_columns.reshape(depth * experts, cond_rows, columns),
        everyone,
        split_axis=0,
        concat_axis=0,
        tiled=True,
    ).reshape(depth * experts * cond_rows, columns)
    grad_columns, last_sum = together(grad_columns, last_sum)
    ada_weight_grad = product_left_operand(silu_all, grad_columns)
    own_ada = lax.dynamic_slice_in_dim(ada_weight, plane_index * columns, columns, 1)
    silu_back = product_right_operand(grad_columns, own_ada)
    silu_back = lax.all_to_all(
        silu_back.reshape(depth * experts, cond_rows, local),
        everyone,
        split_axis=0,
        concat_axis=0,
        tiled=True,
    )
    silu_back, late_final = together(silu_back, late_final)
    silu_back = jnp.sum(silu_back.reshape(depth, experts, cond_rows, local), axis=1)
    grad_silu = jnp.transpose(silu_back, (1, 0, 2)).reshape(cond_rows, width)
    cond_grad = jax.vjp(jax.nn.silu, cond_wide)[1](grad_silu)[0]
    last_final = depth_scatter(last_sum)
    edge_one, edge_two = 3 * width // experts, 4 * width // experts
    qkv_weight_grad = last_final[:, :edge_one]
    out_weight_grad = last_final[:, edge_one:edge_two]
    router_weight_grad = last_final[:, edge_two : edge_two + 1]

    middle_final = late_final[:, hidden:].astype(WIDE_TYPE)
    shared_up_grad = middle_final[:, : hidden // experts]
    shared_down_grad = jnp.transpose(
        middle_final[:, hidden // experts :].reshape(local, 4, width // experts), (1, 0, 2)
    ).reshape(4 * local, width // experts)
    expert_up_grad, expert_down_grad = expert_sums(early_final, late_final)
    return (
        block_out,
        patches_grad,
        cond_grad,
        ada_weight_grad,
        qkv_weight_grad,
        out_weight_grad,
        router_weight_grad,
        shared_up_grad,
        shared_down_grad,
        expert_up_grad[None],
        expert_down_grad[None],
    )


def solution(mesh):
    in_specs = (
        P(("dp", "expert", "stream"), None),
        P(("dp", "expert", "stream"), None),
        P(("dp", "expert", "stream")),
        P(("dp", "expert", "stream"), None),
        P("dp", None),
        P("dp", None),
        P("dp", None),
        P("dp", None),
        P("dp", None),
        P("dp", None),
        P(("expert", "stream"), "dp", None),
        P(("expert", "stream"), "dp", None),
        P(("dp", "expert", "stream"), None),
    )
    out_specs = (
        P(("dp", "expert", "stream"), None),
        P(("dp", "expert", "stream"), None),
        P(("dp", "expert", "stream"), None),
        P("dp", ("expert", "stream")),
        P("dp", ("expert", "stream")),
        P("dp", ("expert", "stream")),
        P("dp", ("expert", "stream")),
        P("dp", ("expert", "stream")),
        P("dp", ("expert", "stream")),
        P(("expert", "stream"), "dp", None),
        P(("expert", "stream"), "dp", None),
    )
    return jax.shard_map(
        on_device, mesh=mesh, in_specs=in_specs, out_specs=out_specs, check_vma=False
    )
```
